32 devices in a mesh: grp: 4 (over x, core), fs: 8 (over z, y).
Axes of the slice: x: 2, y: 2, z: 4, core: 2. Of those that a mesh axis runs over, the one named last changes fastest.
Arguments:
- image_patches: bfloat16 [32, 24, 24, 384], P(('grp', 'fs')), may hold values from -6 to 6
- cotangent: bfloat16 [32, 24, 24, 384], P(('grp', 'fs')), may hold values from -6 to 6
- image_count: int32 [4, 8], P('grp', 'fs'), may hold values from 0 to 1, as said below
- resolution: int32 [32], P(('grp', 'fs')), may hold values from 14 to 24, as said below
- owner_list: int32 [6], replicated, may hold values from 0 to 3, as said below
- focal_weight: float32 [4, 384, 768], P('grp', 'fs'), may hold values from -0.3125 to 0.3125
- focal_first: float32 [4, 384, 768], P('grp', 'fs'), may hold values from -96 to 96
- focal_second: float32 [4, 384, 768], P('grp', 'fs'), may hold values from 480 to 7520
- modulate_weight: float32 [4, 384, 384], P('grp', 'fs'), may hold values from -0.3125 to 0.3125
- modulate_first: float32 [4, 384, 384], P('grp', 'fs'), may hold values from -112 to 112
- modulate_second: float32 [4, 384, 384], P('grp', 'fs'), may hold values from 768 to 12320
- project_weight: float32 [4, 384, 384], P('grp', 'fs'), may hold values from -0.3125 to 0.3125
- project_first: float32 [4, 384, 384], P('grp', 'fs'), may hold values from -112 to 112
- project_second: float32 [4, 384, 384], P('grp', 'fs'), may hold values from 768 to 12320
- expand_weight: float32 [4, 384, 1536], P('grp', 'fs'), may hold values from -0.3125 to 0.3125
- expand_first: float32 [4, 384, 1536], P('grp', 'fs'), may hold values from -40 to 40
- expand_second: float32 [4, 384, 1536], P('grp', 'fs'), may hold values from 86.4 to 1376
- shrink_weight: float32 [4, 1536, 384], P('grp', 'fs'), may hold values from -0.15625 to 0.15625
- shrink_first: float32 [4, 1536, 384], P('grp', 'fs'), may hold values from -64 to 64
- shrink_second: float32 [4, 1536, 384], P('grp', 'fs'), may hold values from 288 to 4608
- vector_weight: float32 [4, 102, 384], P('grp', None, 'fs'), as said below
- vector_first: float32 [4, 102, 384], P('grp', None, 'fs'), may hold values from -80 to 80
- vector_second: float32 [4, 102, 384], P('grp', None, 'fs'), may hold values from 384 to 6560
Outputs:
- block_output: bfloat16 [32, 24, 24, 384], P(('grp', 'fs'))
- input_grad: float32 [32, 24, 24, 384], P(('grp', 'fs'))
- focal_new: float32 [4, 384, 768], P('grp', 'fs')
- focal_first_new: float32 [4, 384, 768], P('grp', 'fs')
- focal_second_new: float32 [4, 384, 768], P('grp', 'fs')
- modulate_new: float32 [4, 384, 384], P('grp', 'fs')
- modulate_first_new: float32 [4, 384, 384], P('grp', 'fs')
- modulate_second_new: float32 [4, 384, 384], P('grp', 'fs')
- project_new: float32 [4, 384, 384], P('grp', 'fs')
- project_first_new: float32 [4, 384, 384], P('grp', 'fs')
- project_second_new: float32 [4, 384, 384], P('grp', 'fs')
- expand_new: float32 [4, 384, 1536], P('grp', 'fs')
- expand_first_new: float32 [4, 384, 1536], P('grp', 'fs')
- expand_second_new: float32 [4, 384, 1536], P('grp', 'fs')
- shrink_new: float32 [4, 1536, 384], P('grp', 'fs')
- shrink_first_new: float32 [4, 1536, 384], P('grp', 'fs')
- shrink_second_new: float32 [4, 1536, 384], P('grp', 'fs')
- vector_new: float32 [4, 102, 384], P('grp', None, 'fs')
- vector_first_new: float32 [4, 102, 384], P('grp', None, 'fs')
- vector_second_new: float32 [4, 102, 384], P('grp', None, 'fs')
The draws below stay inside these ranges and needn't reach their ends.
Inputs may be any that keep to these rules, and one draw needn't show every extreme that they name: A device's first image_count slots hold images, the others are padding. The device at the head of both axes holds none, and in every draw some devices hold 1. `resolution`: each image is 14, 16 or 24 patches on a side (images of 224, 256 and 384 pixels); both 14 and 24 occur in every draw. `owner_list`: owners in the order focal, modulate, project, expand, shrink, vector; group 0 and group 4 - 1 own something in every draw. `vector_weight`: rows 0 and 7 lie in 0.5 to 1.5, rows 6 and 10 in 1 to 2.5.
All inputs are finite; a program needn't handle non-finite values.
Results may differ from the reference program's by a relative error of at most 0.0097.
Values may be sent and summed in bfloat16 or wider, within the bound.
A program may use at most 128 MiB of HBM per device.

```python
import math
import jax
import jax.numpy as jnp
import numpy as np
from jax import lax

C = 384
HID = 1536
LEVELS = 3
GATES = 4
SIDE = 24
IMG_DEV = 1
STEP = 10
TENSORS = 6
NVEC = 102
IMAGES = 32
N_GRP = 4
N_FS = 8


def vector_table():
    bias_rows = HID // C
    offsets = np.zeros(NVEC, np.float32)
    widths = np.zeros(NVEC, np.float32)
    sigmas = np.zeros(NVEC, np.float32)
    for row_index in (0, 7):
        offsets[row_index] = 0.5
        widths[row_index] = 1.0
    for row_index in (6, 10):
        offsets[row_index] = 1.0
        widths[row_index] = 1.5
    for row_index in (1, 2, 3, 4, 8):
        sigmas[row_index] = 0.5
    for row_index in (5, 9):
        sigmas[row_index] = 0.3
    sigmas[11:11 + bias_rows] = 0.5
    gate_start = 11 + bias_rows
    sigmas[gate_start:gate_start + GATES] = C ** (-0.5)
    offset = gate_start + GATES
    for number in range(LEVELS):
        kernel_side = 2 * number + 3
        sigmas[offset:offset + kernel_side * kernel_side] = 1.0 / kernel_side
        offset = offset + kernel_side * kernel_side
    return (offsets, widths, sigmas)


def draw_vector_weight(key, part):
    key = jax.random.fold_in(key, 14)
    first_key, second_key = jax.random.split(key)
    offsets, widths, sigmas = vector_table()
    normal_part = jax.random.truncated_normal(first_key, -4.0, 4.0, (N_GRP, NVEC, C), jnp.float32)
    uniform_part = jax.random.uniform(second_key, (N_GRP, NVEC, C), jnp.float32)
    return jnp.asarray(offsets)[None, :, None] + jnp.asarray(widths)[None, :, None] * uniform_part + jnp.asarray(sigmas)[None, :, None] * normal_part


def draw_image_count(key, part):
    key = jax.random.fold_in(key, 11)
    first_key, second_key = jax.random.split(key)
    groups = jnp.arange(N_GRP, dtype=jnp.int32)[:, None]
    shards = jnp.arange(N_FS, dtype=jnp.int32)[None, :]
    placed = shards * N_GRP + groups * N_FS
    jitter = jax.random.randint(first_key, (N_GRP, N_FS), 0, N_GRP * N_FS, dtype=jnp.int32)
    counts = jnp.minimum(IMG_DEV, (IMG_DEV + 1) * (placed + jitter) // (2 * N_GRP * N_FS))
    filled = jax.random.randint(second_key, (), N_FS // 2, N_FS, dtype=jnp.int32)
    counts = jnp.where(shards == filled, IMG_DEV, counts)
    counts = jnp.where((groups == 0) & (shards == 0), 0, counts)
    counts = jnp.where((groups == N_GRP - 1) & (shards == filled), 0, counts)
    return counts.astype(jnp.int32)


def draw_resolution(key, part):
    key = jax.random.fold_in(key, 12)
    slot_index = jnp.arange(IMAGES, dtype=jnp.int32)
    device = slot_index // IMG_DEV
    groups = device // N_FS
    shards = device % N_FS
    placed = shards * N_GRP + groups * N_FS
    jitter = jax.random.randint(key, (IMAGES,), 0, 2 * N_GRP * N_FS, dtype=jnp.int32)
    section = 3 * (placed + jitter) // (4 * N_GRP * N_FS)
    sides = jnp.where(section >= 2, 24, jnp.where(section >= 1, 16, 14))
    sides = sides.at[0].set(14).at[IMAGES - IMG_DEV].set(24)
    return sides.astype(jnp.int32)


def draw_owner_list(key, part):
    key = jax.random.fold_in(key, 13)
    first_key, second_key = jax.random.split(key)
    owners = jax.random.randint(first_key, (TENSORS,), 0, N_GRP, dtype=jnp.int32)
    order = jax.random.permutation(second_key, TENSORS)
    owners = owners.at[order[0]].set(0).at[order[1]].set(N_GRP - 1)
    return owners.astype(jnp.int32)


def level_of(stream_key, extent, pieces, least, top_value):
    level, own = 1.0, jax.random.fold_in(stream_key, 6)
    for position, parts in pieces:
        draws = jnp.exp(jax.random.uniform(jax.random.fold_in(own, position), (parts,), jnp.float32, least / len(pieces), top_value / len(pieces)))
        level = level * jnp.repeat(draws, extent[position] // parts).reshape([-1 if axis == position else 1 for axis in range(len(extent))])
    return level


def bell_draw(stream_key, extent, spread, bound, pieces=(), kind=jnp.bfloat16):
    level = level_of(stream_key, extent, pieces, -0.22, 0.18) if pieces else 1.0
    values = jax.random.normal(stream_key, extent, jnp.float32) * spread * level
    return jnp.minimum(jnp.maximum(values, -bound), bound).astype(kind)


def setup_inputs(seed: int = 0) -> dict:
    arg_keys = jax.random.split(jax.random.key(seed), 24)
    return {
        "image_patches": bell_draw(arg_keys[0], (IMAGES, SIDE, SIDE, C), 1.0, 6.0, ((0, 32),)),
        "cotangent": bell_draw(arg_keys[1], (IMAGES, SIDE, SIDE, C), 1.0, 6.0, ((0, 32),)),
        "image_count": draw_image_count(jax.random.fold_in(arg_keys[23], 71), 0),
        "resolution": draw_resolution(jax.random.fold_in(arg_keys[23], 71), 0),
        "owner_list": draw_owner_list(jax.random.fold_in(arg_keys[23], 71), 0),
        "focal_weight": bell_draw(arg_keys[5], (N_GRP, C, 2 * C), C ** -0.5, 0.3125, ((0, 4), (1, 8)), jnp.float32),
        "focal_first": bell_draw(arg_keys[6], (N_GRP, C, 2 * C), (0.16 * (285 * IMAGES) ** 0.5), 96.0, ((0, 4), (1, 8)), jnp.float32),
        "focal_second": jnp.clip(jnp.exp(math.log(7520.0) - 2.7515353 * jax.random.uniform(arg_keys[7], (N_GRP, C, 2 * C), jnp.float32) ** level_of(arg_keys[7], (N_GRP, C, 2 * C), ((0, 4), (1, 8)), -0.2, 0.2)), 480.0, 7520.0),
        "modulate_weight": bell_draw(arg_keys[8], (N_GRP, C, C), C ** -0.5, 0.3125, ((0, 4), (1, 8)), jnp.float32),
        "modulate_first": bell_draw(arg_keys[9], (N_GRP, C, C), (0.2 * (285 * IMAGES) ** 0.5), 112.0, ((0, 4), (1, 8)), jnp.float32),
        "modulate_second": jnp.clip(jnp.exp(math.log(12320.0) - 2.7751895 * jax.random.uniform(arg_keys[10], (N_GRP, C, C), jnp.float32) ** level_of(arg_keys[10], (N_GRP, C, C), ((0, 4), (1, 8)), -0.2, 0.2)), 768.0, 12320.0),
        "project_weight": bell_draw(arg_keys[11], (N_GRP, C, C), C ** -0.5, 0.3125, ((0, 4), (1, 8)), jnp.float32),
        "project_first": bell_draw(arg_keys[12], (N_GRP, C, C), (0.2 * (285 * IMAGES) ** 0.5), 112.0, ((0, 4), (1, 8)), jnp.float32),
        "project_second": jnp.clip(jnp.exp(math.log(12320.0) - 2.7751895 * jax.random.uniform(arg_keys[13], (N_GRP, C, C), jnp.float32) ** level_of(arg_keys[13], (N_GRP, C, C), ((0, 4), (1, 8)), -0.2, 0.2)), 768.0, 12320.0),
        "expand_weight": bell_draw(arg_keys[14], (N_GRP, C, HID), C ** -0.5, 0.3125, ((0, 4), (1, 8)), jnp.float32),
        "expand_first": bell_draw(arg_keys[15], (N_GRP, C, HID), (0.066 * (285 * IMAGES) ** 0.5), 40.0, ((0, 4), (1, 8)), jnp.float32),
        "expand_second": jnp.clip(jnp.exp(math.log(1376.0) - 2.7679483 * jax.random.uniform(arg_keys[16], (N_GRP, C, HID), jnp.float32) ** level_of(arg_keys[16], (N_GRP, C, HID), ((0, 4), (1, 8)), -0.2, 0.2)), 86.4, 1376.0),
        "shrink_weight": bell_draw(arg_keys[17], (N_GRP, HID, C), HID ** -0.5, 0.15625, ((0, 4), (1, 8)), jnp.float32),
        "shrink_first": bell_draw(arg_keys[18], (N_GRP, HID, C), (0.12 * (285 * IMAGES) ** 0.5), 64.0, ((0, 4), (1, 8)), jnp.float32),
        "shrink_second": jnp.clip(jnp.exp(math.log(4608.0) - 2.7725887 * jax.random.uniform(arg_keys[19], (N_GRP, HID, C), jnp.float32) ** level_of(arg_keys[19], (N_GRP, HID, C), ((0, 4), (1, 8)), -0.2, 0.2)), 288.0, 4608.0),
        "vector_weight": draw_vector_weight(jax.random.fold_in(arg_keys[23], 71), 0),
        "vector_first": bell_draw(arg_keys[21], (N_GRP, NVEC, C), (0.14 * (285 * IMAGES) ** 0.5), 80.0, ((0, 4), (2, 8)), jnp.float32),
        "vector_second": jnp.clip(jnp.exp(math.log(6560.0) - 2.8381033 * jax.random.uniform(arg_keys[22], (N_GRP, NVEC, C), jnp.float32) ** level_of(arg_keys[22], (N_GRP, NVEC, C), ((0, 4), (2, 8)), -0.2, 0.2)), 384.0, 6560.0),
    }


highest = lax.Precision.HIGHEST
beta_one = 0.9
beta_two = 0.95
adam_eps = 1e-08
weight_decay = 0.05
norm_eps = 1e-05

@jax.custom_vjp
def low(v):
    return lax.optimization_barrier(v.astype(jnp.bfloat16)).astype(jnp.float32)

@jax.custom_vjp
def low_back(v):
    return v

def low_keep(v):
    return (low(v), None)

def low_pass(kept, grad):
    return (grad,)

def back_keep(v):
    return (v, None)

def back_low(kept, grad):
    return (low(grad),)
low.defvjp(low_keep, low_pass)
low_back.defvjp(back_keep, back_low)

def matmul_high(left_side, right_side):
    return jnp.dot(left_side, right_side, precision=highest)

def layer_norm(values, norm_gain, norm_shift):
    row_mean = lax.optimization_barrier(jnp.mean(values, axis=-1, keepdims=True))
    centred = values - row_mean
    row_var = lax.optimization_barrier(jnp.mean(centred * centred, axis=-1, keepdims=True))
    return centred * lax.rsqrt(row_var + norm_eps) * norm_gain + norm_shift

def gelu_exact(values):
    return jax.nn.gelu(values, approximate=False)

def depthwise(feature_map, kernel):
    return lax.conv_general_dilated(feature_map, kernel, (1, 1), 'SAME', dimension_numbers=('NHWC', 'HWIO', 'NHWC'), feature_group_count=feature_map.shape[-1], precision=highest)

def focal_context(context, gate_values, kernel_rows, live_mask, live_area):
    current = context * live_mask
    combined = jnp.zeros_like(context)
    offset = 0
    for number in range(LEVELS):
        kernel_side = 2 * number + 3
        kernel = kernel_rows[offset:offset + kernel_side * kernel_side].reshape(kernel_side, kernel_side, 1, -1)
        offset = offset + kernel_side * kernel_side
        current = gelu_exact(depthwise(current, kernel)) * live_mask
        combined = combined + current * gate_values[..., number:number + 1]
    pooled = gelu_exact(lax.optimization_barrier(jnp.sum(current, axis=(1, 2))) / live_area[:, None])
    return combined + pooled[:, None, None, :] * gate_values[..., LEVELS:LEVELS + 1]

def split_vector(vector):
    channels = vector.shape[1]
    bias_rows = HID // channels
    single_rows = [vector[row_index] for row_index in range(11)]
    expand_bias = vector[11:11 + bias_rows].reshape(-1)
    gate_rows = vector[11 + bias_rows:11 + bias_rows + GATES]
    kernel_rows = vector[11 + bias_rows + GATES:]
    return (single_rows, expand_bias, gate_rows, kernel_rows)

def image_mask(live_count, resolution, grid_side):
    slot_index = jnp.arange(resolution.shape[0])
    cell_index = jnp.arange(grid_side)
    inside = cell_index[None, :] < resolution[:, None]
    is_live = slot_index < live_count
    joint_mask = is_live[:, None, None] & inside[:, :, None] & inside[:, None, :]
    live_area = (resolution * resolution).astype(jnp.float32)
    return (joint_mask.astype(jnp.float32)[..., None], live_area)

def tensor_rates():
    wide_rate = 1.5 / math.sqrt(C)
    return (wide_rate, wide_rate, wide_rate, wide_rate, 1.5 / math.sqrt(HID), 0.2)

def adam_step(weight, first_moment, second_moment, gradient, step_rate):
    first_new = beta_one * first_moment + (1.0 - beta_one) * gradient
    second_new = beta_two * second_moment + (1.0 - beta_two) * gradient * gradient
    first_hat = first_new / (1.0 - beta_one ** STEP)
    second_hat = second_new / (1.0 - beta_two ** STEP)
    weight_new = weight - step_rate * (first_hat / (jnp.sqrt(second_hat) + adam_eps) + weight_decay * weight)
    return (weight_new, first_new, second_new)

def block_forward(params, patches, live_mask, live_area):
    focal_mat, modulate_mat, project_mat, expand_mat, shrink_mat, vector = params
    single_rows, expand_bias, gate_rows, kernel_rows = split_vector(vector)
    first_gain, first_shift, query_bias, context_bias, modulate_bias, project_bias, first_scale, second_gain, second_shift, shrink_bias, second_scale = single_rows
    channels = patches.shape[-1]
    grid_shape = patches.shape[:3]
    inputs = patches.reshape(-1, channels)
    normed = layer_norm(inputs, first_gain, first_shift)
    pre_focal = low_back(matmul_high(low(normed), low(focal_mat)))
    query_rows = pre_focal[:, :channels] + query_bias
    context = pre_focal[:, channels:] + context_bias
    gate_values = matmul_high(normed, gate_rows.T)
    summed = focal_context(context.reshape(grid_shape + (channels,)), gate_values.reshape(grid_shape + (GATES,)), kernel_rows, live_mask, live_area).reshape(-1, channels)
    modulator = low_back(matmul_high(low(summed), low(modulate_mat))) + modulate_bias
    mixed_rows = query_rows * modulator
    projected = low_back(matmul_high(low(mixed_rows), low(project_mat))) + project_bias
    middle = inputs + first_scale * projected
    second = layer_norm(middle, second_gain, second_shift)
    hidden = low_back(matmul_high(low(second), low(expand_mat))) + expand_bias
    active = gelu_exact(hidden)
    shrunk = low_back(matmul_high(low(active), low(shrink_mat))) + shrink_bias
    result = (middle + second_scale * shrunk) * live_mask.reshape(-1, 1)
    return result.reshape(patches.shape)

def reference(image_patches, cotangent, image_count, resolution, owner_list, focal_weight, focal_first, focal_second, modulate_weight, modulate_first, modulate_second, project_weight, project_first, project_second, expand_weight, expand_first, expand_second, shrink_weight, shrink_first, shrink_second, vector_weight, vector_first, vector_second):
    stacks = (focal_weight, modulate_weight, project_weight, expand_weight, shrink_weight, vector_weight)
    firsts = (focal_first, modulate_first, project_first, expand_first, shrink_first, vector_first)
    seconds = (focal_second, modulate_second, project_second, expand_second, shrink_second, vector_second)
    params = tuple((stacked[owner_list[row_index]] for row_index, stacked in enumerate(stacks)))
    devices = N_GRP * N_FS
    patches = image_patches.reshape(devices, IMG_DEV, SIDE, SIDE, C)
    upstream = cotangent.reshape(devices, IMG_DEV, SIDE, SIDE, C)
    counts = image_count.reshape(devices)
    side_lists = resolution.reshape(devices, IMG_DEV)

    def one_device(totals, device_items):
        device_patches, device_upstream, live_count, device_sides = device_items
        live_mask, live_area = image_mask(live_count, device_sides, SIDE)

        def forward(params_in, patches_in):
            return block_forward(params_in, patches_in, live_mask, live_area)
        outputs, pullback = jax.vjp(forward, params, device_patches.astype(jnp.float32))
        param_grads, patch_grads = pullback(device_upstream.astype(jnp.float32))
        totals = jax.tree.map(lambda running, addend: running + addend, totals, param_grads)
        return (totals, (outputs.astype(jnp.bfloat16), patch_grads))
    zero_grads = jax.tree.map(jnp.zeros_like, params)
    param_total, (outputs, patch_grads) = lax.scan(one_device, zero_grads, (patches, upstream, counts, side_lists))
    results = [outputs.reshape(image_patches.shape), patch_grads.reshape(image_patches.shape)]
    group_index = jnp.arange(N_GRP)
    step_rates = tensor_rates()
    for row_index in range(TENSORS):
        owner_index = owner_list[row_index]
        updated = adam_step(params[row_index], firsts[row_index][owner_index], seconds[row_index][owner_index], param_total[row_index], step_rates[row_index])
        for new_value in updated:
            chosen = (group_index == owner_index).reshape((N_GRP,) + (1,) * new_value.ndim)
            results.append(jnp.where(chosen, new_value[None], 0.0))
    return (results[0], results[1], results[2], results[3], results[4], results[5], results[6], results[7], results[8], results[9], results[10], results[11], results[12], results[13], results[14], results[15], results[16], results[17], results[18], results[19])
```

```python
import math

import jax
import jax.numpy as jnp
from jax import lax
from jax.experimental import pallas as pl
from jax.experimental.pallas import tpu as pltpu
from jax.sharding import PartitionSpec as P

f32 = jnp.float32
b16 = jnp.bfloat16
LEVELS = 3
GATES = 4
LANE = 128
norm_eps = 1e-05
PAD = 3
EDGE = 8
SQRT_HALF = math.sqrt(0.5)
INV_SQRT_2PI = 1.0 / math.sqrt(2.0 * math.pi)
BLK = 48


def gelu_parts(z):
    az = jnp.abs(z)
    t = 1.0 / (1.0 + (0.3275911 * SQRT_HALF) * az)
    e = jnp.exp(z * z * -0.5)
    poly = t * (
        0.5 * 0.254829592
        + t * (0.5 * -0.284496736 + t * (0.5 * 1.421413741 + t * (0.5 * -1.453152027 + t * (0.5 * 1.061405429))))
    )
    tail = poly * e
    phi = jnp.where(z >= 0.0, 1.0 - tail, tail)
    return z * phi, phi + z * e * INV_SQRT_2PI


def mm(a, b):
    return jnp.dot(a, b, preferred_element_type=f32)


def mm_t(a, b):
    return lax.dot_general(a, b, (((1,), (1,)), ((), ())), preferred_element_type=f32)


def mm_g(a, b):
    return lax.dot_general(a, b, (((0,), (0,)), ((), ())), preferred_element_type=f32)


def tall(values):
    rows, cols = values.shape
    return jnp.sum(values.reshape(rows // 8, 8, cols), axis=0)


def lane_sum(values):
    parts = values[:, :LANE]
    for start in range(LANE, values.shape[1], LANE):
        parts = parts + values[:, start : start + LANE]
    return jnp.sum(parts, axis=1, keepdims=True)


class Shape:
    def __init__(self, side, channels, hid):
        self.side = side
        self.rows = side * side
        self.c = channels
        self.nc = channels // LANE
        self.hid = hid
        self.bias_rows = hid // channels
        self.gate_at = 11 + self.bias_rows
        self.kernel_at = self.gate_at + GATES
        self.taps = [(2 * n + 3) ** 2 for n in range(LEVELS)]
        self.nvec = self.kernel_at + sum(self.taps)
        self.padded = (self.nc, side + 2 * PAD, side + 2 * EDGE, LANE)


def compute_scratch(s):
    flat = (s.rows, s.c)
    split = (s.nc, s.rows, LANE)
    grid = (s.nc, s.side, s.side, LANE)
    return dict(
        vc=pltpu.VMEM((s.nc, s.nvec, LANE), f32),
        mask=pltpu.VMEM((s.rows, LANE), f32),
        xh1=pltpu.VMEM(flat, f32),
        r1=pltpu.VMEM((s.rows, LANE), f32),
        n1b=pltpu.VMEM(flat, b16),
        gate=pltpu.VMEM((GATES, s.rows, LANE), f32),
        q=pltpu.VMEM(flat, f32),
        pads=[pltpu.VMEM(s.padded, f32) for _ in range(LEVELS + 1)],
        gd=[pltpu.VMEM(grid, f32) for _ in range(LEVELS)],
        summed=pltpu.VMEM(grid, f32),
        sumb=pltpu.VMEM(flat, b16),
        mod=pltpu.VMEM(flat, f32),
        mixb=pltpu.VMEM(flat, b16),
        proj=pltpu.VMEM(flat, f32),
        mid=pltpu.VMEM(flat, f32),
        xh2=pltpu.VMEM(flat, f32),
        r2=pltpu.VMEM((s.rows, LANE), f32),
        n2b=pltpu.VMEM(flat, b16),
        dshrb=pltpu.VMEM(flat, b16),
        actb=pltpu.VMEM((s.rows, s.hid), b16),
        dhidb=pltpu.VMEM((s.rows, s.hid), b16),
        shr=pltpu.VMEM(flat, f32),
        dn=pltpu.VMEM(flat, f32),
        dqb=pltpu.VMEM(flat, b16),
        dsum=pltpu.VMEM(split, f32),
        dgate=pltpu.VMEM((GATES, s.rows, LANE), f32),
        dctxb=pltpu.VMEM(flat, b16),
        gacc=pltpu.VMEM((s.nc, sum(s.taps), 8, LANE), f32),
        pool=pltpu.VMEM((2, 8, s.c), f32),
    )


class Compute:
    def __init__(self, s, refs, scratch):
        self.s = s
        self.__dict__.update(refs)
        self.__dict__.update(scratch)
        self.dmid, self.dprojb, self.dmodb = self.mid, self.dshrb, self.n2b

    def row(self, index):
        return self.v[index : index + 1, :]

    def wide_mask(self, at):
        m = self.mask[at, :]
        return jnp.concatenate([m] * self.s.nc, axis=1)

    def wide(self, ref, at):
        m = ref[at, :]
        return jnp.concatenate([m] * self.s.nc, axis=1)

    def blocks(self, body, sums=0):
        s = self.s
        start = tuple(jnp.zeros((8, s.c), f32) for _ in range(sums))

        def step(index, carry):
            at = pl.ds(pl.multiple_of(index * BLK, BLK), BLK)
            parts = body(at, pl.ds(index * (BLK // s.side), BLK // s.side))
            if not sums:
                return carry
            return tuple(total + tall(part) for total, part in zip(carry, parts))

        return lax.fori_loop(0, s.rows // BLK, step, start)

    def image(self, ref, lines):
        return ref[0, lines].astype(f32).reshape(BLK, self.s.c)

    def store(self, ref, lines, values):
        ref[0, lines] = values.reshape(BLK // self.s.side, self.s.side, self.s.c).astype(ref.dtype)

    def put(self, index, total):
        self.gv[index : index + 1, :] = jnp.sum(total, axis=0, keepdims=True)

    def prepare(self):
        s = self.s
        shape = (s.side, s.side, LANE)
        side = jnp.where(self.count > 0, self.sides, 0)
        inside = (lax.broadcasted_iota(jnp.int32, shape, 0) < side) & (
            lax.broadcasted_iota(jnp.int32, shape, 1) < side
        )
        self.mask[...] = jnp.where(inside, 1.0, 0.0).astype(f32).reshape(s.rows, LANE)

        def zero_plane(index, carry):
            for pad in self.pads:
                for ch in range(s.nc):
                    pad[ch, index, 0:EDGE, :] = jnp.zeros((EDGE, LANE), f32)
                    pad[ch, index, EDGE + s.side :, :] = jnp.zeros((EDGE, LANE), f32)
            return carry

        lax.fori_loop(0, s.side + 2 * PAD, zero_plane, 0)
        for pad in self.pads:
            for ch in range(s.nc):
                for edge in list(range(PAD)) + list(range(PAD + s.side, s.side + 2 * PAD)):
                    pad[ch, edge, EDGE : EDGE + s.side, :] = jnp.zeros((s.side, LANE), f32)

        def norm(at, lines):
            x = self.image(self.x, lines)
            centred = x - lane_sum(x) * (1.0 / s.c)
            r = lax.rsqrt(lane_sum(centred * centred) * (1.0 / s.c) + norm_eps)
            self.xh1[at, :] = centred * r
            self.r1[at, :] = jnp.broadcast_to(r, (BLK, LANE))

        self.blocks(norm)

        def clear(index, carry):
            for ch in range(s.nc):
                self.gacc[ch, index] = jnp.zeros((8, LANE), f32)
            return carry

        lax.fori_loop(0, sum(s.taps), clear, 0)

    def first(self):
        s = self.s
        for ch in range(s.nc):
            self.vc[ch] = self.v[: s.nvec, ch * LANE : (ch + 1) * LANE]
        gain, shift = self.row(0), self.row(1)
        weights = [self.row(s.gate_at + l) for l in range(GATES)]

        def step(at, lines):
            n1 = self.xh1[at, :] * gain + shift
            self.n1b[at, :] = n1.astype(b16)
            for l in range(GATES):
                self.gate[l, at, :] = jnp.broadcast_to(lane_sum(n1 * weights[l]), (BLK, LANE))

        self.blocks(step)
        n1b = self.n1b[...]
        self.q[...] = mm(n1b, self.wf(0)) + self.row(2)
        ctx = mm(n1b, self.wf(1)) + self.row(3)
        m = self.mask[...]
        for ch in range(s.nc):
            part = ctx[:, ch * LANE : (ch + 1) * LANE] * m
            self.pads[0][ch, PAD : PAD + s.side, EDGE : EDGE + s.side, :] = part.reshape(
                s.side, s.side, LANE
            )

    def level(self, l, block=4):
        s = self.s
        k = 2 * l + 3
        p = l + 1
        offset = s.kernel_at + sum(s.taps[:l])
        source = self.pads[l]
        per = s.side // block

        def step(index, carry):
            ch = lax.div(index, per)
            r0 = lax.rem(index, per) * block
            acc = [None] * block
            for dc in range(-p, p + 1):
                taps = [
                    self.vc[ch, pl.ds(offset + (dr + p) * k + dc + p, 1), :]
                    for dr in range(-p, p + 1)
                ]
                for a in range(-p, block + p):
                    x = source[ch, r0 + PAD + a, pl.ds(EDGE + dc, s.side), :]
                    for o in range(max(0, a - p), min(block, a + p + 1)):
                        term = x * taps[a - o + p]
                        acc[o] = term if acc[o] is None else acc[o] + term
            for o in range(block):
                at = pl.ds(pl.multiple_of((r0 + o) * s.side, s.side), s.side)
                m = self.mask[at, :]
                value, slope = gelu_parts(acc[o])
                value = value * m
                self.gd[l][ch, r0 + o] = slope * m
                self.pads[l + 1][ch, r0 + o + PAD, EDGE : EDGE + s.side, :] = value
                term = value * self.gate[l, at, :]
                if l:
                    term = term + self.summed[ch, r0 + o]
                self.summed[ch, r0 + o] = term
            return carry

        lax.fori_loop(0, s.nc * per, step, 0)

    def pooling(self):
        s = self.s
        area = (self.sides * self.sides).astype(f32)
        for ch in range(s.nc):
            last = self.pads[LEVELS][ch, PAD : PAD + s.side, EDGE : EDGE + s.side, :]
            total = jnp.sum(tall(last.reshape(s.rows, LANE)), axis=0, keepdims=True)
            value, slope = gelu_parts(total / area)
            cols = slice(ch * LANE, (ch + 1) * LANE)
            self.pool[0, :, cols] = jnp.broadcast_to(value, (8, LANE))
            self.pool[1, :, cols] = jnp.broadcast_to(slope / area, (8, LANE))

        def step(index, carry):
            at = pl.ds(pl.multiple_of(index * s.side * 2, s.side * 2), s.side * 2)
            gate = self.gate[LEVELS, at, :]
            for ch in range(s.nc):
                cols = slice(ch * LANE, (ch + 1) * LANE)
                part = self.summed[ch, pl.ds(index * 2, 2)].reshape(2 * s.side, LANE)
                self.sumb[at, cols] = (part + gate * self.pool[0, 0:1, cols]).astype(b16)
            return carry

        lax.fori_loop(0, s.side // 2, step, 0)

    def modulate(self):
        s = self.s
        self.mod[...] = mm(self.sumb[...], self.wh()) + self.row(4)

        def mix(at, lines):
            self.mixb[at, :] = (self.q[at, :] * self.mod[at, :]).astype(b16)

        self.blocks(mix)
        self.proj[...] = mm(self.mixb[...], self.wp()) + self.row(5)
        scale, gain, shift = self.row(6), self.row(7), self.row(8)
        upscale = self.row(10)

        def norm(at, lines):
            mid = self.image(self.x, lines) + scale * self.proj[at, :]
            self.mid[at, :] = mid
            centred = mid - lane_sum(mid) * (1.0 / s.c)
            r = lax.rsqrt(lane_sum(centred * centred) * (1.0 / s.c) + norm_eps)
            xh = centred * r
            self.xh2[at, :] = xh
            self.r2[at, :] = jnp.broadcast_to(r, (BLK, LANE))
            self.n2b[at, :] = (xh * gain + shift).astype(b16)
            d_shr = self.image(self.cot, lines) * self.wide_mask(at) * upscale
            self.dshrb[at, :] = d_shr.astype(b16)
            return (d_shr,)

        (g_b2,) = self.blocks(norm, 1)
        self.put(9, g_b2)

    def feed(self, wide=256):
        s = self.s
        half = s.hid // 2
        per = half // wide
        for j in range(s.hid // wide):
            h, at = j // per, (j % per) * wide
            cols = slice(j * wide, (j + 1) * wide)
            first_row, first_col = divmod(j * wide, s.c)
            bias = []
            for start in range(j * wide, (j + 1) * wide, LANE):
                r, c = divmod(start, s.c)
                bias.append(self.v[11 + r : 12 + r, c : c + LANE])
            bias = jnp.concatenate(bias, axis=1)
            w1 = self.w1(h, at, wide)
            hid = mm(self.n2b[...], w1) + bias
            act, slope = gelu_parts(hid)
            self.actb[:, cols] = act.astype(b16)
            d_hid = mm_t(self.dshrb[...], self.w2(j * wide, wide)) * slope
            self.dhidb[:, cols] = d_hid.astype(b16)
            g_bias = jnp.sum(tall(d_hid), axis=0, keepdims=True)
            for i, start in enumerate(range(j * wide, (j + 1) * wide, LANE)):
                r, c = divmod(start, s.c)
                self.gv[11 + r : 12 + r, c : c + LANE] = g_bias[:, i * LANE : (i + 1) * LANE]

    def feed_grads(self, wide=256):
        s = self.s
        half = s.hid // 2
        for j in range(s.hid // wide):
            cols = slice(j * wide, (j + 1) * wide)
            h, at = divmod(j * wide, half)
            self.put_g2(j * wide, wide, mm_g(self.actb[:, cols], self.dshrb[...]))
            self.put_g1(h, at, wide, mm_g(self.n2b[...], self.dhidb[:, cols]))

    def feed_out(self):
        s = self.s
        half = s.hid // 2
        self.shr[...] = mm(self.actb[...], self.w2(0, s.hid)) + self.row(9)
        self.dn[...] = mm_t(self.dhidb[:, :half], self.w1(0, 0, half)) + mm_t(
            self.dhidb[:, half:], self.w1(1, 0, half)
        )

    def middle(self):
        s = self.s
        gain, scale, upscale = self.row(7), self.row(6), self.row(10)

        def step(at, lines):
            shr, mid, proj, xh = self.shr[at, :], self.mid[at, :], self.proj[at, :], self.xh2[at, :]
            m = self.wide_mask(at)
            u = self.image(self.cot, lines) * m
            self.store(self.out, lines, (mid + upscale * shr) * m)
            d = self.dn[at, :]
            e = d * gain
            mean_e = lane_sum(e) * (1.0 / s.c)
            mean_x = lane_sum(e * xh) * (1.0 / s.c)
            d_mid = u + self.wide(self.r2, at) * (e - mean_e - xh * mean_x)
            self.dmid[at, :] = d_mid
            d_proj = scale * d_mid
            self.dprojb[at, :] = d_proj.astype(b16)
            return u * shr, d * xh, d, d_mid * proj, d_proj

        sums = self.blocks(step, 5)
        for index, total in zip((10, 7, 8, 6, 5), sums):
            self.put(index, total)
        self.dn[...] = mm_t(self.dprojb[...], self.wp())

        def split(at, lines):
            d = self.dn[at, :]
            d_q = d * self.mod[at, :]
            d_mod = d * self.q[at, :]
            self.dqb[at, :] = d_q.astype(b16)
            self.dmodb[at, :] = d_mod.astype(b16)
            return d_q, d_mod

        g_bq, g_bh = self.blocks(split, 2)
        self.put(2, g_bq)
        self.put(4, g_bh)
        d_sum = mm_t(self.dmodb[...], self.wh())
        for ch in range(s.nc):
            self.dsum[ch] = d_sum[:, ch * LANE : (ch + 1) * LANE]

    def middle_grads(self):
        self.put_gp(mm_g(self.mixb[...], self.dprojb[...]))
        self.put_gh(mm_g(self.sumb[...], self.dmodb[...]))

    def focal_top(self):
        s = self.s

        def step(index, carry):
            at = pl.ds(pl.multiple_of(index * s.side * 2, s.side * 2), s.side * 2)
            gate = self.gate[LEVELS, at, :]
            sums = [jnp.zeros((2 * s.side, LANE), f32) for _ in range(GATES)]
            out = []
            for ch in range(s.nc):
                cols = slice(ch * LANE, (ch + 1) * LANE)
                d = self.dsum[ch, at, :]
                values = [
                    self.pads[l][ch, pl.ds(index * 2 + PAD, 2), EDGE : EDGE + s.side, :]
                    for l in range(1, LEVELS + 1)
                ]
                for l in range(LEVELS):
                    sums[l] = sums[l] + d * values[l].reshape(2 * s.side, LANE)
                sums[LEVELS] = sums[LEVELS] + d * self.pool[0, 0:1, cols]
                out.append(carry[ch] + tall(d * gate))
            for l in range(GATES):
                self.dgate[l, at, :] = jnp.broadcast_to(
                    jnp.sum(sums[l], axis=1, keepdims=True), (2 * s.side, LANE)
                )
            return tuple(out)

        zero = jnp.zeros((8, LANE), f32)
        totals = lax.fori_loop(0, s.side // 2, step, (zero,) * s.nc)
        for ch in range(s.nc):
            cols = slice(ch * LANE, (ch + 1) * LANE)
            total = jnp.sum(totals[ch], axis=0, keepdims=True)
            self.pool[1, :, cols] = self.pool[1, :, cols] * total

        def last(index, carry):
            at = pl.ds(pl.multiple_of(index * s.side * 2, s.side * 2), s.side * 2)
            gate = self.gate[LEVELS - 1, at, :]
            for ch in range(s.nc):
                cols = slice(ch * LANE, (ch + 1) * LANE)
                e = self.dsum[ch, at, :] * gate + self.pool[1, 0:1, cols]
                d = e.reshape(2, s.side, LANE) * self.gd[LEVELS - 1][ch, pl.ds(index * 2, 2)]
                self.pads[LEVELS][ch, pl.ds(index * 2 + PAD, 2), EDGE : EDGE + s.side, :] = d
            return carry

        lax.fori_loop(0, s.side // 2, last, 0)

    def level_back(self, l, block=4):
        s = self.s
        k = 2 * l + 3
        p = l + 1
        base = sum(s.taps[:l])
        offset = s.kernel_at + base
        source = self.pads[l + 1]
        inputs = self.pads[l]
        per = s.side // block

        def step(index, carry):
            ch = lax.div(index, per)
            r0 = lax.rem(index, per) * block
            acc = [None] * block
            xs = [
                inputs[ch, r0 + PAD + o, EDGE : EDGE + s.side, :] for o in range(block)
            ]
            for dc in range(-p, p + 1):
                taps = [
                    self.vc[ch, pl.ds(offset + (dr + p) * k + dc + p, 1), :]
                    for dr in range(-p, p + 1)
                ]
                sums = [None] * k
                for a in range(-p, block + p):
                    d = source[ch, r0 + PAD + a, pl.ds(EDGE - dc, s.side), :]
                    for o in range(max(0, a - p), min(block, a + p + 1)):
                        dr = o - a
                        term = d * taps[dr + p]
                        acc[o] = term if acc[o] is None else acc[o] + term
                        part = tall(d * xs[o])
                        sums[dr + p] = part if sums[dr + p] is None else sums[dr + p] + part
                for dr in range(-p, p + 1):
                    tap = base + (dr + p) * k + dc + p
                    self.gacc[ch, tap] = self.gacc[ch, tap] + sums[dr + p]
            total = None
            for o in range(block):
                at = pl.ds(pl.multiple_of((r0 + o) * s.side, s.side), s.side)
                if l:
                    e = acc[o] + self.dsum[ch, at, :] * self.gate[l - 1, at, :]
                    self.pads[l][ch, r0 + o + PAD, EDGE : EDGE + s.side, :] = (
                        e * self.gd[l - 1][ch, r0 + o]
                    )
                else:
                    self.summed[ch, r0 + o] = acc[o] * self.mask[at, :]
            return carry

        lax.fori_loop(0, s.nc * per, step, 0)

    def focal_end(self):
        s = self.s

        def step(index, carry):
            at = pl.ds(pl.multiple_of(index * s.side * 2, s.side * 2), s.side * 2)
            out = []
            for ch in range(s.nc):
                cols = slice(ch * LANE, (ch + 1) * LANE)
                d = self.summed[ch, pl.ds(index * 2, 2)].reshape(2 * s.side, LANE)
                self.dctxb[at, cols] = d.astype(b16)
                out.append(carry[ch] + tall(d))
            return tuple(out)

        zero = jnp.zeros((8, LANE), f32)
        totals = lax.fori_loop(0, s.side // 2, step, (zero,) * s.nc)
        for ch in range(s.nc):
            cols = slice(ch * LANE, (ch + 1) * LANE)
            self.gv[3:4, cols] = jnp.sum(totals[ch], axis=0, keepdims=True)
            self.gv[s.kernel_at : s.nvec, cols] = jnp.sum(self.gacc[ch], axis=1)

    def last_grads(self):
        n1b = self.n1b[...]
        self.put_gf(0, mm_g(n1b, self.dqb[...]))
        self.put_gf(1, mm_g(n1b, self.dctxb[...]))

    def last_back(self):
        s = self.s
        self.dn[...] = mm_t(self.dqb[...], self.wf(0)) + mm_t(self.dctxb[...], self.wf(1))
        gain, shift = self.row(0), self.row(1)
        weights = [self.row(s.gate_at + l) for l in range(GATES)]

        def step(at, lines):
            xh = self.xh1[at, :]
            n1 = xh * gain + shift
            d = self.dn[at, :]
            sums = []
            for l in range(GATES):
                dg = self.wide(self.dgate.at[l], at)
                d = d + dg * weights[l]
                sums.append(dg * n1)
            e = d * gain
            mean_e = lane_sum(e) * (1.0 / s.c)
            mean_x = lane_sum(e * xh) * (1.0 / s.c)
            d_in = self.dmid[at, :] + self.wide(self.r1, at) * (e - mean_e - xh * mean_x)
            self.store(self.grad, lines, d_in)
            return (d * xh, d) + tuple(sums)

        sums = self.blocks(step, 2 + GATES)
        for index, total in zip((0, 1) + tuple(s.gate_at + l for l in range(GATES)), sums):
            self.put(index, total)

    def run(self):
        self.prepare()
        self.first()
        for l in range(LEVELS):
            self.level(l)
        self.pooling()
        self.modulate()
        self.feed()
        self.feed_grads()
        self.feed_out()
        self.middle()
        self.middle_grads()
        self.focal_top()
        for l in reversed(range(LEVELS)):
            self.level_back(l)
        self.focal_end()
        self.last_grads()
        self.last_back()


MESH = pl.DeviceIdType.MESH
STEP = 10
TENSORS = 6
beta_one = 0.9
beta_two = 0.95
adam_eps = 1e-08
weight_decay = 0.05
VMEM_BYTES = 63 * 2**20 + 2**19


class Plan:
    def __init__(self, n_grp, n_fs, s):
        self.X = n_grp // 2
        self.Y = 2 ** (int(math.log2(n_fs)) // 2)
        self.Z = n_fs // self.Y
        self.fs = n_fs
        self.s = s
        self.rows = s.c // n_fs
        self.rp = -(-self.rows // 16) * 16
        self.rows2 = s.hid // n_fs // 2
        self.rp2 = -(-self.rows2 // 16) * 16
        self.rv = self.rp // 2
        half = s.c
        self.pieces = {
            "f": (self.rp, half, b16),
            "v": (self.rv, LANE, f32),
            "m": (self.rp, half, b16),
            "e": (self.rp, s.hid // 2, b16),
            "s": (self.rp2, s.c, b16),
        }

    def whole(self, name):
        rows, cols, kind = self.pieces[name]
        if name in "sv":
            return (self.Z, self.Y, 2, rows, cols)
        return (2, self.Z, self.Y, rows, cols)


def comm_scratch(p):
    out = {}
    for name, (rows, cols, kind) in p.pieces.items():
        out[name] = dict(
            cand=pltpu.VMEM((2, rows, cols), kind),
            rx1=pltpu.VMEM((rows, cols), kind),
            sel=pltpu.VMEM((rows, cols), kind),
            rx2=pltpu.VMEM((p.X - 1, rows, cols), kind),
            full=pltpu.VMEM(p.whole(name), kind),
            grad=pltpu.VMEM(p.whole(name), kind),
            r1=pltpu.VMEM((p.Z, p.Y, rows, cols), kind),
            r2=pltpu.VMEM((p.Y - 1, p.Z, rows, cols), kind),
            a2=pltpu.VMEM((p.Z, rows, cols), kind),
            r3=pltpu.VMEM((p.Z - 1, rows, cols), kind),
            a3=pltpu.VMEM((rows, cols), kind),
            r4=pltpu.VMEM((p.X - 1, rows, cols), kind),
            a4=pltpu.VMEM((rows, cols), f32),
            r5=pltpu.VMEM((rows, cols), f32),
        )
    return out


def sem_count(p):
    per = 1 + (p.X - 1) + (p.Z - 1) + p.Z * (p.Y - 1) + p.fs
    per += 1 + (p.Y - 1) + (p.Z - 1) + (p.X - 1) + 1
    return per * len(p.pieces)


class Links:
    def __init__(self, p, send_sem, recv_sem):
        self.p = p
        self.send_sem, self.recv_sem = send_sem, recv_sem
        self.used = 0
        self.sent = []
        self.g, self.f = lax.axis_index("grp"), lax.axis_index("fs")
        self.x, self.c = lax.div(self.g, 2), lax.rem(self.g, 2)
        self.z, self.y = lax.div(self.f, p.Y), lax.rem(self.f, p.Y)

    def sibling(self):
        return (self.x * 2 + 1 - self.c, self.f)

    def by_x(self, d):
        return (lax.rem(self.x + d, self.p.X) * 2 + self.c, self.f)

    def by_z(self, d):
        return (self.g, lax.rem(self.z + d, self.p.Z) * self.p.Y + self.y)

    def by_y(self, d):
        return (self.g, self.z * self.p.Y + lax.rem(self.y + d, self.p.Y))

    def partners(self):
        p = self.p
        return (
            [self.sibling()]
            + [self.by_x(d) for d in range(1, p.X)]
            + [self.by_z(d) for d in range(1, p.Z)]
            + [self.by_y(d) for d in range(1, p.Y)]
        )

    def barrier(self):
        sem = pltpu.get_barrier_semaphore()
        partners = self.partners()
        for partner in partners:
            pl.semaphore_signal(sem, inc=1, device_id=partner, device_id_type=MESH)
        pl.semaphore_wait(sem, len(partners))

    def send(self, source, target, partner, arriving=None):
        index = self.used
        self.used += 1

        def copy(src, dst):
            return pltpu.make_async_remote_copy(
                src_ref=src,
                dst_ref=dst,
                send_sem=self.send_sem.at[index],
                recv_sem=self.recv_sem.at[index],
                device_id=partner,
                device_id_type=MESH,
            )

        started = copy(source, target)
        started.start()
        self.sent.append(started)
        coming = copy(source, target if arriving is None else arriving)
        return coming.wait_recv

    def finish(self):
        for copy in self.sent:
            copy.wait_send()


class Gather:
    def __init__(self, name, links, refs):
        self.name, self.links, self.p = name, links, links.p
        self.__dict__.update(refs)

    def piece(self, half, z, y):
        return self.full.at[z, y, half] if self.name in "sv" else self.full.at[half, z, y]

    def core_send(self, z, y):
        k = self.links
        here = self.piece(k.c, z, y)
        return k.send(here, here, k.sibling(), self.piece(1 - k.c, z, y))

    def one(self):
        k = self.links
        self.wait1 = k.send(self.cand.at[1 - k.c], self.rx1, k.sibling())

    def two(self):
        k, p = self.links, self.p
        self.wait1()
        self.sel[...] = self.cand[k.c] + self.rx1[...]
        self.wait2 = [
            k.send(self.sel, self.rx2.at[d - 1], k.by_x(d)) for d in range(1, p.X)
        ]

    def y_sends(self, z):
        k, p = self.links, self.p
        here = self.piece(k.c, z, k.y)
        for d in range(1, p.Y):
            other = lax.rem(k.y + p.Y - d, p.Y)
            wait = k.send(here, here, k.by_y(d), self.piece(k.c, z, other))
            self.wait4.append((wait, z, other))

    def three(self):
        k, p = self.links, self.p
        for wait in self.wait2:
            wait()
        total = self.sel[...]
        for d in range(p.X - 1):
            total = total + self.rx2[d]
        self.piece(k.c, k.z, k.y)[...] = total
        here = self.piece(k.c, k.z, k.y)
        self.wait3, self.wait4, self.wait5 = [], [], []
        for d in range(1, p.Z):
            other = lax.rem(k.z + p.Z - d, p.Z)
            wait = k.send(here, here, k.by_z(d), self.piece(k.c, other, k.y))
            self.wait3.append((wait, other))
        self.y_sends(k.z)
        self.wait5.append(self.core_send(k.z, k.y))

    def four(self):
        k = self.links
        for wait, z in self.wait3:
            wait()
            self.y_sends(z)
            self.wait5.append(self.core_send(z, k.y))

    def five(self):
        for wait, z, y in self.wait4:
            wait()
            self.wait5.append(self.core_send(z, y))

    def six(self):
        for wait in self.wait5:
            wait()


class Reduce:
    def __init__(self, name, links, refs, result):
        self.name, self.links, self.p = name, links, links.p
        self.__dict__.update(refs)
        self.result = result

    def half(self, h):
        return self.grad.at[:, :, h] if self.name in "sv" else self.grad.at[h]

    def one(self):
        k = self.links
        self.wait1 = k.send(self.half(1 - k.c), self.r1, k.sibling())

    def two(self):
        k, p = self.links, self.p
        self.wait1()
        mine = self.half(k.c)

        def add(index, carry):
            z, y = lax.div(index, p.Y), lax.rem(index, p.Y)
            self.r1[z, y] = self.r1[z, y] + mine[z, y]
            return carry

        lax.fori_loop(0, p.fs, add, 0)
        self.wait2 = [
            k.send(self.r1.at[:, lax.rem(k.y + d, p.Y)], self.r2.at[d - 1], k.by_y(d))
            for d in range(1, p.Y)
        ]

    def three(self):
        k, p = self.links, self.p
        for wait in self.wait2:
            wait()

        def add(z, carry):
            total = self.r1[z, k.y].astype(f32)
            for d in range(p.Y - 1):
                total = total + self.r2[d, z].astype(f32)
            self.a2[z] = total.astype(self.a2.dtype)
            return carry

        lax.fori_loop(0, p.Z, add, 0)
        self.wait3 = [
            k.send(self.a2.at[lax.rem(k.z + d, p.Z)], self.r3.at[d - 1], k.by_z(d))
            for d in range(1, p.Z)
        ]

    def four(self):
        k, p = self.links, self.p
        for wait in self.wait3:
            wait()
        total = self.a2[k.z].astype(f32)
        for d in range(p.Z - 1):
            total = total + self.r3[d].astype(f32)
        self.a3[...] = total.astype(self.a3.dtype)
        self.wait4 = [
            k.send(self.a3, self.r4.at[d - 1], k.by_x(d)) for d in range(1, p.X)
        ]

    def five(self):
        k, p = self.links, self.p
        for wait in self.wait4:
            wait()
        total = self.a3[...].astype(f32)
        for d in range(p.X - 1):
            total = total + self.r4[d].astype(f32)
        self.a4[...] = total
        self.result[k.c] = total
        self.wait5 = k.send(self.a4, self.r5, k.sibling())

    def six(self):
        k = self.links
        self.wait5()
        self.result[1 - k.c] = self.r5[...]


def spread_matrix(rows, rp, count):
    bits = int(math.log2(rp))
    shape = (count * rows, count * rp)
    a = lax.broadcasted_iota(jnp.int32, shape, 0)
    b = lax.broadcasted_iota(jnp.int32, shape, 1)
    i = lax.bitwise_and(b, rp - 1)
    hit = (a == lax.shift_right_logical(b, bits) * rows + i) & (i < rows)
    return jnp.where(hit, 1.0, 0.0).astype(b16)


def block_kernel(p, tree, *refs):
    s = p.s
    (count, sides, owners, x, cot, wf, wh, wp, w1, w2, v_own) = refs[:11]
    (out, grad, fin_f, fin_v, fin_m, fin_e, fin_s) = refs[11:18]
    own = jax.tree.unflatten(tree, refs[18:])
    comm = own["comm"]
    k = Links(p, own["send_sem"], own["recv_sem"])
    even = p.rp == p.rows and p.rp2 == p.rows2

    def mine(index):
        return jnp.where(owners[index] == k.g, 1.0, 0.0).astype(f32)

    def cut(values, rows, rp):
        if rows == rp:
            return values
        return jnp.concatenate([values, jnp.zeros((rp - rows, values.shape[1]), f32)], axis=0)

    half, wide = s.c, s.hid // 2
    for name, parts in (
        ("f", ((0, wf, 0, 0), (0, wf, 0, half))),
        ("m", ((1, wh, 0, 0), (2, wp, 0, 0))),
        ("e", ((3, w1, 0, 0), (3, w1, 0, wide))),
        ("s", ((4, w2, 0, 0), (4, w2, p.rows2, 0))),
    ):
        rp, cols, kind = p.pieces[name]
        rows = p.rows2 if name == "s" else p.rows
        for h, (index, ref, row, col) in enumerate(parts):
            values = ref[0, row : row + rows, col : col + cols] * mine(index)
            comm[name]["cand"][h] = cut(values, rows, rp).astype(kind)
    values = cut(v_own[0] * mine(5), p.rows, p.rp)
    values = jnp.concatenate([values, jnp.zeros((p.rp, LANE - s.nvec), f32)], axis=1)
    for h in range(2):
        comm["v"]["cand"][h] = values[h * p.rv : (h + 1) * p.rv]

    k.barrier()
    order = ("f", "v", "m", "e", "s")
    gathers = [Gather(name, k, comm[name]) for name in order]
    for stage in ("one", "two", "three", "four", "five", "six"):
        for gather in gathers:
            getattr(gather, stage)()

    full = {name: comm[name]["full"] for name in order}
    if not even:
        own["map"][...] = spread_matrix(p.rows, p.rp, p.fs)

    vector = full["v"][...].reshape(p.fs * p.rp, LANE)
    if not even:
        vector = jnp.dot(own["map"][...].astype(f32), vector, precision=lax.Precision.HIGHEST)
    own["v"][...] = vector.T

    def compact(values):
        return values if even else mm(own["map"][...], values).astype(b16)

    def spread(values):
        values = values.astype(b16)
        return values if even else mm_g(own["map"][...], values).astype(b16)

    def matrix(name, h, at, cols):
        part = full[name][h, :, :, :, at : at + cols]
        return compact(part.reshape(p.fs * p.rp, cols))

    if even:
        shrink = full["s"]

        def take_shrink(at, rows):
            return shrink[...].reshape(s.hid, s.c)[at : at + rows]
    else:
        def close(f, carry):
            z, y = lax.div(f, p.Y), lax.rem(f, p.Y)
            parts = [full["s"][z, y, h].astype(f32)[: p.rows2] for h in range(2)]
            at = pl.ds(pl.multiple_of(f * 2 * p.rows2, 2 * p.rows2), 2 * p.rows2)
            own["w2n"][at, :] = jnp.concatenate(parts, axis=0).astype(b16)
            return carry

        lax.fori_loop(0, p.fs, close, 0)

        def take_shrink(at, rows):
            return own["w2n"][at : at + rows, :]

    def put(name, h, at, values):
        cols = values.shape[1]
        grads = spread(values).reshape(p.Z, p.Y, p.rp, cols)
        comm[name]["grad"][h, :, :, :, at : at + cols] = grads

    def put_shrink(at, rows, values):
        if even:
            low = values.astype(b16)
            start = at
            while start < at + rows:
                piece = start // p.rp2
                inner = start - piece * p.rp2
                size = min(p.rp2 - inner, at + rows - start)
                f, h = piece // 2, piece % 2
                comm["s"]["grad"][f // p.Y, f % p.Y, h, inner : inner + size, :] = low[
                    start - at : start - at + size
                ]
                start += size
        else:
            own["g2n"][at : at + rows, :] = values.astype(b16)

    refs = dict(
        x=x,
        cot=cot,
        v=own["v"],
        count=count[0, 0],
        sides=sides[0],
        out=out,
        grad=grad,
        gv=own["gv"],
        wf=lambda h: matrix("f", h, 0, half),
        wh=lambda: matrix("m", 0, 0, s.c),
        wp=lambda: matrix("m", 1, 0, s.c),
        w1=lambda h, at, cols: matrix("e", h, at, cols),
        w2=take_shrink,
        put_gf=lambda h, values: put("f", h, 0, values),
        put_gh=lambda values: put("m", 0, 0, values),
        put_gp=lambda values: put("m", 1, 0, values),
        put_g1=lambda h, at, cols, values: put("e", h, at, values),
        put_g2=put_shrink,
    )
    own["gv"][s.nvec :, :] = jnp.zeros((LANE - s.nvec, s.c), f32)
    block = Compute(s, refs, own["compute"])
    block.run()

    if not even:

        def open_up(f, carry):
            z, y = lax.div(f, p.Y), lax.rem(f, p.Y)
            at = pl.ds(pl.multiple_of(f * 2 * p.rows2, 2 * p.rows2), 2 * p.rows2)
            both = own["g2n"][at, :].astype(f32)
            for h in range(2):
                part = cut(both[h * p.rows2 : (h + 1) * p.rows2], p.rows2, p.rp2)
                comm["s"]["grad"][z, y, h] = part.astype(b16)
            return carry

        lax.fori_loop(0, p.fs, open_up, 0)
    grads = own["gv"][...].T
    if not even:
        grads = lax.dot_general(
            own["map"][...].astype(f32),
            grads,
            (((0,), (0,)), ((), ())),
            precision=lax.Precision.HIGHEST,
        )
    comm["v"]["grad"][...] = grads.reshape(p.whole("v"))
    results = dict(f=fin_f, v=fin_v, m=fin_m, e=fin_e, s=fin_s)
    reduces = [Reduce(name, k, comm[name], results[name]) for name in ("s", "e", "m", "f", "v")]
    for stage in ("one", "two", "three", "four", "five", "six"):
        for reduce in reduces:
            getattr(reduce, stage)()
    k.finish()


def adam_kernel(p, rates, *refs):
    s = p.s
    owners = refs[0]
    fins = dict(zip("fvmes", refs[1:6]))
    olds, news = refs[6:24], refs[24:42]
    g = lax.axis_index("grp")
    half, wide = s.c, s.hid // 2
    parts = (
        [("f", h, 0, p.rows, h * half, half) for h in range(2)],
        [("m", 0, 0, p.rows, 0, s.c)],
        [("m", 1, 0, p.rows, 0, s.c)],
        [("e", h, 0, p.rows, h * wide, wide) for h in range(2)],
        [("s", h, h * p.rows2, p.rows2, 0, s.c) for h in range(2)],
        [
            ("v", h, h * p.rv, min(p.rows - h * p.rv, p.rv), 0, s.nvec)
            for h in range(2)
        ],
    )
    for index, pieces in enumerate(parts):
        keep = owners[index] == g
        scale = jnp.where(keep, 1.0, 0.0).astype(f32)
        for name, h, row, rows, col, cols in pieces:
            at = (0, slice(row, row + rows), slice(col, col + cols))
            gradient = fins[name][h, :rows, :cols]
            weight, first, second = (olds[3 * index + i][at] for i in range(3))
            first_new = beta_one * first + (1.0 - beta_one) * gradient
            second_new = beta_two * second + (1.0 - beta_two) * gradient * gradient
            first_hat = first_new / (1.0 - beta_one**STEP)
            second_hat = second_new / (1.0 - beta_two**STEP)
            weight_new = weight - rates[index] * (
                first_hat / (jnp.sqrt(second_hat) + adam_eps) + weight_decay * weight
            )
            for i, value in enumerate((weight_new, first_new, second_new)):
                news[3 * index + i][at] = value * scale


def solution(mesh):
    n_grp, n_fs = mesh.shape["grp"], mesh.shape["fs"]

    def shards(image_patches, cotangent, image_count, resolution, owner_list, *tensors):
        side, channels = image_patches.shape[1], image_patches.shape[3]
        hid = tensors[9].shape[2]
        s = Shape(side, channels, hid)
        p = Plan(n_grp, n_fs, s)
        even = p.rp == p.rows and p.rp2 == p.rows2
        scratch = dict(
            comm=comm_scratch(p),
            compute=compute_scratch(s),
            v=pltpu.VMEM((LANE, s.c), f32),
            gv=pltpu.VMEM((LANE, s.c), f32),
            send_sem=pltpu.SemaphoreType.DMA((sem_count(p),)),
            recv_sem=pltpu.SemaphoreType.DMA((sem_count(p),)),
        )
        if not even:
            scratch["map"] = pltpu.VMEM((s.c, p.fs * p.rp), b16)
            scratch["w2n"] = pltpu.VMEM((s.hid, s.c), b16)
            scratch["g2n"] = pltpu.VMEM((s.hid, s.c), b16)
        leaves, tree = jax.tree.flatten(scratch, is_leaf=lambda v: not isinstance(v, (dict, list)))
        vmem = pl.BlockSpec(memory_space=pltpu.VMEM)
        smem = pl.BlockSpec(memory_space=pltpu.SMEM)
        shape = jax.ShapeDtypeStruct
        fins = [shape((2,) + p.pieces[name][:2], f32) for name in "fvmes"]
        tensors = tensors[:15] + tuple(t.transpose(0, 2, 1) for t in tensors[15:])
        results = pl.pallas_call(
            lambda *refs: block_kernel(p, tree, *refs),
            out_shape=[shape(image_patches.shape, b16), shape(image_patches.shape, f32)] + fins,
            in_specs=[smem] * 3 + [vmem] * 8,
            out_specs=[vmem] * 7,
            scratch_shapes=leaves,
            compiler_params=pltpu.CompilerParams(
                collective_id=0, has_side_effects=True, vmem_limit_bytes=VMEM_BYTES
            ),
            name="block",
        )(
            image_count,
            resolution,
            owner_list,
            image_patches,
            cotangent,
            tensors[0],
            tensors[3],
            tensors[6],
            tensors[9],
            tensors[12],
            tensors[15],
        )
        wide_rate = 1.5 / math.sqrt(channels)
        rates = (wide_rate,) * 4 + (1.5 / math.sqrt(hid), 0.2)
        news = pl.pallas_call(
            lambda *refs: adam_kernel(p, rates, *refs),
            out_shape=[shape(t.shape, f32) for t in tensors],
            in_specs=[smem] + [vmem] * 23,
            out_specs=[vmem] * 18,
            compiler_params=pltpu.CompilerParams(vmem_limit_bytes=VMEM_BYTES),
            name="adam",
        )(owner_list, *results[2:], *tensors)
        news = tuple(news[:15]) + tuple(t.transpose(0, 2, 1) for t in news[15:])
        return tuple(results[:2]) + news

    images = P(("grp", "fs"), None, None, None)
    weights = (P("grp", "fs", None),) * 15 + (P("grp", None, "fs"),) * 3
    return jax.shard_map(
        shards,
        mesh=mesh,
        in_specs=(images, images, P("grp", "fs"), P(("grp", "fs")), P()) + weights,
        out_specs=(images, images) + weights,
        check_vma=False,
    )
```

```python
import math

import jax
import jax.numpy as jnp
from jax import lax
from jax.experimental import pallas as pl
from jax.experimental.pallas import tpu as pltpu
from jax.sharding import PartitionSpec as P

f32 = jnp.float32
b16 = jnp.bfloat16
LEVELS = 3
GATES = 4
LANE = 128
norm_eps = 1e-05
PAD = 3
EDGE = 8
SQRT_HALF = math.sqrt(0.5)
INV_SQRT_2PI = 1.0 / math.sqrt(2.0 * math.pi)
BLK = 192


def gelu_parts(z):
    az = jnp.abs(z)
    t = 1.0 / (1.0 + (0.3275911 * SQRT_HALF) * az)
    e = jnp.exp(z * z * -0.5)
    poly = t * (
        0.5 * 0.254829592
        + t * (0.5 * -0.284496736 + t * (0.5 * 1.421413741 + t * (0.5 * -1.453152027 + t * (0.5 * 1.061405429))))
    )
    tail = poly * e
    phi = jnp.where(z >= 0.0, 1.0 - tail, tail)
    return z * phi, phi + z * e * INV_SQRT_2PI


def mm(a, b):
    return jnp.dot(a, b, preferred_element_type=f32)


def mm_t(a, b):
    return lax.dot_general(a, b, (((1,), (1,)), ((), ())), preferred_element_type=f32)


def mm_g(a, b):
    return lax.dot_general(a, b, (((0,), (0,)), ((), ())), preferred_element_type=f32)


def tall(values):
    rows, cols = values.shape
    return jnp.sum(values.reshape(rows // 8, 8, cols), axis=0)


def lane_sum(values):
    parts = values[:, :LANE]
    for start in range(LANE, values.shape[1], LANE):
        parts = parts + values[:, start : start + LANE]
    return jnp.sum(parts, axis=1, keepdims=True)


class Shape:
    def __init__(self, side, channels, hid):
        self.side = side
        self.rows = side * side
        self.c = channels
        self.nc = channels // LANE
        self.hid = hid
        self.bias_rows = hid // channels
        self.gate_at = 11 + self.bias_rows
        self.kernel_at = self.gate_at + GATES
        self.taps = [(2 * n + 3) ** 2 for n in range(LEVELS)]
        self.nvec = self.kernel_at + sum(self.taps)
        self.padded = (self.nc, side + 2 * PAD, side + 2 * EDGE, LANE)


def compute_scratch(s):
    flat = (s.rows, s.c)
    split = (s.nc, s.rows, LANE)
    grid = (s.nc, s.side, s.side, LANE)
    return dict(
        vc=pltpu.VMEM((s.nc, s.nvec, LANE), f32),
        mask=pltpu.VMEM((s.rows, LANE), f32),
        xh1=pltpu.VMEM(flat, f32),
        r1=pltpu.VMEM((s.rows, LANE), f32),
        n1b=pltpu.VMEM(flat, b16),
        gate=pltpu.VMEM((GATES, s.rows, LANE), f32),
        q=pltpu.VMEM(flat, f32),
        pads=[pltpu.VMEM(s.padded, f32) for _ in range(LEVELS + 1)],
        gd=[pltpu.VMEM(grid, f32) for _ in range(LEVELS)],
        summed=pltpu.VMEM(grid, f32),
        sumb=pltpu.VMEM(flat, b16),
        mod=pltpu.VMEM(flat, f32),
        mixb=pltpu.VMEM(flat, b16),
        proj=pltpu.VMEM(flat, f32),
        mid=pltpu.VMEM(flat, f32),
        xh2=pltpu.VMEM(flat, f32),
        r2=pltpu.VMEM((s.rows, LANE), f32),
        n2b=pltpu.VMEM(flat, b16),
        dshrb=pltpu.VMEM(flat, b16),
        actb=pltpu.VMEM((s.rows, s.hid), b16),
        dhidb=pltpu.VMEM((s.rows, s.hid), b16),
        shr=pltpu.VMEM(flat, f32),
        dn=pltpu.VMEM(flat, f32),
        dqb=pltpu.VMEM(flat, b16),
        dsum=pltpu.VMEM(split, f32),
        dgate=pltpu.VMEM((GATES, s.rows, LANE), f32),
        dctxb=pltpu.VMEM(flat, b16),
        gacc=pltpu.VMEM((s.nc, sum(s.taps), 8, LANE), f32),
        pool=pltpu.VMEM((2, 8, s.c), f32),
    )


class Compute:
    def __init__(self, s, refs, scratch):
        self.s = s
        self.__dict__.update(refs)
        self.__dict__.update(scratch)
        self.dmid, self.dprojb, self.dmodb = self.mid, self.dshrb, self.n2b

    def row(self, index):
        return self.v[index : index + 1, :]

    def wide_mask(self, at):
        m = self.mask[at, :]
        return jnp.concatenate([m] * self.s.nc, axis=1)

    def wide(self, ref, at):
        m = ref[at, :]
        return jnp.concatenate([m] * self.s.nc, axis=1)

    def blocks(self, body, sums=0):
        s = self.s
        start = tuple(jnp.zeros((8, s.c), f32) for _ in range(sums))

        def step(index, carry):
            at = pl.ds(pl.multiple_of(index * BLK, BLK), BLK)
            parts = body(at, pl.ds(index * (BLK // s.side), BLK // s.side))
            if not sums:
                return carry
            return tuple(total + tall(part) for total, part in zip(carry, parts))

        return lax.fori_loop(0, s.rows // BLK, step, start)

    def image(self, ref, lines):
        return ref[lines].astype(f32).reshape(BLK, self.s.c)

    def store(self, ref, lines, values):
        ref[lines] = values.reshape(BLK // self.s.side, self.s.side, self.s.c).astype(ref.dtype)

    def put(self, index, total):
        self.gv[index : index + 1, :] = jnp.sum(total, axis=0, keepdims=True)

    def prepare(self):
        s = self.s
        shape = (s.side, s.side, LANE)
        side = jnp.where(self.count > 0, self.sides, 0)
        inside = (lax.broadcasted_iota(jnp.int32, shape, 0) < side) & (
            lax.broadcasted_iota(jnp.int32, shape, 1) < side
        )
        self.mask[...] = jnp.where(inside, 1.0, 0.0).astype(f32).reshape(s.rows, LANE)

        def zero_plane(index, carry):
            for pad in self.pads:
                for ch in range(s.nc):
                    pad[ch, index, 0:EDGE, :] = jnp.zeros((EDGE, LANE), f32)
                    pad[ch, index, EDGE + s.side :, :] = jnp.zeros((EDGE, LANE), f32)
            return carry

        lax.fori_loop(0, s.side + 2 * PAD, zero_plane, 0)
        for pad in self.pads:
            for ch in range(s.nc):
                for edge in list(range(PAD)) + list(range(PAD + s.side, s.side + 2 * PAD)):
                    pad[ch, edge, EDGE : EDGE + s.side, :] = jnp.zeros((s.side, LANE), f32)

        def norm(at, lines):
            x = self.image(self.x, lines)
            centred = x - lane_sum(x) * (1.0 / s.c)
            r = lax.rsqrt(lane_sum(centred * centred) * (1.0 / s.c) + norm_eps)
            self.xh1[at, :] = centred * r
            self.r1[at, :] = jnp.broadcast_to(r, (BLK, LANE))

        self.blocks(norm)

        def clear(index, carry):
            for ch in range(s.nc):
                self.gacc[ch, index] = jnp.zeros((8, LANE), f32)
            return carry

        lax.fori_loop(0, sum(s.taps), clear, 0)

    def first(self):
        s = self.s
        for ch in range(s.nc):
            self.vc[ch] = self.v[: s.nvec, ch * LANE : (ch + 1) * LANE]
        gain, shift = self.row(0), self.row(1)
        weights = [self.row(s.gate_at + l) for l in range(GATES)]

        def step(at, lines):
            n1 = self.xh1[at, :] * gain + shift
            self.n1b[at, :] = n1.astype(b16)
            for l in range(GATES):
                self.gate[l, at, :] = jnp.broadcast_to(lane_sum(n1 * weights[l]), (BLK, LANE))

        self.blocks(step)

    def context(self, chunks):
        s = self.s
        lanes = slice(chunks[0] * LANE, (chunks[-1] + 1) * LANE)
        ctx = mm(self.n1b[...], self.wc(chunks)) + self.v[3:4, lanes]
        m = self.mask[...]
        for i, ch in enumerate(chunks):
            part = ctx[:, i * LANE : (i + 1) * LANE] * m
            self.pads[0][ch, PAD : PAD + s.side, EDGE : EDGE + s.side, :] = part.reshape(
                s.side, s.side, LANE
            )

    def query(self):
        self.q[...] = mm(self.n1b[...], self.wq()) + self.row(2)

    def level(self, l, chunks, block=6):
        s = self.s
        k = 2 * l + 3
        p = l + 1
        offset = s.kernel_at + sum(s.taps[:l])
        source = self.pads[l]
        per = s.side // block

        def step(index, carry):
            ch = chunks[0] + lax.div(index, per)
            r0 = lax.rem(index, per) * block
            acc = [None] * block
            for dc in range(-p, p + 1):
                taps = [
                    self.vc[ch, pl.ds(offset + (dr + p) * k + dc + p, 1), :]
                    for dr in range(-p, p + 1)
                ]
                for a in range(-p, block + p):
                    x = source[ch, r0 + PAD + a, pl.ds(EDGE + dc, s.side), :]
                    for o in range(max(0, a - p), min(block, a + p + 1)):
                        term = x * taps[a - o + p]
                        acc[o] = term if acc[o] is None else acc[o] + term
            for o in range(block):
                at = pl.ds(pl.multiple_of((r0 + o) * s.side, s.side), s.side)
                m = self.mask[at, :]
                value, slope = gelu_parts(acc[o])
                value = value * m
                self.gd[l][ch, r0 + o] = slope * m
                self.pads[l + 1][ch, r0 + o + PAD, EDGE : EDGE + s.side, :] = value
                term = value * self.gate[l, at, :]
                if l:
                    term = term + self.summed[ch, r0 + o]
                self.summed[ch, r0 + o] = term
            return carry

        lax.fori_loop(0, len(chunks) * per, step, 0)

    def pooling(self):
        s = self.s
        area = (self.sides * self.sides).astype(f32)
        for ch in range(s.nc):
            last = self.pads[LEVELS][ch, PAD : PAD + s.side, EDGE : EDGE + s.side, :]
            total = jnp.sum(tall(last.reshape(s.rows, LANE)), axis=0, keepdims=True)
            value, slope = gelu_parts(total / area)
            cols = slice(ch * LANE, (ch + 1) * LANE)
            self.pool[0, :, cols] = jnp.broadcast_to(value, (8, LANE))
            self.pool[1, :, cols] = jnp.broadcast_to(slope / area, (8, LANE))

        def step(index, carry):
            at = pl.ds(pl.multiple_of(index * BLK, BLK), BLK)
            gate = self.gate[LEVELS, at, :]
            for ch in range(s.nc):
                cols = slice(ch * LANE, (ch + 1) * LANE)
                part = self.summed[ch, pl.ds(index * (BLK // s.side), BLK // s.side)].reshape(BLK, LANE)
                self.sumb[at, cols] = (part + gate * self.pool[0, 0:1, cols]).astype(b16)
            return carry

        lax.fori_loop(0, s.rows // BLK, step, 0)

    def modulate(self):
        s = self.s
        self.mod[...] = mm(self.sumb[...], self.wh()) + self.row(4)

        def mix(at, lines):
            self.mixb[at, :] = (self.q[at, :] * self.mod[at, :]).astype(b16)

        self.blocks(mix)
        self.proj[...] = mm(self.mixb[...], self.wp()) + self.row(5)
        scale, gain, shift = self.row(6), self.row(7), self.row(8)
        upscale = self.row(10)

        def norm(at, lines):
            mid = self.image(self.x, lines) + scale * self.proj[at, :]
            self.mid[at, :] = mid
            centred = mid - lane_sum(mid) * (1.0 / s.c)
            r = lax.rsqrt(lane_sum(centred * centred) * (1.0 / s.c) + norm_eps)
            xh = centred * r
            self.xh2[at, :] = xh
            self.r2[at, :] = jnp.broadcast_to(r, (BLK, LANE))
            self.n2b[at, :] = (xh * gain + shift).astype(b16)
            d_shr = self.image(self.cot, lines) * self.wide_mask(at) * upscale
            self.dshrb[at, :] = d_shr.astype(b16)
            return (d_shr,)

        (g_b2,) = self.blocks(norm, 1)
        self.put(9, g_b2)

    def slope_tile(self, tile):
        s = self.s
        index, part = divmod(tile, s.nc)
        lanes = slice(part * LANE, (part + 1) * LANE)
        if index == 0:
            return self.dsum.at[part], (s.rows, LANE)
        if index == 1:
            return self.grad.at[:, :, lanes], (s.side, s.side, LANE)
        return (self.dn if index == 2 else self.shr).at[:, lanes], (s.rows, LANE)

    def feed(self, wide=256):
        s = self.s
        half = s.hid // 2
        for j in range(s.hid // wide):
            cols = slice(j * wide, (j + 1) * wide)
            h, at = divmod(j * wide, half)
            bias = []
            for start in range(j * wide, (j + 1) * wide, LANE):
                r, c = divmod(start, s.c)
                bias.append(self.v[11 + r : 12 + r, c : c + LANE])
            hid = mm(self.n2b[...], self.w1(h, at, wide)) + jnp.concatenate(bias, axis=1)
            act, slope = gelu_parts(hid)
            self.actb[:, cols] = act.astype(b16)
            for i in range(wide // LANE):
                ref, shape = self.slope_tile(j * wide // LANE + i)
                ref[...] = slope[:, i * LANE : (i + 1) * LANE].reshape(shape)

    def feed_back(self, wide=256):
        s = self.s
        for j in range(s.hid // wide):
            d_act = mm_t(self.dshrb[...], self.w2(j * wide, wide))
            for i in range(wide // LANE):
                ref, _ = self.slope_tile(j * wide // LANE + i)
                d_hid = d_act[:, i * LANE : (i + 1) * LANE] * ref[...].reshape(s.rows, LANE)
                start = j * wide + i * LANE
                self.dhidb[:, start : start + LANE] = d_hid.astype(b16)
                r, c = divmod(start, s.c)
                self.gv[11 + r : 12 + r, c : c + LANE] = jnp.sum(tall(d_hid), axis=0, keepdims=True)

    def shrink_grad(self):
        s = self.s
        for at in range(0, s.hid, s.c):
            self.put_g2(at, s.c, mm_g(self.actb[:, at : at + s.c], self.dshrb[...]))

    def expand_grad(self):
        s = self.s
        half = s.hid // 2
        for at in range(0, s.hid, s.c):
            self.put_g1(at // half, at % half, mm_g(self.n2b[...], self.dhidb[:, at : at + s.c]))

    def feed_out(self):
        s = self.s
        half = s.hid // 2
        self.shr[...] = mm(self.actb[...], self.w2(0, s.hid)) + self.row(9)
        self.dn[...] = mm_t(self.dhidb[:, :half], self.w1(0, 0, half)) + mm_t(
            self.dhidb[:, half:], self.w1(1, 0, half)
        )

    def middle(self):
        s = self.s
        gain, scale, upscale = self.row(7), self.row(6), self.row(10)

        def step(at, lines):
            shr, mid, proj, xh = self.shr[at, :], self.mid[at, :], self.proj[at, :], self.xh2[at, :]
            m = self.wide_mask(at)
            u = self.image(self.cot, lines) * m
            self.store(self.out, lines, (mid + upscale * shr) * m)
            d = self.dn[at, :]
            e = d * gain
            mean_e = lane_sum(e) * (1.0 / s.c)
            mean_x = lane_sum(e * xh) * (1.0 / s.c)
            d_mid = u + self.wide(self.r2, at) * (e - mean_e - xh * mean_x)
            self.dmid[at, :] = d_mid
            d_proj = scale * d_mid
            self.dprojb[at, :] = d_proj.astype(b16)
            return u * shr, d * xh, d, d_mid * proj, d_proj

        sums = self.blocks(step, 5)
        for index, total in zip((10, 7, 8, 6, 5), sums):
            self.put(index, total)
        self.dn[...] = mm_t(self.dprojb[...], self.wp())

        def split(at, lines):
            d = self.dn[at, :]
            d_q = d * self.mod[at, :]
            d_mod = d * self.q[at, :]
            self.dqb[at, :] = d_q.astype(b16)
            self.dmodb[at, :] = d_mod.astype(b16)
            return d_q, d_mod

        g_bq, g_bh = self.blocks(split, 2)
        self.put(2, g_bq)
        self.put(4, g_bh)
        d_sum = mm_t(self.dmodb[...], self.wh())
        for ch in range(s.nc):
            self.dsum[ch] = d_sum[:, ch * LANE : (ch + 1) * LANE]

    def middle_grads(self):
        self.put_gp(mm_g(self.mixb[...], self.dprojb[...]))
        self.put_gh(mm_g(self.sumb[...], self.dmodb[...]))

    def query_grad(self):
        self.put_gq(mm_g(self.n1b[...], self.dqb[...]))

    def focal_top(self):
        s = self.s

        def step(index, carry):
            at = pl.ds(pl.multiple_of(index * BLK, BLK), BLK)
            gate = self.gate[LEVELS, at, :]
            sums = [jnp.zeros((BLK, LANE), f32) for _ in range(GATES)]
            out = []
            for ch in range(s.nc):
                cols = slice(ch * LANE, (ch + 1) * LANE)
                d = self.dsum[ch, at, :]
                values = [
                    self.pads[l][ch, pl.ds(index * (BLK // s.side) + PAD, BLK // s.side), EDGE : EDGE + s.side, :]
                    for l in range(1, LEVELS + 1)
                ]
                for l in range(LEVELS):
                    sums[l] = sums[l] + d * values[l].reshape(BLK, LANE)
                sums[LEVELS] = sums[LEVELS] + d * self.pool[0, 0:1, cols]
                out.append(carry[ch] + tall(d * gate))
            for l in range(GATES):
                self.dgate[l, at, :] = jnp.broadcast_to(
                    jnp.sum(sums[l], axis=1, keepdims=True), (BLK, LANE)
                )
            return tuple(out)

        zero = jnp.zeros((8, LANE), f32)
        totals = lax.fori_loop(0, s.rows // BLK, step, (zero,) * s.nc)
        for ch in range(s.nc):
            cols = slice(ch * LANE, (ch + 1) * LANE)
            total = jnp.sum(totals[ch], axis=0, keepdims=True)
            self.pool[1, :, cols] = self.pool[1, :, cols] * total

        def last(index, carry):
            at = pl.ds(pl.multiple_of(index * BLK, BLK), BLK)
            gate = self.gate[LEVELS - 1, at, :]
            for ch in range(s.nc):
                cols = slice(ch * LANE, (ch + 1) * LANE)
                e = self.dsum[ch, at, :] * gate + self.pool[1, 0:1, cols]
                d = e.reshape(BLK // s.side, s.side, LANE) * self.gd[LEVELS - 1][ch, pl.ds(index * (BLK // s.side), BLK // s.side)]
                self.pads[LEVELS][ch, pl.ds(index * (BLK // s.side) + PAD, BLK // s.side), EDGE : EDGE + s.side, :] = d
            return carry

        lax.fori_loop(0, s.rows // BLK, last, 0)

    def level_back(self, l, chunks, block=4):
        s = self.s
        k = 2 * l + 3
        p = l + 1
        base = sum(s.taps[:l])
        offset = s.kernel_at + base
        source = self.pads[l + 1]
        inputs = self.pads[l]
        per = s.side // block

        def step(index, carry):
            ch = chunks[0] + lax.div(index, per)
            r0 = lax.rem(index, per) * block
            acc = [None] * block
            xs = [
                inputs[ch, r0 + PAD + o, EDGE : EDGE + s.side, :] for o in range(block)
            ]
            for dc in range(-p, p + 1):
                taps = [
                    self.vc[ch, pl.ds(offset + (dr + p) * k + dc + p, 1), :]
                    for dr in range(-p, p + 1)
                ]
                sums = [None] * k
                for a in range(-p, block + p):
                    d = source[ch, r0 + PAD + a, pl.ds(EDGE - dc, s.side), :]
                    for o in range(max(0, a - p), min(block, a + p + 1)):
                        dr = o - a
                        term = d * taps[dr + p]
                        acc[o] = term if acc[o] is None else acc[o] + term
                        part = tall(d * xs[o])
                        sums[dr + p] = part if sums[dr + p] is None else sums[dr + p] + part
                for dr in range(-p, p + 1):
                    tap = base + (dr + p) * k + dc + p
                    self.gacc[ch, tap] = self.gacc[ch, tap] + sums[dr + p]
            total = None
            for o in range(block):
                at = pl.ds(pl.multiple_of((r0 + o) * s.side, s.side), s.side)
                if l:
                    e = acc[o] + self.dsum[ch, at, :] * self.gate[l - 1, at, :]
                    self.pads[l][ch, r0 + o + PAD, EDGE : EDGE + s.side, :] = (
                        e * self.gd[l - 1][ch, r0 + o]
                    )
                else:
                    self.summed[ch, r0 + o] = acc[o] * self.mask[at, :]
            return carry

        lax.fori_loop(0, len(chunks) * per, step, 0)

    def context_grad(self, chunks):
        s = self.s

        def step(index, carry):
            at = pl.ds(pl.multiple_of(index * BLK, BLK), BLK)
            out = []
            for i, ch in enumerate(chunks):
                cols = slice(ch * LANE, (ch + 1) * LANE)
                lines = pl.ds(index * (BLK // s.side), BLK // s.side)
                d = self.summed[ch, lines].reshape(BLK, LANE)
                self.dctxb[at, cols] = d.astype(b16)
                out.append(carry[i] + tall(d))
            return tuple(out)

        zero = jnp.zeros((8, LANE), f32)
        totals = lax.fori_loop(0, s.rows // BLK, step, (zero,) * len(chunks))
        for i, ch in enumerate(chunks):
            cols = slice(ch * LANE, (ch + 1) * LANE)
            self.gv[3:4, cols] = jnp.sum(totals[i], axis=0, keepdims=True)
            self.gv[s.kernel_at : s.nvec, cols] = jnp.sum(self.gacc[ch], axis=1)
        lanes = slice(chunks[0] * LANE, (chunks[-1] + 1) * LANE)
        self.put_gc(chunks, mm_g(self.n1b[...], self.dctxb[:, lanes]))

    def last_back(self):
        s = self.s
        wc = self.wc(tuple(range(s.nc)))
        self.dn[...] = mm_t(self.dqb[...], self.wq()) + mm_t(self.dctxb[...], wc)
        gain, shift = self.row(0), self.row(1)
        weights = [self.row(s.gate_at + l) for l in range(GATES)]

        def step(at, lines):
            xh = self.xh1[at, :]
            n1 = xh * gain + shift
            d = self.dn[at, :]
            sums = []
            for l in range(GATES):
                dg = self.wide(self.dgate.at[l], at)
                d = d + dg * weights[l]
                sums.append(dg * n1)
            e = d * gain
            mean_e = lane_sum(e) * (1.0 / s.c)
            mean_x = lane_sum(e * xh) * (1.0 / s.c)
            d_in = self.dmid[at, :] + self.wide(self.r1, at) * (e - mean_e - xh * mean_x)
            self.store(self.grad, lines, d_in)
            return (d * xh, d) + tuple(sums)

        sums = self.blocks(step, 2 + GATES)
        for index, total in zip((0, 1) + tuple(s.gate_at + l for l in range(GATES)), sums):
            self.put(index, total)


MESH = pl.DeviceIdType.MESH
STEP = 10
beta_one = 0.9
beta_two = 0.95
adam_eps = 1e-08
weight_decay = 0.05
VMEM_BYTES = 63 * 2**20 + 2**19
GATHERED = "vabmes"
REDUCED = "sedmqtu"
DIRECT = "qtu"
NEAR = "va"
AT_ONCE = "vab"


class Plan:
    def __init__(self, n_grp, n_fs, s):
        self.X = n_grp // 2
        self.Y = 2 ** (int(math.log2(n_fs)) // 2)
        self.Z = n_fs // self.Y
        self.fs = n_fs
        self.s = s
        self.rows = s.c // n_fs
        self.rp = -(-self.rows // 16) * 16
        self.rows2 = s.hid // n_fs // 2
        self.rp2 = -(-self.rows2 // 16) * 16
        self.even = self.rp == self.rows and self.rp2 == self.rows2
        self.rv = self.rp // 2
        self.gather_cols = dict(v=LANE, a=LANE, b=2 * LANE, m=s.c, e=s.hid // 2, s=s.c)
        self.reduce_cols = dict(s=s.c, e=s.hid // 4, d=s.hid // 4, m=s.c, q=2 * LANE, t=LANE, u=LANE)

    def piece(self, name, cols):
        return (dict(s=self.rp2, v=self.rv).get(name, self.rp), cols[name])

    def whole(self, name, cols):
        if name in "sv":
            return (self.Z, self.Y, 2) + self.piece(name, cols)
        return (2, self.Z, self.Y) + self.piece(name, cols)


def gather_scratch(p, name):
    piece = p.piece(name, p.gather_cols)
    kind = f32 if name == "v" else b16
    return dict(
        cand=pltpu.VMEM((2,) + piece, kind),
        rx1=pltpu.VMEM(piece, kind),
        sel=pltpu.VMEM(piece, kind),
        rx2=pltpu.VMEM((p.X - 1, 2 if name in NEAR else 1) + piece, kind),
        full=pltpu.VMEM(p.whole(name, p.gather_cols), kind),
    )


def reduce_scratch(p, name):
    piece = p.piece(name, p.reduce_cols)
    out = dict(
        grad=pltpu.VMEM(p.whole(name, p.reduce_cols), b16),
        r1=pltpu.VMEM((p.Z, p.Y) + piece, b16),
        a3=pltpu.VMEM(piece, b16),
        a4=pltpu.VMEM(piece, f32),
        r4=pltpu.VMEM((p.X - 1, 2) + piece, b16),
        r5=pltpu.VMEM(piece, b16),
        fin=pltpu.VMEM((2,) + piece, f32),
    )
    if name in DIRECT:
        out["r3"] = pltpu.VMEM((p.fs - 1,) + piece, b16)
    else:
        out["r2"] = pltpu.VMEM((p.Y - 1, p.Z) + piece, b16)
        out["a2"] = pltpu.VMEM((p.Z,) + piece, b16)
        out["r3"] = pltpu.VMEM((p.Z - 1,) + piece, b16)
    return out


def sem_count(p):
    gather = 1 + 2 * (p.X - 1) + (p.Z - 1) + p.Z * (p.Y - 1) + p.fs
    reduce = 1 + max((p.Y - 1) + (p.Z - 1), p.fs - 1) + 2 * (p.X - 1) + 1
    return gather * len(GATHERED) + reduce * len(REDUCED)


class Links:
    def __init__(self, p, send_sem, recv_sem):
        self.p = p
        self.send_sem, self.recv_sem = send_sem, recv_sem
        self.used = 0
        self.sent = []
        self.g, self.f = lax.axis_index("grp"), lax.axis_index("fs")
        self.x, self.c = lax.div(self.g, 2), lax.rem(self.g, 2)
        self.z, self.y = lax.div(self.f, p.Y), lax.rem(self.f, p.Y)

    def sibling(self):
        return (self.x * 2 + 1 - self.c, self.f)

    def at_x(self, x, other_core=0):
        core = 1 - self.c if other_core else self.c
        return (x * 2 + core, self.f)

    def at_z(self, z):
        return (self.g, z * self.p.Y + self.y)

    def at_y(self, y):
        return (self.g, self.z * self.p.Y + y)

    def flip_z(self, bit):
        return self.z + bit - 2 * bit * lax.rem(lax.div(self.z, bit), 2)

    def signal_partners(self):
        p = self.p
        partners = (
            [self.sibling()]
            + [self.at_x(lax.rem(self.x + d, p.X), i) for d in range(1, p.X) for i in range(2)]
            + [(self.g, lax.rem(self.f + d, p.fs)) for d in range(1, p.fs)]
        )
        self.partners = len(partners)
        barrier = pltpu.get_barrier_semaphore()
        for partner in partners:
            pl.semaphore_signal(barrier, inc=1, device_id=partner, device_id_type=MESH)

    def wait_partners(self):
        pl.semaphore_wait(pltpu.get_barrier_semaphore(), self.partners)

    def send(self, source, target, partner, arriving=None):
        index = self.used
        self.used += 1

        def copy(src, dst):
            return pltpu.make_async_remote_copy(
                src_ref=src,
                dst_ref=dst,
                send_sem=self.send_sem.at[index],
                recv_sem=self.recv_sem.at[index],
                device_id=partner,
                device_id_type=MESH,
            )

        started = copy(source, target)
        started.start()
        self.sent.append(started)
        coming = copy(source, target if arriving is None else arriving)
        return coming.wait_recv

    def finish(self):
        for copy in self.sent:
            copy.wait_send()


class Gather:
    def __init__(self, name, links, refs):
        self.name, self.links, self.p = name, links, links.p
        self.near, self.direct = name in NEAR, name in AT_ONCE
        self.__dict__.update(refs)
        self.held, self.wait3, self.wait4, self.wait5 = [], [], [], []

    def piece(self, half, z, y):
        return self.full.at[z, y, half] if self.name in "sv" else self.full.at[half, z, y]

    def core_send(self, z, y):
        k = self.links
        here = self.piece(k.c, z, y)
        self.wait5.append(k.send(here, here, k.sibling(), self.piece(1 - k.c, z, y)))

    def one(self):
        k, p = self.links, self.p
        self.wait1 = k.send(self.cand.at[1 - k.c], self.rx1, k.sibling())
        if self.near:
            self.wait2 = []
            for d in range(1, p.X):
                x = lax.rem(k.x + d, p.X)
                for i, h in enumerate((k.c, 1 - k.c)):
                    self.wait2.append(k.send(self.cand.at[h], self.rx2.at[d - 1, i], k.at_x(x, i)))

    def two(self):
        k, p = self.links, self.p
        self.wait1()
        self.sel[...] = self.cand[k.c] + self.rx1[...]
        if not self.near:
            self.wait2 = [
                k.send(self.sel, self.rx2.at[d - 1, 0], k.at_x(lax.rem(k.x + d, p.X)))
                for d in range(1, p.X)
            ]

    def y_sends(self, z):
        k, p = self.links, self.p
        here = self.piece(k.c, z, k.y)
        for d in range(1, p.Y):
            other = lax.rem(k.y + p.Y - d, p.Y)
            partner = k.at_y(lax.rem(k.y + d, p.Y))
            wait = k.send(here, here, partner, self.piece(k.c, z, other))
            self.wait4.append((wait, z, other))

    def pair_round(self):
        k = self.links
        bit = self.p.Z >> (self.rounds + 1)
        partner = k.at_z(k.flip_z(bit))
        self.rounds += 1
        for z in self.held:
            other = z + bit - 2 * bit * lax.rem(lax.div(z, bit), 2)
            here = self.piece(k.c, z, k.y)
            wait = k.send(here, here, partner, self.piece(k.c, other, k.y))
            self.wait3.append((wait, other))

    def three(self):
        k, p = self.links, self.p
        for wait in self.wait2:
            wait()
        total = self.sel[...]
        for d in range(p.X - 1):
            for i in range(2 if self.near else 1):
                total = total + self.rx2[d, i]
        here = self.piece(k.c, k.z, k.y)
        here[...] = total
        self.held, self.rounds = [k.z], 0
        if self.direct:
            for d in range(1, p.Z):
                other = lax.rem(k.z + p.Z - d, p.Z)
                partner = k.at_z(lax.rem(k.z + d, p.Z))
                wait = k.send(here, here, partner, self.piece(k.c, other, k.y))
                self.wait3.append((wait, other))
        else:
            self.pair_round()

    def own(self):
        self.y_sends(self.links.z)
        self.core_send(self.links.z, self.links.y)

    def four(self):
        waits, self.wait3 = self.wait3, []
        for wait, z in waits:
            wait()
            self.held.append(z)
        if len(self.held) < self.p.Z:
            self.pair_round()
        for _, z in waits:
            self.y_sends(z)
            self.core_send(z, self.links.y)

    def five(self):
        while self.wait3:
            self.four()
        for wait, z, y in self.wait4:
            wait()
            self.core_send(z, y)

    def six(self):
        for wait in self.wait5:
            wait()


class Reduce:
    def __init__(self, name, links, refs):
        self.name, self.links, self.p = name, links, links.p
        self.direct = name in DIRECT
        self.__dict__.update(refs)

    def half(self, h):
        return self.grad.at[:, :, h] if self.name == "s" else self.grad.at[h]

    def one(self):
        k = self.links
        self.wait1 = k.send(self.half(1 - k.c), self.r1, k.sibling())

    def two(self):
        k, p = self.links, self.p
        self.wait1()
        mine = self.half(k.c)

        def add(index, carry):
            z, y = lax.div(index, p.Y), lax.rem(index, p.Y)
            self.r1[z, y] = self.r1[z, y] + mine[z, y]
            return carry

        lax.fori_loop(0, p.fs, add, 0)
        self.wait2 = []
        if self.direct:
            for d in range(1, p.fs):
                f = lax.rem(k.f + d, p.fs)
                source = self.r1.at[lax.div(f, p.Y), lax.rem(f, p.Y)]
                self.wait2.append(k.send(source, self.r3.at[d - 1], (k.g, f)))
            return
        for d in range(1, p.Y):
            other = lax.rem(k.y + d, p.Y)
            self.wait2.append(k.send(self.r1.at[:, other], self.r2.at[d - 1], k.at_y(other)))

    def three(self):
        k, p = self.links, self.p
        for wait in self.wait2:
            wait()
        self.wait3 = []
        if self.direct:
            total = self.r1[k.z, k.y].astype(f32)
            for d in range(p.fs - 1):
                total = total + self.r3[d].astype(f32)
            self.a4[...] = total
            return

        def add(z, carry):
            total = self.r1[z, k.y].astype(f32)
            for d in range(p.Y - 1):
                total = total + self.r2[d, z].astype(f32)
            self.a2[z] = total.astype(b16)
            return carry

        lax.fori_loop(0, p.Z, add, 0)
        self.bit, self.slot = 1, 0
        self.pair_round()

    def pair_round(self):
        k, p = self.links, self.p
        bit = self.bit
        partner = k.flip_z(bit)
        low_partner, own = lax.rem(partner, 2 * bit), lax.rem(k.z, 2 * bit)
        self.wait3 = []
        for step in range(p.Z // (2 * bit)):
            target = low_partner + 2 * bit * step
            mine = own + 2 * bit * step
            wait = k.send(self.a2.at[target], self.r3.at[self.slot], k.at_z(partner))
            self.wait3.append((wait, mine, self.slot))
            self.slot += 1
        self.bit = 2 * bit

    def four(self):
        for wait, z, slot in self.wait3:
            wait()
            total = self.a2[z].astype(f32) + self.r3[slot].astype(f32)
            if self.bit < self.p.Z:
                self.a2[z] = total.astype(b16)
            else:
                self.a4[...] = total
        self.wait3 = []
        if not self.direct and self.bit < self.p.Z:
            self.pair_round()

    def five(self):
        k, p = self.links, self.p
        while self.wait3:
            self.four()
        self.a3[...] = self.a4[...].astype(b16)
        self.wait4 = []
        for d in range(1, p.X):
            x = lax.rem(k.x + d, p.X)
            for i in range(2):
                self.wait4.append(k.send(self.a3, self.r4.at[d - 1, i], k.at_x(x, i)))
        self.wait4.append(k.send(self.a3, self.r5, k.sibling()))

    def six(self):
        k, p = self.links, self.p
        for wait in self.wait4:
            wait()
        for h, total, i in ((k.c, self.a4[...], 0), (1 - k.c, self.r5[...].astype(f32), 1)):
            for d in range(p.X - 1):
                total = total + self.r4[d, i].astype(f32)
            self.fin[h] = total


def spread_matrix(rows, rp, count):
    bits = int(math.log2(rp))
    shape = (count * rows, count * rp)
    a = lax.broadcasted_iota(jnp.int32, shape, 0)
    b = lax.broadcasted_iota(jnp.int32, shape, 1)
    i = lax.bitwise_and(b, rp - 1)
    hit = (a == lax.shift_right_logical(b, bits) * rows + i) & (i < rows)
    return jnp.where(hit, 1.0, 0.0).astype(b16)


def block_kernel(p, tree, *refs):
    s = p.s
    count, sides, owners = refs[:3]
    sources = dict(zip(("x", "cot", "focal", "modulate", "project", "expand", "shrink", "vector"), refs[3:11]))
    out_hbm, grad_hbm = refs[11:13]
    fin_hbm = dict(zip(REDUCED, refs[13:20]))
    own = jax.tree.unflatten(tree, refs[20:])
    k = Links(p, own["send_sem"], own["recv_sem"])
    land, local_sem = own["land"], own["local_sem"]
    local_used = []

    def local(source, target):
        copy = pltpu.make_async_copy(source, target, local_sem.at[len(local_used)])
        local_used.append(copy)
        copy.start()
        return copy

    loads = {}
    for name in ("focal", "vector", "modulate", "project", "x", "expand", "shrink", "cot"):
        loads[name] = local(sources[name].at[0], land[name])
    k.signal_partners()

    def mine(index):
        return jnp.where(owners[index] == k.g, 1.0, 0.0).astype(f32)

    def cut(values, rows, rp):
        if rows == rp:
            return values
        return jnp.concatenate([values, jnp.zeros((rp - rows, values.shape[1]), f32)], axis=0)

    def candidate(name, h, values):
        rows, rp = values.shape[0], p.piece(name, p.gather_cols)[0]
        own["g" + name]["cand"][h] = cut(values, rows, rp).astype(b16)

    gathers = {
        name: Gather(name, k, own["g" + name]) for name in GATHERED
    }
    gv, ga, gb, gm, ge, gs = (gathers[name] for name in GATHERED)
    reduces = {name: Reduce(name, k, own["r" + name]) for name in REDUCED}
    rs, re, rd, rm, rq, rt, ru = (reduces[name] for name in REDUCED)
    c, wide = s.c, s.hid // 2

    loads["focal"].wait()
    loads["vector"].wait()
    focal = land["focal"]
    values = cut(land["vector"][...] * mine(5), p.rows, p.rp)
    values = jnp.concatenate([values, jnp.zeros((p.rp, LANE - s.nvec), f32)], axis=1)
    for h in range(2):
        own["gv"]["cand"][h] = values[h * p.rv : (h + 1) * p.rv]
        at = c + h * LANE
        candidate("a", h, focal[:, at : at + LANE] * mine(0))
    k.wait_partners()
    gv.one()
    ga.one()
    candidate("b", 0, jnp.concatenate([focal[:, c + 2 * LANE :], focal[:, :LANE]], axis=1) * mine(0))
    candidate("b", 1, focal[:, LANE:c] * mine(0))
    gb.one()
    loads["modulate"].wait()
    loads["project"].wait()
    candidate("m", 0, land["modulate"][...] * mine(1))
    candidate("m", 1, land["project"][...] * mine(2))
    gm.one()
    gb.two()
    loads["expand"].wait()
    for h in range(2):
        candidate("e", h, land["expand"][:, h * wide : (h + 1) * wide] * mine(3))
    ge.one()
    loads["shrink"].wait()
    for h in range(2):
        candidate("s", h, land["shrink"][h * p.rows2 : (h + 1) * p.rows2, :] * mine(4))
    gs.one()

    if not p.even:
        own["map"][...] = spread_matrix(p.rows, p.rp, p.fs)

    def compact(values):
        return values if p.even else mm(own["map"][...], values).astype(b16)

    def spread(values):
        values = values.astype(b16)
        return values if p.even else mm_g(own["map"][...], values).astype(b16)

    def matrix(name, h, at, cols):
        part = own["g" + name]["full"][h, :, :, :, at : at + cols]
        return compact(part.reshape(p.fs * p.rp, cols))

    def take_context(chunks):
        parts = []
        if chunks[0] < 2:
            parts += [matrix("a", ch, 0, LANE) for ch in chunks if ch < 2]
        if chunks[-1] == 2:
            parts.append(matrix("b", 0, 0, LANE))
        return jnp.concatenate(parts, axis=1) if len(parts) > 1 else parts[0]

    def take_query():
        return jnp.concatenate([matrix("b", 0, LANE, LANE), matrix("b", 1, 0, 2 * LANE)], axis=1)

    def take_shrink(at, rows):
        if p.even:
            return own["gs"]["full"][...].reshape(s.hid, s.c)[at : at + rows]
        return own["w2n"][at : at + rows, :]

    def put(name, h, at, values):
        cols = values.shape[1]
        grads = spread(values).reshape(p.Z, p.Y, p.rp, cols)
        own["r" + name]["grad"][h, :, :, :, at : at + cols] = grads

    def put_query(values):
        put("q", 0, 0, values[:, : 2 * LANE])
        put("q", 1, 0, values[:, 2 * LANE :])

    def put_context(chunks, values):
        for i, ch in enumerate(chunks):
            name, h = (("t", 0), ("t", 1), ("u", 0))[ch]
            put(name, h, 0, values[:, i * LANE : (i + 1) * LANE])

    def put_shrink(at, rows, values):
        low = values.astype(b16)
        if not p.even:
            own["g2n"][at : at + rows, :] = low
            return
        start = at
        while start < at + rows:
            piece, inner = divmod(start, p.rp2)
            size = min(p.rp2 - inner, at + rows - start)
            (f, h), first = divmod(piece, 2), start - at
            own["rs"]["grad"][f // p.Y, f % p.Y, h, inner : inner + size, :] = low[first : first + size]
            start += size

    block = Compute(
        s,
        dict(
            x=land["x"],
            cot=land["cot"],
            v=own["v"],
            count=count[0, 0],
            sides=sides[0],
            out=own["out"],
            grad=own["grad"],
            gv=own["gvec"],
            wc=take_context,
            wq=take_query,
            wh=lambda: matrix("m", 0, 0, c),
            wp=lambda: matrix("m", 1, 0, c),
            w1=lambda h, at, cols: matrix("e", h, at, cols),
            w2=take_shrink,
            put_gq=put_query,
            put_gc=put_context,
            put_gh=lambda values: put("m", 0, 0, values),
            put_gp=lambda values: put("m", 1, 0, values),
            put_g1=lambda h, at, values: put("d" if at else "e", h, 0, values),
            put_g2=put_shrink,
        ),
        own["compute"],
    )

    stores = []

    def settle(name):
        reduces[name].six()
        stores.append(local(own["r" + name]["fin"], fin_hbm[name]))

    def prepare():
        loads["x"].wait()
        block.prepare()
        own["gvec"][s.nvec :, :] = jnp.zeros((LANE - s.nvec, s.c), f32)
        put("q", 1, LANE, jnp.zeros((s.c, LANE), f32))

    def take_vector():
        vector = own["gv"]["full"][...].reshape(p.fs * p.rp, LANE)
        if not p.even:
            vector = jnp.dot(own["map"][...].astype(f32), vector, precision=lax.Precision.HIGHEST)
        own["v"][...] = vector.T

    def modulate():
        loads["cot"].wait()
        block.modulate()

    def close_shrink():
        def close(f, carry):
            z, y = lax.div(f, p.Y), lax.rem(f, p.Y)
            parts = [own["gs"]["full"][z, y, h].astype(f32)[: p.rows2] for h in range(2)]
            at = pl.ds(pl.multiple_of(f * 2 * p.rows2, 2 * p.rows2), 2 * p.rows2)
            own["w2n"][at, :] = jnp.concatenate(parts, axis=0).astype(b16)
            return carry

        if not p.even:
            lax.fori_loop(0, p.fs, close, 0)

    def shrink_grad():
        block.shrink_grad()

        def open_up(f, carry):
            z, y = lax.div(f, p.Y), lax.rem(f, p.Y)
            at = pl.ds(pl.multiple_of(f * 2 * p.rows2, 2 * p.rows2), 2 * p.rows2)
            both = own["g2n"][at, :].astype(f32)
            for h in range(2):
                part = cut(both[h * p.rows2 : (h + 1) * p.rows2], p.rows2, p.rp2)
                own["rs"]["grad"][z, y, h] = part.astype(b16)
            return carry

        if not p.even:
            lax.fori_loop(0, p.fs, open_up, 0)

    def middle():
        block.middle()
        stores.append(local(own["out"], out_hbm.at[0]))

    def last_back():
        block.last_back()
        stores.append(local(own["grad"], grad_hbm.at[0]))

    def put_vector():
        grads = own["gvec"][...].T
        if not p.even:
            grads = mm_g(own["map"][...], grads.astype(b16))
        own["ru"]["grad"][1] = grads.astype(b16).reshape(p.Z, p.Y, p.rp, LANE)

    gm.two()
    ga.two()
    gv.two()
    gv.three()
    ga.three()
    ge.two()
    gb.three()
    gv.own()
    gm.three()
    ga.own()
    gs.two()
    gm.own()
    ge.three()
    gb.own()
    gv.four()
    ge.own()
    gs.three()
    ga.four()
    gv.five()
    gb.four()
    gv.six()
    prepare()
    ge.four()
    take_vector()
    gs.own()
    gm.four()
    ga.five()
    gb.five()
    block.first()
    ga.six()
    block.context((0, 1))
    block.level(0, (0, 1))
    gs.four()
    block.level(1, (0, 1))
    ge.four()
    gb.six()
    block.context((2,))
    block.level(2, (0, 1))
    gm.four()
    block.level(0, (2,))
    block.query()
    block.level(1, (2,))
    gs.four()
    ge.five()
    block.level(2, (2,))
    gm.five()
    ge.six()
    block.pooling()
    gm.six()
    modulate()
    gs.five()
    block.feed()
    gs.six()
    shrink_grad()
    rs.one()
    close_shrink()
    block.feed_back()
    block.expand_grad()
    rs.two()
    re.one()
    block.feed_out()
    middle()
    block.query_grad()
    block.middle_grads()
    rq.one()
    rm.one()
    block.focal_top()
    re.two()
    rm.two()
    rq.two()
    block.level_back(2, (0, 1))
    rs.three()
    block.level_back(1, (0, 1))
    rd.one()
    re.three()
    block.level_back(0, (0, 1))
    rd.two()
    block.context_grad((0, 1))
    rm.three()
    rt.one()
    rs.four()
    rt.two()
    block.level_back(2, (2,))
    block.level_back(1, (2,))
    block.level_back(0, (2,))
    rd.three()
    block.context_grad((2,))
    re.four()
    rq.three()
    last_back()
    rm.four()
    rs.five()
    put_vector()
    ru.one()
    rq.five()
    ru.two()
    rd.four()
    re.five()
    rt.three()
    rm.five()
    rt.five()
    ru.three()
    ru.five()
    rd.five()
    settle("e")
    settle("m")
    settle("s")
    settle("u")
    settle("t")
    settle("q")
    settle("d")
    k.finish()
    for store in stores:
        store.wait()


def adam_kernel(p, rates, tree, *refs):
    s = p.s
    owners = refs[0]
    fins = dict(zip(REDUCED, refs[1:8]))
    passed, olds = refs[8:10], refs[10:28]
    passed_out, news = refs[28:30], refs[30:48]
    own = jax.tree.unflatten(tree, refs[48:])
    sems = own["sem"]
    g = lax.axis_index("grp")
    used = []

    def local(source, target):
        copy = pltpu.make_async_copy(source, target, sems.at[len(used)])
        used.append(copy)
        copy.start()
        return copy

    wide = s.hid // 2
    groups = (
        (3, [(n, h, 0, p.rows, h * wide + i * s.c, s.c) for h in range(2) for i, n in enumerate("ed")]),
        (4, [("s", h, h * p.rows2, p.rows2, 0, s.c) for h in range(2)]),
        (1, [("m", 0, 0, p.rows, 0, s.c)]),
        (2, [("m", 1, 0, p.rows, 0, s.c)]),
        (
            0,
            [
                ("q", 0, 0, p.rows, 0, 2 * LANE),
                ("q", 1, 0, p.rows, 2 * LANE, LANE),
                ("t", 0, 0, p.rows, s.c, LANE),
                ("t", 1, 0, p.rows, s.c + LANE, LANE),
                ("u", 0, 0, p.rows, s.c + 2 * LANE, LANE),
            ],
        ),
        (5, [("u", 1, 0, p.rows, 0, s.nvec)]),
    )
    waits = {}
    for index, pieces in groups:
        waits[index] = []
        for name in dict.fromkeys(piece[0] for piece in pieces):
            if name not in waits:
                waits[name] = local(fins[name], own["fin"][name])
        for i in range(3):
            waits[index].append(local(olds[3 * index + i], own["old"][3 * index + i]))
    passing = [local(a, b) for a, b in zip(passed, own["passed"])]
    stores, arrived = [], set()
    for index, pieces in groups:
        scale = jnp.where(owners[index] == g, 1.0, 0.0).astype(f32)
        for wait in waits[index]:
            wait.wait()
        for name, h, row, rows, col, cols in pieces:
            if name not in arrived:
                arrived.add(name)
                waits[name].wait()
            at = (0, slice(row, row + rows), slice(col, col + cols))
            gradient = own["fin"][name][h, :rows, :cols]
            weight, first, second = (own["old"][3 * index + i][at] for i in range(3))
            first_new = beta_one * first + (1.0 - beta_one) * gradient
            second_new = beta_two * second + (1.0 - beta_two) * gradient * gradient
            first_hat = first_new / (1.0 - beta_one**STEP)
            second_hat = second_new / (1.0 - beta_two**STEP)
            weight_new = weight - rates[index] * (
                first_hat / (jnp.sqrt(second_hat) + adam_eps) + weight_decay * weight
            )
            for i, value in enumerate((weight_new, first_new, second_new)):
                own["new"][3 * index + i][at] = value * scale
        for i in range(3):
            stores.append(local(own["new"][3 * index + i], news[3 * index + i]))
    for wait, a, b in zip(passing, own["passed"], passed_out):
        wait.wait()
        stores.append(local(a, b))
    for store in stores:
        store.wait()


def solution(mesh):
    n_grp, n_fs = mesh.shape["grp"], mesh.shape["fs"]

    def shards(image_patches, cotangent, image_count, resolution, owner_list, *tensors):
        side, channels = image_patches.shape[1], image_patches.shape[3]
        hid = tensors[9].shape[2]
        s = Shape(side, channels, hid)
        p = Plan(n_grp, n_fs, s)
        grid = (side, side, channels)
        scratch = dict(
            compute=compute_scratch(s),
            land=dict(
                x=pltpu.VMEM(grid, b16),
                cot=pltpu.VMEM(grid, b16),
                focal=pltpu.VMEM((p.rows, 2 * channels), f32),
                modulate=pltpu.VMEM((p.rows, channels), f32),
                project=pltpu.VMEM((p.rows, channels), f32),
                expand=pltpu.VMEM((p.rows, hid), f32),
                shrink=pltpu.VMEM((2 * p.rows2, channels), f32),
                vector=pltpu.VMEM((p.rows, s.nvec), f32),
            ),
            out=pltpu.VMEM(grid, b16),
            grad=pltpu.VMEM(grid, f32),
            v=pltpu.VMEM((LANE, s.c), f32),
            gvec=pltpu.VMEM((LANE, s.c), f32),
            local_sem=pltpu.SemaphoreType.DMA((24,)),
            send_sem=pltpu.SemaphoreType.DMA((sem_count(p),)),
            recv_sem=pltpu.SemaphoreType.DMA((sem_count(p),)),
        )
        for name in GATHERED:
            scratch["g" + name] = gather_scratch(p, name)
        for name in REDUCED:
            scratch["r" + name] = reduce_scratch(p, name)
        if not p.even:
            scratch["map"] = pltpu.VMEM((s.c, p.fs * p.rp), b16)
            scratch["w2n"] = pltpu.VMEM((s.hid, s.c), b16)
            scratch["g2n"] = pltpu.VMEM((s.hid, s.c), b16)

        def flatten(scratch):
            return jax.tree.flatten(scratch, is_leaf=lambda v: not isinstance(v, (dict, list)))

        leaves, tree = flatten(scratch)
        anywhere = pl.BlockSpec(memory_space=pl.ANY)
        smem = pl.BlockSpec(memory_space=pltpu.SMEM)
        shape = jax.ShapeDtypeStruct
        fins = [shape((2,) + p.piece(name, p.reduce_cols), f32) for name in REDUCED]
        images = [shape(image_patches.shape, b16), shape(image_patches.shape, f32)]
        tensors = tensors[:15] + tuple(t.transpose(0, 2, 1) for t in tensors[15:])
        results = pl.pallas_call(
            lambda *refs: block_kernel(p, tree, *refs),
            out_shape=images + fins,
            in_specs=[smem] * 3 + [anywhere] * 8,
            out_specs=[anywhere] * 9,
            scratch_shapes=leaves,
            compiler_params=pltpu.CompilerParams(
                collective_id=0, has_side_effects=True, vmem_limit_bytes=VMEM_BYTES
            ),
            name="block",
        )(
            image_count,
            resolution,
            owner_list,
            image_patches,
            cotangent,
            *tensors[0:16:3],
        )
        wide_rate = 1.5 / math.sqrt(channels)
        rates = (wide_rate,) * 4 + (1.5 / math.sqrt(hid), 0.2)
        adam_leaves, adam_tree = flatten(
            dict(
                fin={name: pltpu.VMEM((2,) + p.piece(name, p.reduce_cols), f32) for name in REDUCED},
                old=[pltpu.VMEM(t.shape, f32) for t in tensors],
                new=[pltpu.VMEM(t.shape, f32) for t in tensors],
                passed=[pltpu.VMEM(t.shape, t.dtype) for t in images],
                sem=pltpu.SemaphoreType.DMA((56,)),
            )
        )
        news = pl.pallas_call(
            lambda *refs: adam_kernel(p, rates, adam_tree, *refs),
            out_shape=images + [shape(t.shape, f32) for t in tensors],
            in_specs=[smem] + [anywhere] * 27,
            out_specs=[anywhere] * 20,
            scratch_shapes=adam_leaves,
            compiler_params=pltpu.CompilerParams(vmem_limit_bytes=VMEM_BYTES),
            name="adam",
        )(owner_list, *results[2:], *results[:2], *tensors)
        return tuple(news[:17]) + tuple(t.transpose(0, 2, 1) for t in news[17:])

    images = P(("grp", "fs"), None, None, None)
    weights = (P("grp", "fs", None),) * 15 + (P("grp", None, "fs"),) * 3
    return jax.shard_map(
        shards,
        mesh=mesh,
        in_specs=(images, images, P("grp", "fs"), P(("grp", "fs")), P()) + weights,
        out_specs=(images, images) + weights,
        check_vma=False,
    )
```

```python
import math

import jax
import jax.numpy as jnp
from jax import lax
from jax.experimental import pallas as pl
from jax.experimental.pallas import tpu as pltpu
from jax.sharding import PartitionSpec as P

f32 = jnp.float32
b16 = jnp.bfloat16
LEVELS = 3
GATES = 4
LANE = 128
norm_eps = 1e-05
PAD = 3
EDGE = 8
SQRT_HALF = math.sqrt(0.5)
INV_SQRT_2PI = 1.0 / math.sqrt(2.0 * math.pi)
BLK = 576


def gelu_parts(z):
    az = jnp.abs(z)
    t = 1.0 / (1.0 + (0.3275911 * SQRT_HALF) * az)
    e = jnp.exp(z * z * -0.5)
    poly = t * (
        0.5 * 0.254829592
        + t * (0.5 * -0.284496736 + t * (0.5 * 1.421413741 + t * (0.5 * -1.453152027 + t * (0.5 * 1.061405429))))
    )
    tail = poly * e
    phi = jnp.where(z >= 0.0, 1.0 - tail, tail)
    return z * phi, phi + z * e * INV_SQRT_2PI


def mm(a, b):
    return jnp.dot(a, b, preferred_element_type=f32)


def mm_t(a, b):
    return lax.dot_general(a, b, (((1,), (1,)), ((), ())), preferred_element_type=f32)


def mm_g(a, b):
    return lax.dot_general(a, b, (((0,), (0,)), ((), ())), preferred_element_type=f32)


def tall(values):
    rows, cols = values.shape
    return jnp.sum(values.reshape(rows // 8, 8, cols), axis=0)


def lane_sum(values):
    parts = values[:, :LANE]
    for start in range(LANE, values.shape[1], LANE):
        parts = parts + values[:, start : start + LANE]
    return jnp.sum(parts, axis=1, keepdims=True)


class Shape:
    def __init__(self, side, channels, hid):
        self.side = side
        self.rows = side * side
        self.c = channels
        self.nc = channels // LANE
        self.hid = hid
        self.bias_rows = hid // channels
        self.gate_at = 11 + self.bias_rows
        self.kernel_at = self.gate_at + GATES
        self.taps = [(2 * n + 3) ** 2 for n in range(LEVELS)]
        self.nvec = self.kernel_at + sum(self.taps)
        self.high = side + 2 * PAD + 1
        self.padded = (self.nc, self.high, side + 2 * EDGE, LANE)


def compute_scratch(s):
    flat = (s.rows, s.c)
    split = (s.nc, s.rows, LANE)
    grid = (s.nc, s.side, s.side, LANE)
    return dict(
        vc=pltpu.VMEM((s.nc, s.nvec, LANE), f32),
        mask=pltpu.VMEM((s.rows, LANE), f32),
        xh1=pltpu.VMEM(flat, f32),
        r1=pltpu.VMEM((s.rows, LANE), f32),
        n1b=pltpu.VMEM(flat, b16),
        gate=pltpu.VMEM((GATES, s.rows, LANE), f32),
        q=pltpu.VMEM(flat, f32),
        pads=[pltpu.VMEM(s.padded, f32) for _ in range(LEVELS + 1)],
        gd=[pltpu.VMEM(grid, f32) for _ in range(LEVELS)],
        sums=pltpu.VMEM((s.side,) + s.padded[2:], f32),
        summed=pltpu.VMEM(grid, f32),
        sumb=pltpu.VMEM(flat, b16),
        mod=pltpu.VMEM(flat, f32),
        mixb=pltpu.VMEM(flat, b16),
        proj=pltpu.VMEM(flat, f32),
        mid=pltpu.VMEM(flat, f32),
        xh2=pltpu.VMEM(flat, f32),
        r2=pltpu.VMEM((s.rows, LANE), f32),
        n2b=pltpu.VMEM(flat, b16),
        dshrb=pltpu.VMEM(flat, b16),
        actb=pltpu.VMEM((s.rows, s.hid), b16),
        dhidb=pltpu.VMEM((s.rows, s.hid), b16),
        shr=pltpu.VMEM(flat, f32),
        dn=pltpu.VMEM(flat, f32),
        dqb=pltpu.VMEM(flat, b16),
        dsum=pltpu.VMEM(split, f32),
        dgate=pltpu.VMEM((GATES, s.rows, LANE), f32),
        dctxb=pltpu.VMEM(flat, b16),
        gacc=pltpu.VMEM((s.nc, sum(s.taps), 8, LANE), f32),
        pool=pltpu.VMEM((2, 8, s.c), f32),
    )


class Compute:
    def __init__(self, s, refs, scratch):
        self.s = s
        self.__dict__.update(refs)
        self.__dict__.update(scratch)
        self.dmid, self.dprojb, self.dmodb = self.mid, self.dshrb, self.n2b

    def row(self, index):
        return self.v[index : index + 1, :]

    def wide_mask(self, at):
        m = self.mask[at, :]
        return jnp.concatenate([m] * self.s.nc, axis=1)

    def wide(self, ref, at):
        m = ref[at, :]
        return jnp.concatenate([m] * self.s.nc, axis=1)

    def blocks(self, body, sums=0):
        s = self.s
        start = tuple(jnp.zeros((8, s.c), f32) for _ in range(sums))

        def step(index, carry):
            at = pl.ds(pl.multiple_of(index * BLK, BLK), BLK)
            parts = body(at, pl.ds(index * (BLK // s.side), BLK // s.side))
            if not sums:
                return carry
            return tuple(total + tall(part) for total, part in zip(carry, parts))

        return lax.fori_loop(0, s.rows // BLK, step, start)

    def image(self, ref, lines):
        return ref[lines].astype(f32).reshape(BLK, self.s.c)

    def store(self, ref, lines, values):
        ref[lines] = values.reshape(BLK // self.s.side, self.s.side, self.s.c).astype(ref.dtype)

    def put(self, index, total):
        self.gv[index : index + 1, :] = jnp.sum(total, axis=0, keepdims=True)

    def prepare(self):
        s = self.s
        shape = (s.side, s.side, LANE)
        side = jnp.where(self.count > 0, self.sides, 0)
        inside = (lax.broadcasted_iota(jnp.int32, shape, 0) < side) & (
            lax.broadcasted_iota(jnp.int32, shape, 1) < side
        )
        self.mask[...] = jnp.where(inside, 1.0, 0.0).astype(f32).reshape(s.rows, LANE)

        def zero_plane(index, carry):
            for pad in self.pads:
                for ch in range(s.nc):
                    pad[ch, index, 0:EDGE, :] = jnp.zeros((EDGE, LANE), f32)
                    pad[ch, index, EDGE + s.side :, :] = jnp.zeros((EDGE, LANE), f32)
            return carry

        lax.fori_loop(0, s.high, zero_plane, 0)
        for pad in self.pads:
            for ch in range(s.nc):
                for edge in list(range(PAD)) + list(range(PAD + s.side, s.high)):
                    pad[ch, edge, EDGE : EDGE + s.side, :] = jnp.zeros((s.side, LANE), f32)

    def first_norm(self):
        s = self.s

        def norm(at, lines):
            x = self.image(self.x, lines)
            centred = x - lane_sum(x) * (1.0 / s.c)
            r = lax.rsqrt(lane_sum(centred * centred) * (1.0 / s.c) + norm_eps)
            self.xh1[at, :] = centred * r
            self.r1[at, :] = jnp.broadcast_to(r, (BLK, LANE))

        self.blocks(norm)

    def first(self):
        s = self.s
        for ch in range(s.nc):
            self.vc[ch] = self.v[: s.nvec, ch * LANE : (ch + 1) * LANE]
        gain, shift = self.row(0), self.row(1)
        weights = [self.row(s.gate_at + l) for l in range(GATES)]

        def step(at, lines):
            n1 = self.xh1[at, :] * gain + shift
            self.n1b[at, :] = n1.astype(b16)
            for l in range(GATES):
                self.gate[l, at, :] = jnp.broadcast_to(lane_sum(n1 * weights[l]), (BLK, LANE))

        self.blocks(step)

    def context(self, chunks):
        s = self.s
        lanes = slice(chunks[0] * LANE, (chunks[-1] + 1) * LANE)
        ctx = mm(self.n1b[...], self.wc(chunks)) + self.v[3:4, lanes]
        m = self.mask[...]
        for i, ch in enumerate(chunks):
            part = ctx[:, i * LANE : (i + 1) * LANE] * m
            self.pads[0][ch, PAD : PAD + s.side, EDGE : EDGE + s.side, :] = part.reshape(
                s.side, s.side, LANE
            )

    def query(self):
        self.q[...] = mm(self.n1b[...], self.wq()) + self.row(2)

    def plane_sum(self, plane, count, at):
        def row(n):
            ref, base, stride = plane
            return ref[base + stride * n]

        for n in range(count):
            self.sums[at + n] = row(2 * n + 1) + row(2 * n + 2)
        return (self.sums, at, 1)

    def direct_rows(self, plane, taps, rows, weights=None):
        s = self.s
        ref, base, stride = plane
        out, grads = [None] * rows, {}
        for dc, column in taps.items():
            k = len(column)
            sums = [None] * k
            for a in range(rows + k - 1):
                x = ref[base + stride * a, pl.ds(EDGE + dc, s.side), :]
                for o in range(max(0, a - k + 1), min(rows, a + 1)):
                    t = a - o
                    term = x * column[t]
                    out[o] = term if out[o] is None else out[o] + term
                    if weights is not None:
                        part = tall(x * weights[o])
                        sums[t] = part if sums[t] is None else sums[t] + part
            grads[dc] = sums
        return out, grads

    def fast_rows(self, plane, taps, rows, depth, weights=None, at=0):
        length = len(next(iter(taps.values())))
        if depth == 0 or length == 1:
            return self.direct_rows(plane, taps, rows, weights)
        if rows % 2:
            ref, base, stride = plane
            last = (ref, base + stride * (rows - 1), stride)
            head = None if weights is None else weights[:-1]
            out, grads = self.fast_rows(plane, taps, rows - 1, depth, head, at)
            more, more_grads = self.direct_rows(last, taps, 1, None if weights is None else weights[-1:])
            if weights is not None:
                for dc in taps:
                    grads[dc] = [x + y for x, y in zip(grads[dc], more_grads[dc])]
            return out + more, grads
        n = rows // 2
        ref, base, stride = plane
        even, odd = (ref, base, 2 * stride), (ref, base + stride, 2 * stride)
        e_taps = {dc: column[0::2] for dc, column in taps.items()}
        o_taps = {dc: column[1::2] for dc, column in taps.items()}
        s_taps = {
            dc: [x + o_taps[dc][i] if i < len(o_taps[dc]) else x for i, x in enumerate(column)]
            for dc, column in e_taps.items()
        }
        count = n + (length + 1) // 2 - 1
        summed = self.plane_sum(plane, count, at)
        at = at + count
        wa = wb = ws = None
        if weights is not None:
            we, wo = weights[0::2], weights[1::2]
            wa = [we[0]] + [we[i] - wo[i - 1] for i in range(1, n)] + [0.0 - wo[n - 1]]
            wb = [we[i] - wo[i] for i in range(n)]
            ws = wo
        a_out, a_grad = self.fast_rows(even, e_taps, n + 1, depth - 1, wa, at)
        b_out, b_grad = self.fast_rows(odd, o_taps, n, depth - 1, wb, at)
        s_out, s_grad = self.fast_rows(summed, s_taps, n, depth - 1, ws, at)
        out, grads = [], {}
        for i in range(n):
            out += [a_out[i] + b_out[i], s_out[i] - a_out[i + 1] - b_out[i]]
        if weights is not None:
            for dc in taps:
                column = []
                for i in range(length):
                    both = (a_grad if i % 2 == 0 else b_grad)[dc][i // 2]
                    column.append(both + s_grad[dc][i // 2])
                grads[dc] = column
        return out, grads

    def level(self, l, chunks, depth=1):
        s = self.s
        k = 2 * l + 3
        p = l + 1
        offset = s.kernel_at + sum(s.taps[:l])

        def step(ch, carry):
            taps = {
                dc: [
                    self.vc[ch, pl.ds(offset + t * k + dc + p, 1), :]
                    for t in range(k)
                ]
                for dc in range(-p, p + 1)
            }
            plane = (self.pads[l].at[ch], PAD - p, 1)
            out, _ = self.fast_rows(plane, taps, s.side, depth)
            for r in range(s.side):
                at = slice(r * s.side, (r + 1) * s.side)
                m = self.mask[at, :]
                value, slope = gelu_parts(out[r])
                value = value * m
                self.gd[l][ch, r] = slope * m
                self.pads[l + 1][ch, r + PAD, EDGE : EDGE + s.side, :] = value
                term = value * self.gate[l, at, :]
                if l:
                    term = term + self.summed[ch, r]
                self.summed[ch, r] = term
            return carry

        lax.fori_loop(chunks[0], chunks[-1] + 1, step, 0)

    def pooling(self):
        s = self.s
        area = (self.sides * self.sides).astype(f32)
        for ch in range(s.nc):
            last = self.pads[LEVELS][ch, PAD : PAD + s.side, EDGE : EDGE + s.side, :]
            total = jnp.sum(tall(last.reshape(s.rows, LANE)), axis=0, keepdims=True)
            value, slope = gelu_parts(total / area)
            cols = slice(ch * LANE, (ch + 1) * LANE)
            self.pool[0, :, cols] = jnp.broadcast_to(value, (8, LANE))
            self.pool[1, :, cols] = jnp.broadcast_to(slope / area, (8, LANE))

        def step(index, carry):
            at = pl.ds(pl.multiple_of(index * BLK, BLK), BLK)
            gate = self.gate[LEVELS, at, :]
            for ch in range(s.nc):
                cols = slice(ch * LANE, (ch + 1) * LANE)
                part = self.summed[ch, pl.ds(index * (BLK // s.side), BLK // s.side)].reshape(BLK, LANE)
                self.sumb[at, cols] = (part + gate * self.pool[0, 0:1, cols]).astype(b16)
            return carry

        lax.fori_loop(0, s.rows // BLK, step, 0)

    def modulate(self):
        s = self.s
        self.mod[...] = mm(self.sumb[...], self.wh()) + self.row(4)

        def mix(at, lines):
            self.mixb[at, :] = (self.q[at, :] * self.mod[at, :]).astype(b16)

        self.blocks(mix)
        self.proj[...] = mm(self.mixb[...], self.wp()) + self.row(5)
        scale, gain, shift = self.row(6), self.row(7), self.row(8)
        upscale = self.row(10)

        def norm(at, lines):
            mid = self.image(self.x, lines) + scale * self.proj[at, :]
            self.mid[at, :] = mid
            centred = mid - lane_sum(mid) * (1.0 / s.c)
            r = lax.rsqrt(lane_sum(centred * centred) * (1.0 / s.c) + norm_eps)
            xh = centred * r
            self.xh2[at, :] = xh
            self.r2[at, :] = jnp.broadcast_to(r, (BLK, LANE))
            self.n2b[at, :] = (xh * gain + shift).astype(b16)
            d_shr = self.image(self.cot, lines) * self.wide_mask(at) * upscale
            self.dshrb[at, :] = d_shr.astype(b16)
            return (d_shr,)

        (g_b2,) = self.blocks(norm, 1)
        self.put(9, g_b2)

    def slope_tile(self, tile):
        s = self.s
        index, part = divmod(tile, s.nc)
        lanes = slice(part * LANE, (part + 1) * LANE)
        if index == 0:
            return self.dsum.at[part], (s.rows, LANE)
        if index == 1:
            return self.grad.at[:, :, lanes], (s.side, s.side, LANE)
        return (self.dn if index == 2 else self.shr).at[:, lanes], (s.rows, LANE)

    def feed(self, wide=256):
        s = self.s
        half = s.hid // 2
        for j in range(s.hid // wide):
            cols = slice(j * wide, (j + 1) * wide)
            h, at = divmod(j * wide, half)
            bias = []
            for start in range(j * wide, (j + 1) * wide, LANE):
                r, c = divmod(start, s.c)
                bias.append(self.v[11 + r : 12 + r, c : c + LANE])
            hid = mm(self.n2b[...], self.w1(h, at, wide)) + jnp.concatenate(bias, axis=1)
            act, slope = gelu_parts(hid)
            self.actb[:, cols] = act.astype(b16)
            for i in range(wide // LANE):
                ref, shape = self.slope_tile(j * wide // LANE + i)
                ref[...] = slope[:, i * LANE : (i + 1) * LANE].reshape(shape)

    def feed_back(self, wide=256):
        s = self.s
        for j in range(s.hid // wide):
            d_act = mm_t(self.dshrb[...], self.w2(j * wide, wide))
            for i in range(wide // LANE):
                ref, _ = self.slope_tile(j * wide // LANE + i)
                d_hid = d_act[:, i * LANE : (i + 1) * LANE] * ref[...].reshape(s.rows, LANE)
                start = j * wide + i * LANE
                self.dhidb[:, start : start + LANE] = d_hid.astype(b16)
                r, c = divmod(start, s.c)
                self.gv[11 + r : 12 + r, c : c + LANE] = jnp.sum(tall(d_hid), axis=0, keepdims=True)

    def shrink_grad(self):
        s = self.s
        for at in range(0, s.hid, s.c):
            self.put_g2(at, s.c, mm_g(self.actb[:, at : at + s.c], self.dshrb[...]))

    def expand_grad(self):
        s = self.s
        half = s.hid // 2
        for at in range(0, s.hid, s.c):
            self.put_g1(at // half, at % half, mm_g(self.n2b[...], self.dhidb[:, at : at + s.c]))

    def feed_out(self):
        s = self.s
        half = s.hid // 2
        self.shr[...] = mm(self.actb[...], self.w2(0, s.hid)) + self.row(9)
        self.dn[...] = mm_t(self.dhidb[:, :half], self.w1(0, 0, half)) + mm_t(
            self.dhidb[:, half:], self.w1(1, 0, half)
        )

    def middle(self):
        s = self.s
        gain, scale, upscale = self.row(7), self.row(6), self.row(10)

        def step(at, lines):
            shr, mid, proj, xh = self.shr[at, :], self.mid[at, :], self.proj[at, :], self.xh2[at, :]
            m = self.wide_mask(at)
            u = self.image(self.cot, lines) * m
            self.store(self.out, lines, (mid + upscale * shr) * m)
            d = self.dn[at, :]
            e = d * gain
            mean_e = lane_sum(e) * (1.0 / s.c)
            mean_x = lane_sum(e * xh) * (1.0 / s.c)
            d_mid = u + self.wide(self.r2, at) * (e - mean_e - xh * mean_x)
            self.dmid[at, :] = d_mid
            d_proj = scale * d_mid
            self.dprojb[at, :] = d_proj.astype(b16)
            return u * shr, d * xh, d, d_mid * proj, d_proj

        sums = self.blocks(step, 5)
        for index, total in zip((10, 7, 8, 6, 5), sums):
            self.put(index, total)
        self.dn[...] = mm_t(self.dprojb[...], self.wp())

        def split(at, lines):
            d = self.dn[at, :]
            d_q = d * self.mod[at, :]
            d_mod = d * self.q[at, :]
            self.dqb[at, :] = d_q.astype(b16)
            self.dmodb[at, :] = d_mod.astype(b16)
            return d_q, d_mod

        g_bq, g_bh = self.blocks(split, 2)
        self.put(2, g_bq)
        self.put(4, g_bh)
        d_sum = mm_t(self.dmodb[...], self.wh())
        for ch in range(s.nc):
            self.dsum[ch] = d_sum[:, ch * LANE : (ch + 1) * LANE]

    def middle_grads(self):
        self.put_gp(mm_g(self.mixb[...], self.dprojb[...]))
        self.put_gh(mm_g(self.sumb[...], self.dmodb[...]))

    def query_grad(self):
        self.put_gq(mm_g(self.n1b[...], self.dqb[...]))

    def focal_top(self):
        s = self.s

        def step(index, carry):
            at = pl.ds(pl.multiple_of(index * BLK, BLK), BLK)
            gate = self.gate[LEVELS, at, :]
            sums = [jnp.zeros((BLK, LANE), f32) for _ in range(GATES)]
            out = []
            for ch in range(s.nc):
                cols = slice(ch * LANE, (ch + 1) * LANE)
                d = self.dsum[ch, at, :]
                values = [
                    self.pads[l][ch, pl.ds(index * (BLK // s.side) + PAD, BLK // s.side), EDGE : EDGE + s.side, :]
                    for l in range(1, LEVELS + 1)
                ]
                for l in range(LEVELS):
                    sums[l] = sums[l] + d * values[l].reshape(BLK, LANE)
                sums[LEVELS] = sums[LEVELS] + d * self.pool[0, 0:1, cols]
                out.append(carry[ch] + tall(d * gate))
            for l in range(GATES):
                self.dgate[l, at, :] = jnp.broadcast_to(
                    jnp.sum(sums[l], axis=1, keepdims=True), (BLK, LANE)
                )
            return tuple(out)

        zero = jnp.zeros((8, LANE), f32)
        totals = lax.fori_loop(0, s.rows // BLK, step, (zero,) * s.nc)
        for ch in range(s.nc):
            cols = slice(ch * LANE, (ch + 1) * LANE)
            total = jnp.sum(totals[ch], axis=0, keepdims=True)
            self.pool[1, :, cols] = self.pool[1, :, cols] * total

        def last(index, carry):
            at = pl.ds(pl.multiple_of(index * BLK, BLK), BLK)
            gate = self.gate[LEVELS - 1, at, :]
            for ch in range(s.nc):
                cols = slice(ch * LANE, (ch + 1) * LANE)
                e = self.dsum[ch, at, :] * gate + self.pool[1, 0:1, cols]
                d = e.reshape(BLK // s.side, s.side, LANE) * self.gd[LEVELS - 1][ch, pl.ds(index * (BLK // s.side), BLK // s.side)]
                self.pads[LEVELS][ch, pl.ds(index * (BLK // s.side) + PAD, BLK // s.side), EDGE : EDGE + s.side, :] = d
            return carry

        lax.fori_loop(0, s.rows // BLK, last, 0)

    def level_back(self, l, chunks, depth=2):
        s = self.s
        k = 2 * l + 3
        p = l + 1
        base = sum(s.taps[:l])
        offset = s.kernel_at + base

        def step(ch, carry):
            taps = {
                dc: [
                    self.vc[ch, pl.ds(offset + (k - 1 - t) * k + p - dc, 1), :]
                    for t in range(k)
                ]
                for dc in range(-p, p + 1)
            }
            plane = (self.pads[l + 1].at[ch], PAD - p, 1)
            inputs = [self.pads[l][ch, r + PAD, EDGE : EDGE + s.side, :] for r in range(s.side)]
            out, grads = self.fast_rows(plane, taps, s.side, depth, inputs)
            for dc, column in grads.items():
                for t, value in enumerate(column):
                    self.gacc[ch, base + (k - 1 - t) * k + p - dc] = value
            for r in range(s.side):
                at = slice(r * s.side, (r + 1) * s.side)
                if l:
                    e = out[r] + self.dsum[ch, at, :] * self.gate[l - 1, at, :]
                    self.pads[l][ch, r + PAD, EDGE : EDGE + s.side, :] = e * self.gd[l - 1][ch, r]
                else:
                    self.summed[ch, r] = out[r] * self.mask[at, :]
            return carry

        lax.fori_loop(chunks[0], chunks[-1] + 1, step, 0)

    def context_grad(self, chunks):
        s = self.s

        def step(index, carry):
            at = pl.ds(pl.multiple_of(index * BLK, BLK), BLK)
            out = []
            for i, ch in enumerate(chunks):
                cols = slice(ch * LANE, (ch + 1) * LANE)
                lines = pl.ds(index * (BLK // s.side), BLK // s.side)
                d = self.summed[ch, lines].reshape(BLK, LANE)
                self.dctxb[at, cols] = d.astype(b16)
                out.append(carry[i] + tall(d))
            return tuple(out)

        zero = jnp.zeros((8, LANE), f32)
        totals = lax.fori_loop(0, s.rows // BLK, step, (zero,) * len(chunks))
        for i, ch in enumerate(chunks):
            cols = slice(ch * LANE, (ch + 1) * LANE)
            self.gv[3:4, cols] = jnp.sum(totals[i], axis=0, keepdims=True)
            self.gv[s.kernel_at : s.nvec, cols] = jnp.sum(self.gacc[ch], axis=1)
        lanes = slice(chunks[0] * LANE, (chunks[-1] + 1) * LANE)
        self.put_gc(chunks, mm_g(self.n1b[...], self.dctxb[:, lanes]))

    def last_sums(self):
        s = self.s
        wc = self.wc(tuple(range(s.nc)))
        self.dn[...] = mm_t(self.dqb[...], self.wq()) + mm_t(self.dctxb[...], wc)
        gain, shift = self.row(0), self.row(1)
        weights = [self.row(s.gate_at + l) for l in range(GATES)]

        def step(at, lines):
            xh = self.xh1[at, :]
            n1 = xh * gain + shift
            d = self.dn[at, :]
            sums = []
            for l in range(GATES):
                dg = self.wide(self.dgate.at[l], at)
                d = d + dg * weights[l]
                sums.append(dg * n1)
            self.dn[at, :] = d
            return (d * xh, d) + tuple(sums)

        sums = self.blocks(step, 2 + GATES)
        for index, total in zip((0, 1) + tuple(s.gate_at + l for l in range(GATES)), sums):
            self.put(index, total)

    def last_out(self):
        s = self.s
        gain = self.row(0)

        def step(at, lines):
            xh = self.xh1[at, :]
            e = self.dn[at, :] * gain
            mean_e = lane_sum(e) * (1.0 / s.c)
            mean_x = lane_sum(e * xh) * (1.0 / s.c)
            d_in = self.dmid[at, :] + self.wide(self.r1, at) * (e - mean_e - xh * mean_x)
            self.store(self.grad, lines, d_in)

        self.blocks(step)


MESH = pl.DeviceIdType.MESH
STEP = 10
beta_one = 0.9
beta_two = 0.95
adam_eps = 1e-08
weight_decay = 0.05
VMEM_BYTES = 63 * 2**20 + 2**19
GATHERED = "vabmes"
REDUCED = "semqtu"
PAIRS = "se"
DIRECT = "qtu"
NEAR = "va"
HALVED = "es"
AT_ONCE = "vab"


class Plan:
    def __init__(self, n_grp, n_fs, s):
        self.X = n_grp // 2
        self.Y = 2 ** (int(math.log2(n_fs)) // 2)
        self.Z = n_fs // self.Y
        self.fs = n_fs
        self.s = s
        self.rows = s.c // n_fs
        self.rp = -(-self.rows // 16) * 16
        self.rows2 = s.hid // n_fs // 2
        self.rp2 = -(-self.rows2 // 16) * 16
        self.even = self.rp == self.rows and self.rp2 == self.rows2
        self.rv = self.rp // 2
        self.gather_cols = dict(v=LANE, a=LANE, b=2 * LANE, m=s.c)
        self.rs = self.rp2 // 2
        self.reduce_cols = dict(s=s.c, e=s.hid // 4, m=s.c, q=2 * LANE, t=LANE, u=LANE)

    def piece(self, name):
        if name == "e":
            return (2, self.rp, self.s.c)
        if name == "s":
            return (2, self.rs, self.s.c)
        return (self.rv if name == "v" else self.rp, self.gather_cols[name])

    def whole(self, name):
        piece = self.piece(name)
        if name == "e":
            return (2, 2, self.Z, self.Y) + piece[1:]
        if name in "sv":
            return (self.Z, self.Y, 2) + piece
        return (2, self.Z, self.Y) + piece


def gather_scratch(p, name):
    piece = p.piece(name)
    kind = f32 if name == "v" else b16
    passed = piece[1:] if name in HALVED and p.X == 2 else piece
    return dict(
        cand=pltpu.VMEM((2,) + piece, kind),
        rx1=pltpu.VMEM(piece, kind),
        sel=pltpu.VMEM(piece, kind),
        rx2=pltpu.VMEM((p.X - 1, 2 if name in NEAR else 1) + passed, kind),
        full=pltpu.VMEM(p.whole(name), kind),
    )


def reduce_piece(p, name):
    return (p.rs if name == "s" else p.rp, p.reduce_cols[name])


def fin_shape(p, name):
    return (2, 2) + reduce_piece(p, name) if name in PAIRS else (2,) + reduce_piece(p, name)


def grad_shape(p, name):
    if name == "s":
        return (p.Z, p.Y, 2, 2) + reduce_piece(p, name)
    return ((2, 2) if name in PAIRS else (2,)) + (p.Z, p.Y) + reduce_piece(p, name)


def steps_scratch(p, name):
    piece = reduce_piece(p, name)
    out = dict(
        r1=pltpu.VMEM((p.Z, p.Y) + piece, b16),
        a3=pltpu.VMEM(piece, b16),
        a4=pltpu.VMEM(piece, f32),
        r4=pltpu.VMEM((p.X - 1, 2) + piece, b16),
        r5=pltpu.VMEM(piece, b16),
    )
    if name in DIRECT:
        out["r3"] = pltpu.VMEM((p.fs - 1,) + piece, b16)
    else:
        out["r2"] = pltpu.VMEM((p.Y - 1, p.Z) + piece, b16)
        out["a2"] = pltpu.VMEM((p.Z,) + piece, b16)
        out["r3"] = pltpu.VMEM((p.Z - 1,) + piece, b16)
    return out


def reduce_scratch(p, name):
    out = dict(grad=pltpu.VMEM(grad_shape(p, name), b16), fin=pltpu.VMEM(fin_shape(p, name), f32))
    if name not in PAIRS:
        out["steps"] = steps_scratch(p, name)
    elif p.X == 2:
        out["steps"] = steps_scratch(p, name)
        out["other"] = pltpu.VMEM((p.Z, p.Y) + reduce_piece(p, name), b16)
        out["rx"] = pltpu.VMEM((p.Z, p.Y) + reduce_piece(p, name), b16)
    else:
        out["parts"] = [steps_scratch(p, name) for _ in range(2)]
    return out


def sem_count(p):
    gather = 1 + 2 * (p.X - 1) + (p.Z - 1) + p.Z * (p.Y - 1) + 3 * p.fs
    reduce = 1 + max((p.Y - 1) + (p.Z - 1), p.fs - 1) + 2 * (p.X - 1) + 1
    return gather * len(GATHERED) + reduce * (len(REDUCED) + len(PAIRS))


class Links:
    def __init__(self, p, send_sem, recv_sem, column_sem):
        self.p, self.column_sem = p, column_sem
        self.send_sem, self.recv_sem = send_sem, recv_sem
        self.used = 0
        self.sent = []
        self.g, self.f = lax.axis_index("grp"), lax.axis_index("fs")
        self.x, self.c = lax.div(self.g, 2), lax.rem(self.g, 2)
        self.z, self.y = lax.div(self.f, p.Y), lax.rem(self.f, p.Y)

    def sibling(self):
        return (self.x * 2 + 1 - self.c, self.f)

    def at_x(self, x, other_core=0):
        core = 1 - self.c if other_core else self.c
        return (x * 2 + core, self.f)

    def at_z(self, z):
        return (self.g, z * self.p.Y + self.y)

    def at_y(self, y):
        return (self.g, self.z * self.p.Y + y)

    def flip_z(self, bit):
        return self.z + bit - 2 * bit * lax.rem(lax.div(self.z, bit), 2)

    def signal_partners(self):
        p = self.p
        partners = (
            [self.sibling()]
            + [self.at_x(lax.rem(self.x + d, p.X), i) for d in range(1, p.X) for i in range(2)]
            + [self.at_z(lax.rem(self.z + d, p.Z)) for d in range(1, p.Z)]
            + [self.at_y(lax.rem(self.y + d, p.Y)) for d in range(1, p.Y)]
        )
        self.partners = len(partners)
        barrier = pltpu.get_barrier_semaphore()
        for partner in partners:
            pl.semaphore_signal(barrier, inc=1, device_id=partner, device_id_type=MESH)

    def wait_partners(self):
        pl.semaphore_wait(pltpu.get_barrier_semaphore(), self.partners)
        self.heard = False
        for d in range(1, self.p.Y):
            partner = self.at_y(lax.rem(self.y + d, self.p.Y))
            pl.semaphore_signal(self.column_sem, inc=1, device_id=partner, device_id_type=MESH)

    def hear_columns(self):
        if not self.heard:
            pl.semaphore_wait(self.column_sem, self.p.Y - 1)
            self.heard = True

    def send(self, source, target, partner, arriving=None):
        index = self.used
        self.used += 1

        def copy(src, dst):
            return pltpu.make_async_remote_copy(
                src_ref=src,
                dst_ref=dst,
                send_sem=self.send_sem.at[index],
                recv_sem=self.recv_sem.at[index],
                device_id=partner,
                device_id_type=MESH,
            )

        started = copy(source, target)
        started.start()
        self.sent.append(started)
        coming = copy(source, target if arriving is None else arriving)
        return coming.wait_recv

    def finish(self):
        for copy in self.sent:
            copy.wait_send()


class Gather:
    def __init__(self, name, links, refs):
        self.name, self.links, self.p = name, links, links.p
        self.near, self.direct = name in NEAR, name in AT_ONCE
        self.split = name in HALVED and links.p.X == 2
        self.waitx = []
        self.__dict__.update(refs)
        self.held, self.wait3, self.wait4, self.wait5 = [], [], [], []

    def piece(self, half, z, y, x=None):
        if self.split:
            part = self.links.x if x is None else x
            return self.full.at[z, y, half, part] if self.name == "s" else self.full.at[half, part, z, y]
        if self.name == "e":
            return self.full.at[half, :, z, y]
        return self.full.at[z, y, half] if self.name in "sv" else self.full.at[half, z, y]

    def core_send(self, z, y):
        k = self.links
        here = self.piece(k.c, z, y)
        self.wait5.append(k.send(here, here, k.sibling(), self.piece(1 - k.c, z, y)))
        if self.split:
            there = self.piece(k.c, z, y, 1 - k.x)
            self.waitx.append((k.send(here, here, k.at_x(1 - k.x), there), z, y))

    def one(self):
        k, p = self.links, self.p
        self.wait1 = k.send(self.cand.at[1 - k.c], self.rx1, k.sibling())
        if self.near:
            self.wait2 = []
            for d in range(1, p.X):
                x = lax.rem(k.x + d, p.X)
                for i, h in enumerate((k.c, 1 - k.c)):
                    self.wait2.append(k.send(self.cand.at[h], self.rx2.at[d - 1, i], k.at_x(x, i)))

    def two(self):
        k, p = self.links, self.p
        self.wait1()
        self.sel[...] = self.cand[k.c] + self.rx1[...]
        if self.split:
            self.wait2 = [k.send(self.sel.at[1 - k.x], self.rx2.at[0, 0], k.at_x(1 - k.x))]
        elif not self.near:
            self.wait2 = [
                k.send(self.sel, self.rx2.at[d - 1, 0], k.at_x(lax.rem(k.x + d, p.X)))
                for d in range(1, p.X)
            ]

    def y_sends(self, z):
        k, p = self.links, self.p
        here = self.piece(k.c, z, k.y)
        for d in range(1, p.Y):
            other = lax.rem(k.y + p.Y - d, p.Y)
            partner = k.at_y(lax.rem(k.y + d, p.Y))
            wait = k.send(here, here, partner, self.piece(k.c, z, other))
            self.wait4.append((wait, z, other))

    def pair_round(self):
        k = self.links
        bit = self.p.Z >> (self.rounds + 1)
        partner = k.at_z(k.flip_z(bit))
        self.rounds += 1
        for z in self.held:
            other = z + bit - 2 * bit * lax.rem(lax.div(z, bit), 2)
            here = self.piece(k.c, z, k.y)
            wait = k.send(here, here, partner, self.piece(k.c, other, k.y))
            self.wait3.append((wait, other))

    def three(self):
        k, p = self.links, self.p
        for wait in self.wait2:
            wait()
        total = self.sel[k.x] if self.split else self.sel[...]
        for d in range(p.X - 1):
            for i in range(2 if self.near else 1):
                total = total + self.rx2[d, i]
        here = self.piece(k.c, k.z, k.y)
        here[...] = total
        self.held, self.rounds = [k.z], 0
        if self.direct:
            for d in range(1, p.Z):
                other = lax.rem(k.z + p.Z - d, p.Z)
                partner = k.at_z(lax.rem(k.z + d, p.Z))
                wait = k.send(here, here, partner, self.piece(k.c, other, k.y))
                self.wait3.append((wait, other))
        else:
            self.pair_round()

    def own(self):
        self.y_sends(self.links.z)
        self.core_send(self.links.z, self.links.y)

    def four(self):
        waits, self.wait3 = self.wait3, []
        for wait, z in waits:
            wait()
            self.held.append(z)
        if len(self.held) < self.p.Z:
            self.pair_round()
        for _, z in waits:
            self.y_sends(z)
            self.core_send(z, self.links.y)

    def five(self):
        while self.wait3:
            self.four()
        for wait, z, y in self.wait4:
            wait()
            self.core_send(z, y)

    def cross(self):
        k = self.links
        for wait, z, y in self.waitx:
            wait()
            here = self.piece(k.c, z, y, 1 - k.x)
            self.wait5.append(k.send(here, here, k.sibling(), self.piece(1 - k.c, z, y, 1 - k.x)))

    def six(self):
        for wait in self.wait5:
            wait()


class Reduce:
    def __init__(self, name, links, refs, half, fin):
        self.name, self.links, self.p = name, links, links.p
        self.direct = name in DIRECT
        self.__dict__.update(refs)
        self.half, self.fin = half, fin

    def one(self):
        k = self.links
        self.wait1 = k.send(self.half(1 - k.c), self.r1, k.sibling())

    def two(self):
        k, p = self.links, self.p
        self.wait1()
        mine = self.half(k.c)

        def add(index, carry):
            z, y = lax.div(index, p.Y), lax.rem(index, p.Y)
            self.r1[z, y] = self.r1[z, y] + mine[z, y]
            return carry

        lax.fori_loop(0, p.fs, add, 0)
        self.wait2 = []
        if self.direct:
            k.hear_columns()
            for d in range(1, p.fs):
                f = lax.rem(k.f + d, p.fs)
                source = self.r1.at[lax.div(f, p.Y), lax.rem(f, p.Y)]
                self.wait2.append(k.send(source, self.r3.at[d - 1], (k.g, f)))
            return
        for d in range(1, p.Y):
            other = lax.rem(k.y + d, p.Y)
            self.wait2.append(k.send(self.r1.at[:, other], self.r2.at[d - 1], k.at_y(other)))

    def three(self):
        k, p = self.links, self.p
        for wait in self.wait2:
            wait()
        self.wait3 = []
        if self.direct:
            total = self.r1[k.z, k.y].astype(f32)
            for d in range(p.fs - 1):
                total = total + self.r3[d].astype(f32)
            self.a4[...] = total
            return

        def add(z, carry):
            total = self.r1[z, k.y].astype(f32)
            for d in range(p.Y - 1):
                total = total + self.r2[d, z].astype(f32)
            self.a2[z] = total.astype(b16)
            return carry

        lax.fori_loop(0, p.Z, add, 0)
        self.bit, self.slot = 1, 0
        self.pair_round()

    def pair_round(self):
        k, p = self.links, self.p
        bit = self.bit
        partner = k.flip_z(bit)
        low_partner, own = lax.rem(partner, 2 * bit), lax.rem(k.z, 2 * bit)
        self.wait3 = []
        for step in range(p.Z // (2 * bit)):
            target = low_partner + 2 * bit * step
            mine = own + 2 * bit * step
            wait = k.send(self.a2.at[target], self.r3.at[self.slot], k.at_z(partner))
            self.wait3.append((wait, mine, self.slot))
            self.slot += 1
        self.bit = 2 * bit

    def four(self):
        for wait, z, slot in self.wait3:
            wait()
            total = self.a2[z].astype(f32) + self.r3[slot].astype(f32)
            if self.bit < self.p.Z:
                self.a2[z] = total.astype(b16)
            else:
                self.a4[...] = total
        self.wait3 = []
        if not self.direct and self.bit < self.p.Z:
            self.pair_round()

    def five(self):
        k, p = self.links, self.p
        while self.wait3:
            self.four()
        self.a3[...] = self.a4[...].astype(b16)
        self.wait4 = []
        for d in range(1, p.X):
            x = lax.rem(k.x + d, p.X)
            for i in range(2):
                self.wait4.append(k.send(self.a3, self.r4.at[d - 1, i], k.at_x(x, i)))
        self.wait4.append(k.send(self.a3, self.r5, k.sibling()))

    def six(self):
        k, p = self.links, self.p
        for wait in self.wait4:
            wait()
        for h, total, i in ((k.c, self.a4[...], 0), (1 - k.c, self.r5[...].astype(f32), 1)):
            for d in range(p.X - 1):
                total = total + self.r4[d, i].astype(f32)
            self.fin(h)[...] = total


class Pair(Reduce):
    def __init__(self, name, links, refs):
        grad, fin = refs["grad"], refs["fin"]

        def half(h, part):
            return grad.at[:, :, h, part] if name == "s" else grad.at[h, part]

        self.parts = []
        if "parts" in refs:
            for part, steps in enumerate(refs["parts"]):
                reduce = Reduce(
                    name, links, steps, lambda h, part=part: half(h, part), lambda h, part=part: fin.at[h, part]
                )
                self.parts.append(reduce)
            return
        super().__init__(name, links, refs["steps"], half, fin)
        self.rx, self.other, self.all_fin = refs["rx"], refs["other"], fin

    def one(self):
        if self.parts:
            return [part.one() for part in self.parts]
        k = self.links
        self.wait1 = [
            k.send(self.half(1 - k.c, 1 - k.x), self.other, k.sibling()),
            k.send(self.half(1 - k.c, k.x), self.r1, k.sibling()),
        ]

    def add_pieces(self, total, term):
        p = self.p

        def add(index, carry):
            z, y = lax.div(index, p.Y), lax.rem(index, p.Y)
            total[z, y] = total[z, y] + term[z, y]
            return carry

        lax.fori_loop(0, p.fs, add, 0)

    def two(self):
        if self.parts:
            return [part.two() for part in self.parts]
        k = self.links
        self.wait1[0]()
        self.add_pieces(self.other, self.half(k.c, 1 - k.x))
        self.waitx = k.send(self.other, self.rx, k.at_x(1 - k.x))
        self.wait1[1]()
        self.add_pieces(self.r1, self.half(k.c, k.x))

    def across(self):
        if self.parts:
            return
        k, p = self.links, self.p
        self.waitx()
        self.add_pieces(self.r1, self.rx)
        self.wait2 = []
        for d in range(1, p.Y):
            other = lax.rem(k.y + d, p.Y)
            self.wait2.append(k.send(self.r1.at[:, other], self.r2.at[d - 1], k.at_y(other)))

    def three(self):
        return [part.three() for part in self.parts] if self.parts else super().three()

    def four(self):
        return [part.four() for part in self.parts] if self.parts else super().four()

    def five(self):
        return [part.five() for part in self.parts] if self.parts else super().five()

    def six(self):
        if self.parts:
            return [part.six() for part in self.parts]
        k = self.links
        for wait in self.wait4:
            wait()
        self.all_fin[k.c, k.x] = self.a4[...]
        self.all_fin[1 - k.c, k.x] = self.r5[...].astype(f32)
        self.all_fin[k.c, 1 - k.x] = self.r4[0, 0].astype(f32)
        self.all_fin[1 - k.c, 1 - k.x] = self.r4[0, 1].astype(f32)


def spread_matrix(rows, rp, count):
    bits = int(math.log2(rp))
    shape = (count * rows, count * rp)
    a = lax.broadcasted_iota(jnp.int32, shape, 0)
    b = lax.broadcasted_iota(jnp.int32, shape, 1)
    i = lax.bitwise_and(b, rp - 1)
    hit = (a == lax.shift_right_logical(b, bits) * rows + i) & (i < rows)
    return jnp.where(hit, 1.0, 0.0).astype(b16)


def block_kernel(p, tree, *refs):
    s = p.s
    count, sides, owners = refs[:3]
    sources = dict(zip(("x", "cot", "focal", "modulate", "project", "expand", "shrink", "vector"), refs[3:11]))
    out_hbm, grad_hbm = refs[11:13]
    fin_hbm = dict(zip(REDUCED, refs[13:19]))
    own = jax.tree.unflatten(tree, refs[19:])
    k = Links(p, own["send_sem"], own["recv_sem"], own["column_sem"])
    land, local_sem = own["land"], own["local_sem"]
    local_used = []

    def local(source, target):
        copy = pltpu.make_async_copy(source, target, local_sem.at[len(local_used)])
        local_used.append(copy)
        copy.start()
        return copy

    loads = {}
    for name in ("focal", "vector", "modulate", "project", "x", "expand", "shrink", "cot"):
        loads[name] = local(sources[name].at[0], land[name])
    k.signal_partners()

    def mine(index):
        return jnp.where(owners[index] == k.g, 1.0, 0.0).astype(f32)

    def cut(values, rows, rp):
        if rows == rp:
            return values
        return jnp.concatenate([values, jnp.zeros((rp - rows, values.shape[1]), f32)], axis=0)

    def candidate(name, h, values):
        rows, rp = values.shape[0], p.rp2 if name == "s" else p.rp
        low, target = cut(values, rows, rp).astype(b16), own["g" + name]["cand"]
        if name == "e":
            for part in range(2):
                target[h, part] = low[:, part * c : (part + 1) * c]
        elif name == "s":
            for part in range(2):
                target[h, part] = low[part * p.rs : (part + 1) * p.rs]
        else:
            target[h] = low

    gathers = {
        name: Gather(name, k, own["g" + name]) for name in GATHERED
    }
    gv, ga, gb, gm, ge, gs = (gathers[name] for name in GATHERED)
    reduces = {}
    for name in REDUCED:
        refs = own["r" + name]
        if name in PAIRS:
            reduces[name] = Pair(name, k, refs)
        else:
            reduces[name] = Reduce(
                name, k, refs["steps"], lambda h, r=refs: r["grad"].at[h], lambda h, r=refs: r["fin"].at[h]
            )
    rs, re, rm, rq, rt, ru = (reduces[name] for name in REDUCED)
    c, wide = s.c, s.hid // 2

    def prepare():
        block.prepare()
        own["gvec"][s.nvec :, :] = jnp.zeros((LANE - s.nvec, s.c), f32)
        put("q", 1, LANE, jnp.zeros((s.c, LANE), f32))
        loads["focal"].wait()
        loads["vector"].wait()
        values = cut(land["vector"][...] * mine(5), p.rows, p.rp)
        values = jnp.concatenate([values, jnp.zeros((p.rp, LANE - s.nvec), f32)], axis=1)
        focal = land["focal"]
        for h in range(2):
            own["gv"]["cand"][h] = values[h * p.rv : (h + 1) * p.rv]
            at = c + h * LANE
            candidate("a", h, focal[:, at : at + LANE] * mine(0))
        candidate("b", 0, jnp.concatenate([focal[:, c + 2 * LANE :], focal[:, :LANE]], axis=1) * mine(0))
        candidate("b", 1, focal[:, LANE:c] * mine(0))
        loads["modulate"].wait()
        loads["project"].wait()
        candidate("m", 0, land["modulate"][...] * mine(1))
        candidate("m", 1, land["project"][...] * mine(2))
        loads["expand"].wait()
        for h in range(2):
            candidate("e", h, land["expand"][:, h * wide : (h + 1) * wide] * mine(3))
        loads["shrink"].wait()
        for h in range(2):
            candidate("s", h, land["shrink"][h * p.rows2 : (h + 1) * p.rows2, :] * mine(4))
        loads["x"].wait()
        block.first_norm()

    if not p.even:
        own["map"][...] = spread_matrix(p.rows, p.rp, p.fs)

    def compact(values):
        return values if p.even else mm(own["map"][...], values).astype(b16)

    def spread(values):
        values = values.astype(b16)
        return values if p.even else mm_g(own["map"][...], values).astype(b16)

    def matrix(name, h, at, cols):
        part = own["g" + name]["full"][h, :, :, :, at : at + cols]
        return compact(part.reshape(p.fs * p.rp, cols))

    def take_expand(h, at, cols):
        parts = []
        for part in range(2):
            first, last = max(at, part * c), min(at + cols, (part + 1) * c)
            if first < last:
                values = own["ge"]["full"][h, part, :, :, :, first - part * c : last - part * c]
                parts.append(compact(values.reshape(p.fs * p.rp, last - first)))
        return jnp.concatenate(parts, axis=1) if len(parts) > 1 else parts[0]

    def take_context(chunks):
        parts = []
        if chunks[0] < 2:
            parts += [matrix("a", ch, 0, LANE) for ch in chunks if ch < 2]
        if chunks[-1] == 2:
            parts.append(matrix("b", 0, 0, LANE))
        return jnp.concatenate(parts, axis=1) if len(parts) > 1 else parts[0]

    def take_query():
        return jnp.concatenate([matrix("b", 0, LANE, LANE), matrix("b", 1, 0, 2 * LANE)], axis=1)

    def take_shrink(at, rows):
        if p.even:
            return own["gs"]["full"][...].reshape(s.hid, s.c)[at : at + rows]
        return own["w2n"][at : at + rows, :]

    def put(name, h, at, values):
        cols = values.shape[1]
        grads = spread(values).reshape(p.Z, p.Y, p.rp, cols)
        own["r" + name]["grad"][h, :, :, :, at : at + cols] = grads

    def put_expand(h, at, values):
        grads = spread(values).reshape(p.Z, p.Y, p.rp, values.shape[1])
        own["re"]["grad"][h, 1 if at else 0] = grads

    def put_query(values):
        put("q", 0, 0, values[:, : 2 * LANE])
        put("q", 1, 0, values[:, 2 * LANE :])

    def put_context(chunks, values):
        for i, ch in enumerate(chunks):
            name, h = (("t", 0), ("t", 1), ("u", 0))[ch]
            put(name, h, 0, values[:, i * LANE : (i + 1) * LANE])

    def put_shrink(at, rows, values):
        low = values.astype(b16)
        if not p.even:
            own["g2n"][at : at + rows, :] = low
            return
        start = at
        while start < at + rows:
            piece, inner = divmod(start, p.rs)
            size = min(p.rs - inner, at + rows - start)
            (f, h), part, first = divmod(piece // 2, 2), piece % 2, start - at
            own["rs"]["grad"][f // p.Y, f % p.Y, h, part, inner : inner + size, :] = low[first : first + size]
            start += size

    block = Compute(
        s,
        dict(
            x=land["x"],
            cot=land["cot"],
            v=own["v"],
            count=count[0, 0],
            sides=sides[0],
            out=own["out"],
            grad=own["grad"],
            gv=own["gvec"],
            wc=take_context,
            wq=take_query,
            wh=lambda: matrix("m", 0, 0, c),
            wp=lambda: matrix("m", 1, 0, c),
            w1=take_expand,
            w2=take_shrink,
            put_gq=put_query,
            put_gc=put_context,
            put_gh=lambda values: put("m", 0, 0, values),
            put_gp=lambda values: put("m", 1, 0, values),
            put_g1=put_expand,
            put_g2=put_shrink,
        ),
        own["compute"],
    )

    stores = []

    def settle(name):
        reduces[name].six()
        stores.append(local(own["r" + name]["fin"], fin_hbm[name]))

    def take_vector():
        vector = own["gv"]["full"][...].reshape(p.fs * p.rp, LANE)
        if not p.even:
            vector = jnp.dot(own["map"][...].astype(f32), vector, precision=lax.Precision.HIGHEST)
        own["v"][...] = vector.T

    def modulate():
        loads["cot"].wait()
        block.modulate()

    def close_shrink():
        def close(f, carry):
            z, y = lax.div(f, p.Y), lax.rem(f, p.Y)
            parts = [
                own["gs"]["full"][z, y, h].astype(f32).reshape(p.rp2, s.c)[: p.rows2] for h in range(2)
            ]
            at = pl.ds(pl.multiple_of(f * 2 * p.rows2, 2 * p.rows2), 2 * p.rows2)
            own["w2n"][at, :] = jnp.concatenate(parts, axis=0).astype(b16)
            return carry

        if not p.even:
            lax.fori_loop(0, p.fs, close, 0)

    def shrink_grad():
        block.shrink_grad()

        def open_up(f, carry):
            z, y = lax.div(f, p.Y), lax.rem(f, p.Y)
            at = pl.ds(pl.multiple_of(f * 2 * p.rows2, 2 * p.rows2), 2 * p.rows2)
            both = own["g2n"][at, :].astype(f32)
            for h in range(2):
                part = cut(both[h * p.rows2 : (h + 1) * p.rows2], p.rows2, p.rp2)
                own["rs"]["grad"][z, y, h] = part.reshape(2, p.rs, s.c).astype(b16)
            return carry

        if not p.even:
            lax.fori_loop(0, p.fs, open_up, 0)

    def middle():
        block.middle()
        stores.append(local(own["out"], out_hbm.at[0]))

    def last_out():
        block.last_out()
        stores.append(local(own["grad"], grad_hbm.at[0]))

    def put_vector():
        grads = own["gvec"][...].T
        if not p.even:
            grads = mm_g(own["map"][...], grads.astype(b16))
        own["ru"]["grad"][1] = grads.astype(b16).reshape(p.Z, p.Y, p.rp, LANE)

    prepare()
    k.wait_partners()
    gv.one()
    gb.one()
    gs.one()
    ge.one()
    ga.one()
    gm.one()
    ge.two()
    ga.two()
    gv.two()
    gv.three()
    gb.two()
    ga.three()
    gm.two()
    ge.three()
    gs.two()
    gb.three()
    ga.own()
    gb.own()
    gv.own()
    gv.four()
    gm.three()
    ga.four()
    gs.three()
    ge.own()
    gv.five()
    ge.four()
    gs.own()
    gm.own()
    gv.six()
    take_vector()
    ga.five()
    block.first()
    gb.four()
    ga.six()
    block.context((0, 1))
    block.level(0, (0, 1))
    block.level(1, (0, 1))
    gm.four()
    block.level(2, (0, 1))
    ge.four()
    gs.four()
    gb.five()
    gb.six()
    block.context((2,))
    block.level(0, (2,))
    block.query()
    gm.four()
    ge.five()
    gs.four()
    block.level(1, (2,))
    block.level(2, (2,))
    gm.five()
    block.pooling()
    gm.six()
    gs.five()
    ge.cross()
    modulate()
    ge.six()
    block.feed()
    gs.cross()
    shrink_grad()
    rs.one()
    gs.six()
    close_shrink()
    block.feed_back()
    block.expand_grad()
    rs.two()
    block.feed_out()
    re.one()
    middle()
    block.query_grad()
    block.middle_grads()
    rm.one()
    rq.one()
    block.focal_top()
    re.two()
    rm.two()
    rq.two()
    block.level_back(2, (0, 1))
    rs.across()
    block.level_back(1, (0, 1))
    block.level_back(0, (0, 1))
    rm.three()
    block.context_grad((0, 1))
    rt.one()
    block.level_back(2, (2,))
    rt.two()
    block.level_back(1, (2,))
    block.level_back(0, (2,))
    re.across()
    rm.four()
    block.context_grad((2,))
    rq.three()
    block.last_sums()
    rq.five()
    rs.three()
    put_vector()
    ru.one()
    last_out()
    ru.two()
    rt.three()
    re.three()
    settle("q")
    rm.five()
    rs.four()
    ru.three()
    re.four()
    settle("m")
    ru.five()
    rt.five()
    rs.five()
    re.five()
    settle("t")
    settle("u")
    settle("s")
    settle("e")
    k.finish()
    for store in stores:
        store.wait()


def adam_kernel(p, rates, tree, *refs):
    s = p.s
    owners = refs[0]
    fins = dict(zip(REDUCED, refs[1:7]))
    passed, olds = refs[7:9], refs[9:27]
    passed_out, news = refs[27:29], refs[29:47]
    own = jax.tree.unflatten(tree, refs[47:])
    sems = own["sem"]
    g = lax.axis_index("grp")
    used = []

    def local(source, target):
        copy = pltpu.make_async_copy(source, target, sems.at[len(used)])
        used.append(copy)
        copy.start()
        return copy

    wide = s.hid // 2
    groups = (
        (3, [("e", (h, i), 0, p.rows, h * wide + i * s.c, s.c) for h in range(2) for i in range(2)]),
        (
            4,
            [
                ("s", (h, i), h * p.rows2 + i * p.rs, min(p.rows2 - i * p.rs, p.rs), 0, s.c)
                for h in range(2)
                for i in range(2)
            ],
        ),
        (1, [("m", 0, 0, p.rows, 0, s.c)]),
        (2, [("m", 1, 0, p.rows, 0, s.c)]),
        (
            0,
            [
                ("q", 0, 0, p.rows, 0, 2 * LANE),
                ("q", 1, 0, p.rows, 2 * LANE, LANE),
                ("t", 0, 0, p.rows, s.c, LANE),
                ("t", 1, 0, p.rows, s.c + LANE, LANE),
                ("u", 0, 0, p.rows, s.c + 2 * LANE, LANE),
            ],
        ),
        (5, [("u", 1, 0, p.rows, 0, s.nvec)]),
    )
    waits = {}
    for index, pieces in groups:
        waits[index] = []
        for name in dict.fromkeys(piece[0] for piece in pieces):
            if name not in waits:
                waits[name] = local(fins[name], own["fin"][name])
        for i in range(3):
            waits[index].append(local(olds[3 * index + i], own["old"][3 * index + i]))
    passing = [local(a, b) for a, b in zip(passed, own["passed"])]
    stores, arrived = [], set()
    for index, pieces in groups:
        scale = jnp.where(owners[index] == g, 1.0, 0.0).astype(f32)
        for wait in waits[index]:
            wait.wait()
        for name, h, row, rows, col, cols in pieces:
            if name not in arrived:
                arrived.add(name)
                waits[name].wait()
            at = (0, slice(row, row + rows), slice(col, col + cols))
            gradient = own["fin"][name].at[h][:rows, :cols]
            weight, first, second = (own["old"][3 * index + i][at] for i in range(3))
            first_new = beta_one * first + (1.0 - beta_one) * gradient
            second_new = beta_two * second + (1.0 - beta_two) * gradient * gradient
            first_hat = first_new / (1.0 - beta_one**STEP)
            second_hat = second_new / (1.0 - beta_two**STEP)
            weight_new = weight - rates[index] * (
                first_hat / (jnp.sqrt(second_hat) + adam_eps) + weight_decay * weight
            )
            for i, value in enumerate((weight_new, first_new, second_new)):
                own["new"][3 * index + i][at] = value * scale
        for i in range(3):
            stores.append(local(own["new"][3 * index + i], news[3 * index + i]))
    for wait, a, b in zip(passing, own["passed"], passed_out):
        wait.wait()
        stores.append(local(a, b))
    for store in stores:
        store.wait()


def solution(mesh):
    n_grp, n_fs = mesh.shape["grp"], mesh.shape["fs"]

    def shards(image_patches, cotangent, image_count, resolution, owner_list, *tensors):
        side, channels = image_patches.shape[1], image_patches.shape[3]
        hid = tensors[9].shape[2]
        s = Shape(side, channels, hid)
        p = Plan(n_grp, n_fs, s)
        grid = (side, side, channels)
        scratch = dict(
            compute=compute_scratch(s),
            land=dict(
                x=pltpu.VMEM(grid, b16),
                cot=pltpu.VMEM(grid, b16),
                focal=pltpu.VMEM((p.rows, 2 * channels), f32),
                modulate=pltpu.VMEM((p.rows, channels), f32),
                project=pltpu.VMEM((p.rows, channels), f32),
                expand=pltpu.VMEM((p.rows, hid), f32),
                shrink=pltpu.VMEM((2 * p.rows2, channels), f32),
                vector=pltpu.VMEM((p.rows, s.nvec), f32),
            ),
            out=pltpu.VMEM(grid, b16),
            grad=pltpu.VMEM(grid, f32),
            v=pltpu.VMEM((LANE, s.c), f32),
            gvec=pltpu.VMEM((LANE, s.c), f32),
            local_sem=pltpu.SemaphoreType.DMA((24,)),
            send_sem=pltpu.SemaphoreType.DMA((sem_count(p),)),
            recv_sem=pltpu.SemaphoreType.DMA((sem_count(p),)),
            column_sem=pltpu.SemaphoreType.REGULAR,
        )
        for name in GATHERED:
            scratch["g" + name] = gather_scratch(p, name)
        for name in REDUCED:
            scratch["r" + name] = reduce_scratch(p, name)
        if not p.even:
            scratch["map"] = pltpu.VMEM((s.c, p.fs * p.rp), b16)
            scratch["w2n"] = pltpu.VMEM((s.hid, s.c), b16)
            scratch["g2n"] = pltpu.VMEM((s.hid, s.c), b16)

        def flatten(scratch):
            return jax.tree.flatten(scratch, is_leaf=lambda v: not isinstance(v, (dict, list)))

        leaves, tree = flatten(scratch)
        anywhere = pl.BlockSpec(memory_space=pl.ANY)
        smem = pl.BlockSpec(memory_space=pltpu.SMEM)
        shape = jax.ShapeDtypeStruct
        fins = [shape(fin_shape(p, name), f32) for name in REDUCED]
        images = [shape(image_patches.shape, b16), shape(image_patches.shape, f32)]
        tensors = tensors[:15] + tuple(t.transpose(0, 2, 1) for t in tensors[15:])
        results = pl.pallas_call(
            lambda *refs: block_kernel(p, tree, *refs),
            out_shape=images + fins,
            in_specs=[smem] * 3 + [anywhere] * 8,
            out_specs=[anywhere] * 8,
            scratch_shapes=leaves,
            compiler_params=pltpu.CompilerParams(
                collective_id=0, has_side_effects=True, vmem_limit_bytes=VMEM_BYTES
            ),
            name="block",
        )(
            image_count,
            resolution,
            owner_list,
            image_patches,
            cotangent,
            *tensors[0:16:3],
        )
        wide_rate = 1.5 / math.sqrt(channels)
        rates = (wide_rate,) * 4 + (1.5 / math.sqrt(hid), 0.2)
        adam_leaves, adam_tree = flatten(
            dict(
                fin={name: pltpu.VMEM(fin_shape(p, name), f32) for name in REDUCED},
                old=[pltpu.VMEM(t.shape, f32) for t in tensors],
                new=[pltpu.VMEM(t.shape, f32) for t in tensors],
                passed=[pltpu.VMEM(t.shape, t.dtype) for t in images],
                sem=pltpu.SemaphoreType.DMA((56,)),
            )
        )
        news = pl.pallas_call(
            lambda *refs: adam_kernel(p, rates, adam_tree, *refs),
            out_shape=images + [shape(t.shape, f32) for t in tensors],
            in_specs=[smem] + [anywhere] * 26,
            out_specs=[anywhere] * 20,
            scratch_shapes=adam_leaves,
            compiler_params=pltpu.CompilerParams(vmem_limit_bytes=VMEM_BYTES),
            name="adam",
        )(owner_list, *results[2:], *results[:2], *tensors)
        return tuple(news[:17]) + tuple(t.transpose(0, 2, 1) for t in news[17:])

    images = P(("grp", "fs"), None, None, None)
    weights = (P("grp", "fs", None),) * 15 + (P("grp", None, "fs"),) * 3
    return jax.shard_map(
        shards,
        mesh=mesh,
        in_specs=(images, images, P("grp", "fs"), P(("grp", "fs")), P()) + weights,
        out_specs=(images, images) + weights,
        check_vma=False,
    )
```

```python
import math

import jax
import jax.numpy as jnp
from jax import lax
from jax.experimental import pallas as pl
from jax.experimental.pallas import tpu as pltpu
from jax.sharding import PartitionSpec as P

f32 = jnp.float32
b16 = jnp.bfloat16
LEVELS = 3
GATES = 4
LANE = 128
norm_eps = 1e-05
PAD = 3
EDGE = 8
SQRT_HALF = math.sqrt(0.5)
INV_SQRT_2PI = 1.0 / math.sqrt(2.0 * math.pi)
HALF_LOG2E = -0.5 / math.log(2.0)
BLK = 576


def gelu_parts(z):
    phi = 0.5 + 0.5 * lax.erf(z * SQRT_HALF)
    return z * phi, phi + (z * INV_SQRT_2PI) * jnp.exp2(z * z * HALF_LOG2E)


def mm(a, b):
    return jnp.dot(a, b, preferred_element_type=f32)


def mm_t(a, b):
    return lax.dot_general(a, b, (((1,), (1,)), ((), ())), preferred_element_type=f32)


def mm_g(a, b):
    return lax.dot_general(a, b, (((0,), (0,)), ((), ())), preferred_element_type=f32)


def tall(values):
    rows, cols = values.shape
    return jnp.sum(values.reshape(rows // 8, 8, cols), axis=0)


def lane_sum(values):
    parts = values[:, :LANE]
    for start in range(LANE, values.shape[1], LANE):
        parts = parts + values[:, start : start + LANE]
    return jnp.sum(parts, axis=1, keepdims=True)


class Shape:
    def __init__(self, side, channels, hid):
        self.side = side
        self.rows = side * side
        self.c = channels
        self.nc = channels // LANE
        self.hid = hid
        self.bias_rows = hid // channels
        self.gate_at = 11 + self.bias_rows
        self.kernel_at = self.gate_at + GATES
        self.taps = [(2 * n + 3) ** 2 for n in range(LEVELS)]
        self.nvec = self.kernel_at + sum(self.taps)
        self.high = side + 2 * PAD + 1
        self.padded = (self.nc, self.high, side + 2 * EDGE, LANE)


def compute_scratch(s):
    flat = (s.rows, s.c)
    split = (s.nc, s.rows, LANE)
    grid = (s.nc, s.side, s.side, LANE)
    return dict(
        vc=pltpu.VMEM((s.nc, s.nvec, LANE), f32),
        mask=pltpu.VMEM((s.rows, LANE), f32),
        xh1=pltpu.VMEM(flat, f32),
        r1=pltpu.VMEM((s.rows, LANE), f32),
        n1b=pltpu.VMEM(flat, b16),
        gate=pltpu.VMEM((GATES, s.rows, LANE), f32),
        q=pltpu.VMEM(flat, f32),
        pads=[pltpu.VMEM(s.padded, f32) for _ in range(LEVELS + 1)],
        gd=[pltpu.VMEM(grid, f32) for _ in range(LEVELS)],
        sums=pltpu.VMEM((s.side,) + s.padded[2:], f32),
        summed=pltpu.VMEM(grid, f32),
        sumb=pltpu.VMEM(flat, b16),
        mod=pltpu.VMEM(flat, f32),
        mixb=pltpu.VMEM(flat, b16),
        proj=pltpu.VMEM(flat, f32),
        mid=pltpu.VMEM(flat, f32),
        xh2=pltpu.VMEM(flat, f32),
        r2=pltpu.VMEM((s.rows, LANE), f32),
        n2b=pltpu.VMEM(flat, b16),
        dshrb=pltpu.VMEM(flat, b16),
        actb=pltpu.VMEM((s.rows, s.hid), b16),
        dhidb=pltpu.VMEM((s.rows, s.hid), b16),
        shr=pltpu.VMEM(flat, f32),
        dn=pltpu.VMEM(flat, f32),
        dqb=pltpu.VMEM(flat, b16),
        dsum=pltpu.VMEM(split, f32),
        dgate=pltpu.VMEM((GATES, s.rows, LANE), f32),
        dctxb=pltpu.VMEM(flat, b16),
        gacc=pltpu.VMEM((s.nc, sum(s.taps), 8, LANE), f32),
        pool=pltpu.VMEM((2, 8, s.c), f32),
    )


class Compute:
    def __init__(self, s, refs, scratch):
        self.s = s
        self.__dict__.update(refs)
        self.__dict__.update(scratch)
        self.dmid, self.dprojb, self.dmodb = self.mid, self.dshrb, self.n2b

    def row(self, index):
        return self.v[index : index + 1, :]

    def wide_mask(self, at):
        m = self.mask[at, :]
        return jnp.concatenate([m] * self.s.nc, axis=1)

    def wide(self, ref, at):
        m = ref[at, :]
        return jnp.concatenate([m] * self.s.nc, axis=1)

    def blocks(self, body, sums=0):
        s = self.s
        start = tuple(jnp.zeros((8, s.c), f32) for _ in range(sums))

        def step(index, carry):
            at = pl.ds(pl.multiple_of(index * BLK, BLK), BLK)
            parts = body(at, pl.ds(index * (BLK // s.side), BLK // s.side))
            if not sums:
                return carry
            return tuple(total + tall(part) for total, part in zip(carry, parts))

        return lax.fori_loop(0, s.rows // BLK, step, start)

    def image(self, ref, lines):
        return ref[lines].astype(f32).reshape(BLK, self.s.c)

    def store(self, ref, lines, values):
        ref[lines] = values.reshape(BLK // self.s.side, self.s.side, self.s.c).astype(ref.dtype)

    def put(self, index, total):
        self.gv[index : index + 1, :] = jnp.sum(total, axis=0, keepdims=True)

    def prepare(self):
        s = self.s
        shape = (s.side, s.side, LANE)
        side = jnp.where(self.count > 0, self.sides, 0)
        inside = (lax.broadcasted_iota(jnp.int32, shape, 0) < side) & (
            lax.broadcasted_iota(jnp.int32, shape, 1) < side
        )
        self.mask[...] = jnp.where(inside, 1.0, 0.0).astype(f32).reshape(s.rows, LANE)

        def zero_plane(index, carry):
            for pad in self.pads:
                for ch in range(s.nc):
                    pad[ch, index, 0:EDGE, :] = jnp.zeros((EDGE, LANE), f32)
                    pad[ch, index, EDGE + s.side :, :] = jnp.zeros((EDGE, LANE), f32)
            return carry

        lax.fori_loop(0, s.high, zero_plane, 0)
        for pad in self.pads:
            for ch in range(s.nc):
                for edge in list(range(PAD)) + list(range(PAD + s.side, s.high)):
                    pad[ch, edge, EDGE : EDGE + s.side, :] = jnp.zeros((s.side, LANE), f32)

    def first_norm(self):
        s = self.s

        def norm(at, lines):
            x = self.image(self.x, lines)
            centred = x - lane_sum(x) * (1.0 / s.c)
            r = lax.rsqrt(lane_sum(centred * centred) * (1.0 / s.c) + norm_eps)
            self.xh1[at, :] = centred * r
            self.r1[at, :] = jnp.broadcast_to(r, (BLK, LANE))

        self.blocks(norm)

    def first(self):
        s = self.s
        for ch in range(s.nc):
            self.vc[ch] = self.v[: s.nvec, ch * LANE : (ch + 1) * LANE]
        gain, shift = self.row(0), self.row(1)
        weights = [self.row(s.gate_at + l) for l in range(GATES)]

        def step(at, lines):
            n1 = self.xh1[at, :] * gain + shift
            self.n1b[at, :] = n1.astype(b16)
            for l in range(GATES):
                self.gate[l, at, :] = jnp.broadcast_to(lane_sum(n1 * weights[l]), (BLK, LANE))

        self.blocks(step)

    def context(self, chunks):
        s = self.s
        lanes = slice(chunks[0] * LANE, (chunks[-1] + 1) * LANE)
        ctx = mm(self.n1b[...], self.wc(chunks)) + self.v[3:4, lanes]
        m = self.mask[...]
        for i, ch in enumerate(chunks):
            part = ctx[:, i * LANE : (i + 1) * LANE] * m
            self.pads[0][ch, PAD : PAD + s.side, EDGE : EDGE + s.side, :] = part.reshape(
                s.side, s.side, LANE
            )

    def query(self):
        self.q[...] = mm(self.n1b[...], self.wq()) + self.row(2)

    def plane_sum(self, plane, count, at):
        def row(n):
            ref, base, stride = plane
            return ref[base + stride * n]

        for n in range(count):
            self.sums[at + n] = row(2 * n + 1) + row(2 * n + 2)
        return (self.sums, at, 1)

    def direct_rows(self, plane, taps, rows, weights=None):
        s = self.s
        ref, base, stride = plane
        out, grads = [None] * rows, {}
        for dc, column in taps.items():
            k = len(column)
            sums = [None] * k
            for a in range(rows + k - 1):
                x = ref[base + stride * a, pl.ds(EDGE + dc, s.side), :]
                for o in range(max(0, a - k + 1), min(rows, a + 1)):
                    t = a - o
                    term = x * column[t]
                    out[o] = term if out[o] is None else out[o] + term
                    if weights is not None:
                        part = tall(x * weights[o])
                        sums[t] = part if sums[t] is None else sums[t] + part
            grads[dc] = sums
        return out, grads

    def fast_rows(self, plane, taps, rows, depth, weights=None, at=0):
        length = len(next(iter(taps.values())))
        if depth == 0 or length == 1:
            return self.direct_rows(plane, taps, rows, weights)
        if rows % 2:
            ref, base, stride = plane
            last = (ref, base + stride * (rows - 1), stride)
            head = None if weights is None else weights[:-1]
            out, grads = self.fast_rows(plane, taps, rows - 1, depth, head, at)
            more, more_grads = self.direct_rows(last, taps, 1, None if weights is None else weights[-1:])
            if weights is not None:
                for dc in taps:
                    grads[dc] = [x + y for x, y in zip(grads[dc], more_grads[dc])]
            return out + more, grads
        n = rows // 2
        ref, base, stride = plane
        even, odd = (ref, base, 2 * stride), (ref, base + stride, 2 * stride)
        e_taps = {dc: column[0::2] for dc, column in taps.items()}
        o_taps = {dc: column[1::2] for dc, column in taps.items()}
        s_taps = {
            dc: [x + o_taps[dc][i] if i < len(o_taps[dc]) else x for i, x in enumerate(column)]
            for dc, column in e_taps.items()
        }
        count = n + (length + 1) // 2 - 1
        summed = self.plane_sum(plane, count, at)
        at = at + count
        wa = wb = ws = None
        if weights is not None:
            we, wo = weights[0::2], weights[1::2]
            wa = [we[0]] + [we[i] - wo[i - 1] for i in range(1, n)] + [0.0 - wo[n - 1]]
            wb = [we[i] - wo[i] for i in range(n)]
            ws = wo
        a_out, a_grad = self.fast_rows(even, e_taps, n + 1, depth - 1, wa, at)
        b_out, b_grad = self.fast_rows(odd, o_taps, n, depth - 1, wb, at)
        s_out, s_grad = self.fast_rows(summed, s_taps, n, depth - 1, ws, at)
        out, grads = [], {}
        for i in range(n):
            out += [a_out[i] + b_out[i], s_out[i] - a_out[i + 1] - b_out[i]]
        if weights is not None:
            for dc in taps:
                column = []
                for i in range(length):
                    both = (a_grad if i % 2 == 0 else b_grad)[dc][i // 2]
                    column.append(both + s_grad[dc][i // 2])
                grads[dc] = column
        return out, grads

    def level(self, l, chunks, depth=1):
        s = self.s
        k = 2 * l + 3
        p = l + 1
        offset = s.kernel_at + sum(s.taps[:l])

        def step(ch, carry):
            taps = {
                dc: [
                    self.vc[ch, pl.ds(offset + t * k + dc + p, 1), :]
                    for t in range(k)
                ]
                for dc in range(-p, p + 1)
            }
            plane = (self.pads[l].at[ch], PAD - p, 1)
            out, _ = self.fast_rows(plane, taps, s.side, depth)
            for r in range(s.side):
                at = slice(r * s.side, (r + 1) * s.side)
                m = self.mask[at, :]
                value, slope = gelu_parts(out[r])
                value = value * m
                self.gd[l][ch, r] = slope * m
                self.pads[l + 1][ch, r + PAD, EDGE : EDGE + s.side, :] = value
                term = value * self.gate[l, at, :]
                if l:
                    term = term + self.summed[ch, r]
                self.summed[ch, r] = term
            return carry

        lax.fori_loop(chunks[0], chunks[-1] + 1, step, 0)

    def pooling(self):
        s = self.s
        area = (self.sides * self.sides).astype(f32)
        for ch in range(s.nc):
            last = self.pads[LEVELS][ch, PAD : PAD + s.side, EDGE : EDGE + s.side, :]
            total = jnp.sum(tall(last.reshape(s.rows, LANE)), axis=0, keepdims=True)
            value, slope = gelu_parts(total / area)
            cols = slice(ch * LANE, (ch + 1) * LANE)
            self.pool[0, :, cols] = jnp.broadcast_to(value, (8, LANE))
            self.pool[1, :, cols] = jnp.broadcast_to(slope / area, (8, LANE))

        def step(index, carry):
            at = pl.ds(pl.multiple_of(index * BLK, BLK), BLK)
            gate = self.gate[LEVELS, at, :]
            for ch in range(s.nc):
                cols = slice(ch * LANE, (ch + 1) * LANE)
                part = self.summed[ch, pl.ds(index * (BLK // s.side), BLK // s.side)].reshape(BLK, LANE)
                self.sumb[at, cols] = (part + gate * self.pool[0, 0:1, cols]).astype(b16)
            return carry

        lax.fori_loop(0, s.rows // BLK, step, 0)

    def modulate(self):
        s = self.s
        self.mod[...] = mm(self.sumb[...], self.wh()) + self.row(4)

        def mix(at, lines):
            self.mixb[at, :] = (self.q[at, :] * self.mod[at, :]).astype(b16)

        self.blocks(mix)
        self.proj[...] = mm(self.mixb[...], self.wp()) + self.row(5)
        scale, gain, shift = self.row(6), self.row(7), self.row(8)
        upscale = self.row(10)

        def norm(at, lines):
            mid = self.image(self.x, lines) + scale * self.proj[at, :]
            self.mid[at, :] = mid
            centred = mid - lane_sum(mid) * (1.0 / s.c)
            r = lax.rsqrt(lane_sum(centred * centred) * (1.0 / s.c) + norm_eps)
            xh = centred * r
            self.xh2[at, :] = xh
            self.r2[at, :] = jnp.broadcast_to(r, (BLK, LANE))
            self.n2b[at, :] = (xh * gain + shift).astype(b16)
            d_shr = self.image(self.cot, lines) * self.wide_mask(at) * upscale
            self.dshrb[at, :] = d_shr.astype(b16)
            return (d_shr,)

        (g_b2,) = self.blocks(norm, 1)
        self.put(9, g_b2)

    def slope_tile(self, tile):
        s = self.s
        index, part = divmod(tile, s.nc)
        lanes = slice(part * LANE, (part + 1) * LANE)
        if index == 0:
            return self.dsum.at[part], (s.rows, LANE)
        if index == 1:
            return self.grad.at[:, :, lanes], (s.side, s.side, LANE)
        return (self.dn if index == 2 else self.shr).at[:, lanes], (s.rows, LANE)

    def feed(self, wide=256):
        s = self.s
        half = s.hid // 2
        for j in range(s.hid // wide):
            cols = slice(j * wide, (j + 1) * wide)
            h, at = divmod(j * wide, half)
            bias = []
            for start in range(j * wide, (j + 1) * wide, LANE):
                r, c = divmod(start, s.c)
                bias.append(self.v[11 + r : 12 + r, c : c + LANE])
            hid = mm(self.n2b[...], self.w1(h, at, wide)) + jnp.concatenate(bias, axis=1)
            act, slope = gelu_parts(hid)
            self.actb[:, cols] = act.astype(b16)
            for i in range(wide // LANE):
                ref, shape = self.slope_tile(j * wide // LANE + i)
                ref[...] = slope[:, i * LANE : (i + 1) * LANE].reshape(shape)

    def feed_back(self, wide=256):
        s = self.s
        for j in range(s.hid // wide):
            d_act = mm_t(self.dshrb[...], self.w2(j * wide, wide))
            for i in range(wide // LANE):
                ref, _ = self.slope_tile(j * wide // LANE + i)
                d_hid = d_act[:, i * LANE : (i + 1) * LANE] * ref[...].reshape(s.rows, LANE)
                start = j * wide + i * LANE
                self.dhidb[:, start : start + LANE] = d_hid.astype(b16)
                r, c = divmod(start, s.c)
                self.gv[11 + r : 12 + r, c : c + LANE] = jnp.sum(tall(d_hid), axis=0, keepdims=True)

    def shrink_grad(self):
        s = self.s
        for at in range(0, s.hid, s.c):
            self.put_g2(at, s.c, mm_g(self.actb[:, at : at + s.c], self.dshrb[...]))

    def expand_grad(self):
        s = self.s
        half = s.hid // 2
        for at in range(0, s.hid, s.c):
            self.put_g1(at // half, at % half, mm_g(self.n2b[...], self.dhidb[:, at : at + s.c]))

    def feed_out(self):
        s = self.s
        half = s.hid // 2
        self.shr[...] = mm(self.actb[...], self.w2(0, s.hid)) + self.row(9)
        self.dn[...] = mm_t(self.dhidb[:, :half], self.w1(0, 0, half)) + mm_t(
            self.dhidb[:, half:], self.w1(1, 0, half)
        )

    def middle(self):
        s = self.s
        gain, scale, upscale = self.row(7), self.row(6), self.row(10)

        def step(at, lines):
            shr, mid, proj, xh = self.shr[at, :], self.mid[at, :], self.proj[at, :], self.xh2[at, :]
            m = self.wide_mask(at)
            u = self.image(self.cot, lines) * m
            self.store(self.out, lines, (mid + upscale * shr) * m)
            d = self.dn[at, :]
            e = d * gain
            mean_e = lane_sum(e) * (1.0 / s.c)
            mean_x = lane_sum(e * xh) * (1.0 / s.c)
            d_mid = u + self.wide(self.r2, at) * (e - mean_e - xh * mean_x)
            self.dmid[at, :] = d_mid
            d_proj = scale * d_mid
            self.dprojb[at, :] = d_proj.astype(b16)
            return u * shr, d * xh, d, d_mid * proj, d_proj

        sums = self.blocks(step, 5)
        for index, total in zip((10, 7, 8, 6, 5), sums):
            self.put(index, total)
        self.dn[...] = mm_t(self.dprojb[...], self.wp())

        def split(at, lines):
            d = self.dn[at, :]
            d_q = d * self.mod[at, :]
            d_mod = d * self.q[at, :]
            self.dqb[at, :] = d_q.astype(b16)
            self.dmodb[at, :] = d_mod.astype(b16)
            return d_q, d_mod

        g_bq, g_bh = self.blocks(split, 2)
        self.put(2, g_bq)
        self.put(4, g_bh)
        d_sum = mm_t(self.dmodb[...], self.wh())
        for ch in range(s.nc):
            self.dsum[ch] = d_sum[:, ch * LANE : (ch + 1) * LANE]

    def middle_grads(self):
        self.put_gp(mm_g(self.mixb[...], self.dprojb[...]))
        self.put_gh(mm_g(self.sumb[...], self.dmodb[...]))

    def query_grad(self):
        self.put_gq(mm_g(self.n1b[...], self.dqb[...]))

    def focal_top(self):
        s = self.s

        def step(index, carry):
            at = pl.ds(pl.multiple_of(index * BLK, BLK), BLK)
            gate = self.gate[LEVELS, at, :]
            sums = [jnp.zeros((BLK, LANE), f32) for _ in range(GATES)]
            out = []
            for ch in range(s.nc):
                cols = slice(ch * LANE, (ch + 1) * LANE)
                d = self.dsum[ch, at, :]
                values = [
                    self.pads[l][ch, pl.ds(index * (BLK // s.side) + PAD, BLK // s.side), EDGE : EDGE + s.side, :]
                    for l in range(1, LEVELS + 1)
                ]
                for l in range(LEVELS):
                    sums[l] = sums[l] + d * values[l].reshape(BLK, LANE)
                sums[LEVELS] = sums[LEVELS] + d * self.pool[0, 0:1, cols]
                out.append(carry[ch] + tall(d * gate))
            for l in range(GATES):
                self.dgate[l, at, :] = jnp.broadcast_to(
                    jnp.sum(sums[l], axis=1, keepdims=True), (BLK, LANE)
                )
            return tuple(out)

        zero = jnp.zeros((8, LANE), f32)
        totals = lax.fori_loop(0, s.rows // BLK, step, (zero,) * s.nc)
        for ch in range(s.nc):
            cols = slice(ch * LANE, (ch + 1) * LANE)
            total = jnp.sum(totals[ch], axis=0, keepdims=True)
            self.pool[1, :, cols] = self.pool[1, :, cols] * total

        def last(index, carry):
            at = pl.ds(pl.multiple_of(index * BLK, BLK), BLK)
            gate = self.gate[LEVELS - 1, at, :]
            for ch in range(s.nc):
                cols = slice(ch * LANE, (ch + 1) * LANE)
                e = self.dsum[ch, at, :] * gate + self.pool[1, 0:1, cols]
                d = e.reshape(BLK // s.side, s.side, LANE) * self.gd[LEVELS - 1][ch, pl.ds(index * (BLK // s.side), BLK // s.side)]
                self.pads[LEVELS][ch, pl.ds(index * (BLK // s.side) + PAD, BLK // s.side), EDGE : EDGE + s.side, :] = d
            return carry

        lax.fori_loop(0, s.rows // BLK, last, 0)

    def level_back(self, l, chunks, depth=2):
        s = self.s
        k = 2 * l + 3
        p = l + 1
        base = sum(s.taps[:l])
        offset = s.kernel_at + base

        def step(ch, carry):
            taps = {
                dc: [
                    self.vc[ch, pl.ds(offset + (k - 1 - t) * k + p - dc, 1), :]
                    for t in range(k)
                ]
                for dc in range(-p, p + 1)
            }
            plane = (self.pads[l + 1].at[ch], PAD - p, 1)
            inputs = [self.pads[l][ch, r + PAD, EDGE : EDGE + s.side, :] for r in range(s.side)]
            out, grads = self.fast_rows(plane, taps, s.side, depth, inputs)
            for dc, column in grads.items():
                for t, value in enumerate(column):
                    self.gacc[ch, base + (k - 1 - t) * k + p - dc] = value
            for r in range(s.side):
                at = slice(r * s.side, (r + 1) * s.side)
                if l:
                    e = out[r] + self.dsum[ch, at, :] * self.gate[l - 1, at, :]
                    self.pads[l][ch, r + PAD, EDGE : EDGE + s.side, :] = e * self.gd[l - 1][ch, r]
                else:
                    self.summed[ch, r] = out[r] * self.mask[at, :]
            return carry

        lax.fori_loop(chunks[0], chunks[-1] + 1, step, 0)

    def context_grad(self, chunks):
        s = self.s

        def step(index, carry):
            at = pl.ds(pl.multiple_of(index * BLK, BLK), BLK)
            out = []
            for i, ch in enumerate(chunks):
                cols = slice(ch * LANE, (ch + 1) * LANE)
                lines = pl.ds(index * (BLK // s.side), BLK // s.side)
                d = self.summed[ch, lines].reshape(BLK, LANE)
                self.dctxb[at, cols] = d.astype(b16)
                out.append(carry[i] + tall(d))
            return tuple(out)

        zero = jnp.zeros((8, LANE), f32)
        totals = lax.fori_loop(0, s.rows // BLK, step, (zero,) * len(chunks))
        for i, ch in enumerate(chunks):
            cols = slice(ch * LANE, (ch + 1) * LANE)
            self.gv[3:4, cols] = jnp.sum(totals[i], axis=0, keepdims=True)
            self.gv[s.kernel_at : s.nvec, cols] = jnp.sum(self.gacc[ch], axis=1)
        lanes = slice(chunks[0] * LANE, (chunks[-1] + 1) * LANE)
        self.put_gc(chunks, mm_g(self.n1b[...], self.dctxb[:, lanes]))

    def last_sums(self):
        s = self.s
        wc = self.wc(tuple(range(s.nc)))
        self.dn[...] = mm_t(self.dqb[...], self.wq()) + mm_t(self.dctxb[...], wc)
        gain, shift = self.row(0), self.row(1)
        weights = [self.row(s.gate_at + l) for l in range(GATES)]

        def step(at, lines):
            xh = self.xh1[at, :]
            n1 = xh * gain + shift
            d = self.dn[at, :]
            sums = []
            for l in range(GATES):
                dg = self.wide(self.dgate.at[l], at)
                d = d + dg * weights[l]
                sums.append(dg * n1)
            self.dn[at, :] = d
            return (d * xh, d) + tuple(sums)

        sums = self.blocks(step, 2 + GATES)
        for index, total in zip((0, 1) + tuple(s.gate_at + l for l in range(GATES)), sums):
            self.put(index, total)

    def last_out(self):
        s = self.s
        gain = self.row(0)

        def step(at, lines):
            xh = self.xh1[at, :]
            e = self.dn[at, :] * gain
            mean_e = lane_sum(e) * (1.0 / s.c)
            mean_x = lane_sum(e * xh) * (1.0 / s.c)
            d_in = self.dmid[at, :] + self.wide(self.r1, at) * (e - mean_e - xh * mean_x)
            self.store(self.grad, lines, d_in)

        self.blocks(step)


MESH = pl.DeviceIdType.MESH
STEP = 10
beta_one = 0.9
beta_two = 0.95
adam_eps = 1e-08
weight_decay = 0.05
VMEM_BYTES = 63 * 2**20 + 2**19
GATHERED = "vabmes"
REDUCED = "semqtu"
PAIRS = "se"
DIRECT = "qtu"
NEAR = "va"
HALVED = "es"
AT_ONCE = "vab"


class Plan:
    def __init__(self, n_grp, n_fs, s):
        self.X = n_grp // 2
        self.Y = 2 ** (int(math.log2(n_fs)) // 2)
        self.Z = n_fs // self.Y
        self.fs = n_fs
        self.s = s
        self.rows = s.c // n_fs
        self.rp = -(-self.rows // 16) * 16
        self.rows2 = s.hid // n_fs // 2
        self.rp2 = -(-self.rows2 // 16) * 16
        self.even = self.rp == self.rows and self.rp2 == self.rows2
        self.rv = self.rp // 2
        self.gather_cols = dict(v=LANE, a=LANE, b=2 * LANE, m=s.c)
        self.rs = self.rp2 // 2
        self.reduce_cols = dict(s=s.c, e=s.hid // 4, m=s.c, q=2 * LANE, t=LANE, u=LANE)

    def piece(self, name):
        if name == "e":
            return (2, self.rp, self.s.c)
        if name == "s":
            return (2, self.rs, self.s.c)
        return (self.rv if name == "v" else self.rp, self.gather_cols[name])

    def whole(self, name):
        piece = self.piece(name)
        if name == "e":
            return (2, 2, self.Z, self.Y) + piece[1:]
        if name in "sv":
            return (self.Z, self.Y, 2) + piece
        return (2, self.Z, self.Y) + piece


def gather_scratch(p, name):
    piece = p.piece(name)
    kind = f32 if name == "v" else b16
    passed = piece[1:] if name in HALVED and p.X == 2 else piece
    return dict(
        cand=pltpu.VMEM((2,) + piece, kind),
        rx1=pltpu.VMEM(piece, kind),
        sel=pltpu.VMEM(piece, kind),
        rx2=pltpu.VMEM((p.X - 1, 2 if name in NEAR else 1) + passed, kind),
        full=pltpu.VMEM(p.whole(name), kind),
    )


def reduce_piece(p, name):
    return (p.rs if name == "s" else p.rp, p.reduce_cols[name])


def fin_shape(p, name):
    return (2, 2) + reduce_piece(p, name) if name in PAIRS else (2,) + reduce_piece(p, name)


def grad_shape(p, name):
    if name == "s":
        return (p.Z, p.Y, 2, 2) + reduce_piece(p, name)
    return ((2, 2) if name in PAIRS else (2,)) + (p.Z, p.Y) + reduce_piece(p, name)


def steps_scratch(p, name):
    piece = reduce_piece(p, name)
    out = dict(
        r1=pltpu.VMEM((p.Z, p.Y) + piece, b16),
        a3=pltpu.VMEM(piece, b16),
        a4=pltpu.VMEM(piece, f32),
        r4=pltpu.VMEM((p.X - 1, 2) + piece, b16),
        r5=pltpu.VMEM(piece, b16),
    )
    if name in DIRECT:
        out["r3"] = pltpu.VMEM((p.fs - 1,) + piece, b16)
    else:
        out["r2"] = pltpu.VMEM((p.Y - 1, p.Z) + piece, b16)
        out["a2"] = pltpu.VMEM((p.Z,) + piece, b16)
        out["r3"] = pltpu.VMEM((p.Z - 1,) + piece, b16)
    return out


def reduce_scratch(p, name):
    out = dict(grad=pltpu.VMEM(grad_shape(p, name), b16), fin=pltpu.VMEM(fin_shape(p, name), f32))
    if name not in PAIRS:
        out["steps"] = steps_scratch(p, name)
    elif p.X == 2:
        out["steps"] = steps_scratch(p, name)
        out["other"] = pltpu.VMEM((p.Z, p.Y) + reduce_piece(p, name), b16)
        out["rx"] = pltpu.VMEM((p.Z, p.Y) + reduce_piece(p, name), b16)
    else:
        out["parts"] = [steps_scratch(p, name) for _ in range(2)]
    return out


def sem_count(p):
    gather = 1 + 2 * (p.X - 1) + (p.Z - 1) + p.Z * (p.Y - 1) + 3 * p.fs
    reduce = 1 + max((p.Y - 1) + (p.Z - 1), p.fs - 1) + 2 * (p.X - 1) + 1
    return gather * len(GATHERED) + reduce * (len(REDUCED) + len(PAIRS))


class Links:
    def __init__(self, p, send_sem, recv_sem, column_sem):
        self.p, self.column_sem = p, column_sem
        self.send_sem, self.recv_sem = send_sem, recv_sem
        self.used = 0
        self.sent = []
        self.g, self.f = lax.axis_index("grp"), lax.axis_index("fs")
        self.x, self.c = lax.div(self.g, 2), lax.rem(self.g, 2)
        self.z, self.y = lax.div(self.f, p.Y), lax.rem(self.f, p.Y)

    def sibling(self):
        return (self.x * 2 + 1 - self.c, self.f)

    def at_x(self, x, other_core=0):
        core = 1 - self.c if other_core else self.c
        return (x * 2 + core, self.f)

    def at_z(self, z):
        return (self.g, z * self.p.Y + self.y)

    def at_y(self, y):
        return (self.g, self.z * self.p.Y + y)

    def flip_z(self, bit):
        return self.z + bit - 2 * bit * lax.rem(lax.div(self.z, bit), 2)

    def signal_partners(self):
        p = self.p
        partners = (
            [self.sibling()]
            + [self.at_x(lax.rem(self.x + d, p.X), i) for d in range(1, p.X) for i in range(2)]
            + [self.at_z(lax.rem(self.z + d, p.Z)) for d in range(1, p.Z)]
            + [self.at_y(lax.rem(self.y + d, p.Y)) for d in range(1, p.Y)]
        )
        self.partners = len(partners)
        barrier = pltpu.get_barrier_semaphore()
        for partner in partners:
            pl.semaphore_signal(barrier, inc=1, device_id=partner, device_id_type=MESH)

    def wait_partners(self):
        pl.semaphore_wait(pltpu.get_barrier_semaphore(), self.partners)
        self.heard = False
        for d in range(1, self.p.Y):
            partner = self.at_y(lax.rem(self.y + d, self.p.Y))
            pl.semaphore_signal(self.column_sem, inc=1, device_id=partner, device_id_type=MESH)

    def hear_columns(self):
        if not self.heard:
            pl.semaphore_wait(self.column_sem, self.p.Y - 1)
            self.heard = True

    def send(self, source, target, partner, arriving=None):
        index = self.used
        self.used += 1

        def copy(src, dst):
            return pltpu.make_async_remote_copy(
                src_ref=src,
                dst_ref=dst,
                send_sem=self.send_sem.at[index],
                recv_sem=self.recv_sem.at[index],
                device_id=partner,
                device_id_type=MESH,
            )

        started = copy(source, target)
        started.start()
        self.sent.append(started)
        coming = copy(source, target if arriving is None else arriving)
        return coming.wait_recv

    def finish(self):
        for copy in self.sent:
            copy.wait_send()


class Gather:
    def __init__(self, name, links, refs):
        self.name, self.links, self.p = name, links, links.p
        self.near, self.direct = name in NEAR, name in AT_ONCE
        self.split = name in HALVED and links.p.X == 2
        self.waitx = []
        self.__dict__.update(refs)
        self.held, self.wait3, self.wait4, self.wait5 = [], [], [], []

    def piece(self, half, z, y, x=None):
        if self.split:
            part = self.links.x if x is None else x
            return self.full.at[z, y, half, part] if self.name == "s" else self.full.at[half, part, z, y]
        if self.name == "e":
            return self.full.at[half, :, z, y]
        return self.full.at[z, y, half] if self.name in "sv" else self.full.at[half, z, y]

    def core_send(self, z, y):
        k = self.links
        here = self.piece(k.c, z, y)
        self.wait5.append(k.send(here, here, k.sibling(), self.piece(1 - k.c, z, y)))
        if self.split:
            there = self.piece(k.c, z, y, 1 - k.x)
            self.waitx.append((k.send(here, here, k.at_x(1 - k.x), there), z, y))

    def one(self):
        k, p = self.links, self.p
        self.wait1 = k.send(self.cand.at[1 - k.c], self.rx1, k.sibling())
        if self.near:
            self.wait2 = []
            for d in range(1, p.X):
                x = lax.rem(k.x + d, p.X)
                for i, h in enumerate((k.c, 1 - k.c)):
                    self.wait2.append(k.send(self.cand.at[h], self.rx2.at[d - 1, i], k.at_x(x, i)))

    def two(self):
        k, p = self.links, self.p
        self.wait1()
        self.sel[...] = self.cand[k.c] + self.rx1[...]
        if self.split:
            self.wait2 = [k.send(self.sel.at[1 - k.x], self.rx2.at[0, 0], k.at_x(1 - k.x))]
        elif not self.near:
            self.wait2 = [
                k.send(self.sel, self.rx2.at[d - 1, 0], k.at_x(lax.rem(k.x + d, p.X)))
                for d in range(1, p.X)
            ]

    def y_sends(self, z):
        k, p = self.links, self.p
        here = self.piece(k.c, z, k.y)
        for d in range(1, p.Y):
            other = lax.rem(k.y + p.Y - d, p.Y)
            partner = k.at_y(lax.rem(k.y + d, p.Y))
            wait = k.send(here, here, partner, self.piece(k.c, z, other))
            self.wait4.append((wait, z, other))

    def pair_round(self):
        k = self.links
        bit = self.p.Z >> (self.rounds + 1)
        partner = k.at_z(k.flip_z(bit))
        self.rounds += 1
        for z in self.held:
            other = z + bit - 2 * bit * lax.rem(lax.div(z, bit), 2)
            here = self.piece(k.c, z, k.y)
            wait = k.send(here, here, partner, self.piece(k.c, other, k.y))
            self.wait3.append((wait, other))

    def three(self):
        k, p = self.links, self.p
        for wait in self.wait2:
            wait()
        total = self.sel[k.x] if self.split else self.sel[...]
        for d in range(p.X - 1):
            for i in range(2 if self.near else 1):
                total = total + self.rx2[d, i]
        here = self.piece(k.c, k.z, k.y)
        here[...] = total
        self.held, self.rounds = [k.z], 0
        if self.direct:
            for d in range(1, p.Z):
                other = lax.rem(k.z + p.Z - d, p.Z)
                partner = k.at_z(lax.rem(k.z + d, p.Z))
                wait = k.send(here, here, partner, self.piece(k.c, other, k.y))
                self.wait3.append((wait, other))
        else:
            self.pair_round()

    def own(self):
        self.y_sends(self.links.z)
        self.core_send(self.links.z, self.links.y)

    def four(self):
        waits, self.wait3 = self.wait3, []
        for wait, z in waits:
            wait()
            self.held.append(z)
        if len(self.held) < self.p.Z:
            self.pair_round()
        for _, z in waits:
            self.y_sends(z)
            self.core_send(z, self.links.y)

    def five(self):
        while self.wait3:
            self.four()
        for wait, z, y in self.wait4:
            wait()
            self.core_send(z, y)

    def cross(self):
        k = self.links
        for wait, z, y in self.waitx:
            wait()
            here = self.piece(k.c, z, y, 1 - k.x)
            self.wait5.append(k.send(here, here, k.sibling(), self.piece(1 - k.c, z, y, 1 - k.x)))

    def six(self):
        for wait in self.wait5:
            wait()


class Reduce:
    def __init__(self, name, links, refs, half, fin):
        self.name, self.links, self.p = name, links, links.p
        self.direct = name in DIRECT
        self.__dict__.update(refs)
        self.half, self.fin = half, fin

    def one(self):
        k = self.links
        self.wait1 = k.send(self.half(1 - k.c), self.r1, k.sibling())

    def two(self):
        k, p = self.links, self.p
        self.wait1()
        mine = self.half(k.c)

        def add(index, carry):
            z, y = lax.div(index, p.Y), lax.rem(index, p.Y)
            self.r1[z, y] = self.r1[z, y] + mine[z, y]
            return carry

        lax.fori_loop(0, p.fs, add, 0)
        self.wait2 = []
        if self.direct:
            k.hear_columns()
            for d in range(1, p.fs):
                f = lax.rem(k.f + d, p.fs)
                source = self.r1.at[lax.div(f, p.Y), lax.rem(f, p.Y)]
                self.wait2.append(k.send(source, self.r3.at[d - 1], (k.g, f)))
            return
        for d in range(1, p.Y):
            other = lax.rem(k.y + d, p.Y)
            self.wait2.append(k.send(self.r1.at[:, other], self.r2.at[d - 1], k.at_y(other)))

    def three(self):
        k, p = self.links, self.p
        for wait in self.wait2:
            wait()
        self.wait3 = []
        if self.direct:
            total = self.r1[k.z, k.y].astype(f32)
            for d in range(p.fs - 1):
                total = total + self.r3[d].astype(f32)
            self.a4[...] = total
            return

        def add(z, carry):
            total = self.r1[z, k.y].astype(f32)
            for d in range(p.Y - 1):
                total = total + self.r2[d, z].astype(f32)
            self.a2[z] = total.astype(b16)
            return carry

        lax.fori_loop(0, p.Z, add, 0)
        self.bit, self.slot = 1, 0
        self.pair_round()

    def pair_round(self):
        k, p = self.links, self.p
        bit = self.bit
        partner = k.flip_z(bit)
        low_partner, own = lax.rem(partner, 2 * bit), lax.rem(k.z, 2 * bit)
        self.wait3 = []
        for step in range(p.Z // (2 * bit)):
            target = low_partner + 2 * bit * step
            mine = own + 2 * bit * step
            wait = k.send(self.a2.at[target], self.r3.at[self.slot], k.at_z(partner))
            self.wait3.append((wait, mine, self.slot))
            self.slot += 1
        self.bit = 2 * bit

    def four(self):
        for wait, z, slot in self.wait3:
            wait()
            total = self.a2[z].astype(f32) + self.r3[slot].astype(f32)
            if self.bit < self.p.Z:
                self.a2[z] = total.astype(b16)
            else:
                self.a4[...] = total
        self.wait3 = []
        if not self.direct and self.bit < self.p.Z:
            self.pair_round()

    def five(self):
        k, p = self.links, self.p
        while self.wait3:
            self.four()
        self.a3[...] = self.a4[...].astype(b16)
        self.wait4 = []
        for d in range(1, p.X):
            x = lax.rem(k.x + d, p.X)
            for i in range(2):
                self.wait4.append(k.send(self.a3, self.r4.at[d - 1, i], k.at_x(x, i)))
        self.wait4.append(k.send(self.a3, self.r5, k.sibling()))

    def six(self):
        k, p = self.links, self.p
        for wait in self.wait4:
            wait()
        for h, total, i in ((k.c, self.a4[...], 0), (1 - k.c, self.r5[...].astype(f32), 1)):
            for d in range(p.X - 1):
                total = total + self.r4[d, i].astype(f32)
            self.fin(h)[...] = total


class Pair(Reduce):
    def __init__(self, name, links, refs):
        grad, fin = refs["grad"], refs["fin"]

        def half(h, part):
            return grad.at[:, :, h, part] if name == "s" else grad.at[h, part]

        self.parts = []
        if "parts" in refs:
            for part, steps in enumerate(refs["parts"]):
                reduce = Reduce(
                    name, links, steps, lambda h, part=part: half(h, part), lambda h, part=part: fin.at[h, part]
                )
                self.parts.append(reduce)
            return
        super().__init__(name, links, refs["steps"], half, fin)
        self.rx, self.other, self.all_fin = refs["rx"], refs["other"], fin

    def one(self):
        if self.parts:
            return [part.one() for part in self.parts]
        k = self.links
        self.wait1 = [
            k.send(self.half(1 - k.c, 1 - k.x), self.other, k.sibling()),
            k.send(self.half(1 - k.c, k.x), self.r1, k.sibling()),
        ]

    def add_pieces(self, total, term):
        p = self.p

        def add(index, carry):
            z, y = lax.div(index, p.Y), lax.rem(index, p.Y)
            total[z, y] = total[z, y] + term[z, y]
            return carry

        lax.fori_loop(0, p.fs, add, 0)

    def two(self):
        if self.parts:
            return [part.two() for part in self.parts]
        k = self.links
        self.wait1[0]()
        self.add_pieces(self.other, self.half(k.c, 1 - k.x))
        self.waitx = k.send(self.other, self.rx, k.at_x(1 - k.x))
        self.wait1[1]()
        self.add_pieces(self.r1, self.half(k.c, k.x))

    def across(self):
        if self.parts:
            return
        k, p = self.links, self.p
        self.waitx()
        self.add_pieces(self.r1, self.rx)
        self.wait2 = []
        for d in range(1, p.Y):
            other = lax.rem(k.y + d, p.Y)
            self.wait2.append(k.send(self.r1.at[:, other], self.r2.at[d - 1], k.at_y(other)))

    def three(self):
        return [part.three() for part in self.parts] if self.parts else super().three()

    def four(self):
        return [part.four() for part in self.parts] if self.parts else super().four()

    def five(self):
        return [part.five() for part in self.parts] if self.parts else super().five()

    def six(self):
        if self.parts:
            return [part.six() for part in self.parts]
        k = self.links
        for wait in self.wait4:
            wait()
        self.all_fin[k.c, k.x] = self.a4[...]
        self.all_fin[1 - k.c, k.x] = self.r5[...].astype(f32)
        self.all_fin[k.c, 1 - k.x] = self.r4[0, 0].astype(f32)
        self.all_fin[1 - k.c, 1 - k.x] = self.r4[0, 1].astype(f32)


def spread_matrix(rows, rp, count):
    bits = int(math.log2(rp))
    shape = (count * rows, count * rp)
    a = lax.broadcasted_iota(jnp.int32, shape, 0)
    b = lax.broadcasted_iota(jnp.int32, shape, 1)
    i = lax.bitwise_and(b, rp - 1)
    hit = (a == lax.shift_right_logical(b, bits) * rows + i) & (i < rows)
    return jnp.where(hit, 1.0, 0.0).astype(b16)


def block_kernel(p, tree, *refs):
    s = p.s
    count, sides, owners = refs[:3]
    sources = dict(zip(("x", "cot", "focal", "modulate", "project", "expand", "shrink", "vector"), refs[3:11]))
    out_hbm, grad_hbm = refs[11:13]
    fin_hbm = dict(zip(REDUCED, refs[13:19]))
    own = jax.tree.unflatten(tree, refs[19:])
    k = Links(p, own["send_sem"], own["recv_sem"], own["column_sem"])
    land, local_sem = own["land"], own["local_sem"]
    local_used = []

    def local(source, target):
        copy = pltpu.make_async_copy(source, target, local_sem.at[len(local_used)])
        local_used.append(copy)
        copy.start()
        return copy

    loads = {}
    for name in ("focal", "vector", "modulate", "project", "x", "expand", "shrink", "cot"):
        loads[name] = local(sources[name].at[0], land[name])
    k.signal_partners()

    def mine(index):
        return jnp.where(owners[index] == k.g, 1.0, 0.0).astype(f32)

    def cut(values, rows, rp):
        if rows == rp:
            return values
        return jnp.concatenate([values, jnp.zeros((rp - rows, values.shape[1]), f32)], axis=0)

    def candidate(name, h, values):
        rows, rp = values.shape[0], p.rp2 if name == "s" else p.rp
        low, target = cut(values, rows, rp).astype(b16), own["g" + name]["cand"]
        if name == "e":
            for part in range(2):
                target[h, part] = low[:, part * c : (part + 1) * c]
        elif name == "s":
            for part in range(2):
                target[h, part] = low[part * p.rs : (part + 1) * p.rs]
        else:
            target[h] = low

    gathers = {
        name: Gather(name, k, own["g" + name]) for name in GATHERED
    }
    gv, ga, gb, gm, ge, gs = (gathers[name] for name in GATHERED)
    reduces = {}
    for name in REDUCED:
        refs = own["r" + name]
        if name in PAIRS:
            reduces[name] = Pair(name, k, refs)
        else:
            reduces[name] = Reduce(
                name, k, refs["steps"], lambda h, r=refs: r["grad"].at[h], lambda h, r=refs: r["fin"].at[h]
            )
    rs, re, rm, rq, rt, ru = (reduces[name] for name in REDUCED)
    c, wide = s.c, s.hid // 2

    def prepare():
        block.prepare()
        own["gvec"][s.nvec :, :] = jnp.zeros((LANE - s.nvec, s.c), f32)
        put("q", 1, LANE, jnp.zeros((s.c, LANE), f32))
        loads["focal"].wait()
        loads["vector"].wait()
        values = cut(land["vector"][...] * mine(5), p.rows, p.rp)
        values = jnp.concatenate([values, jnp.zeros((p.rp, LANE - s.nvec), f32)], axis=1)
        focal = land["focal"]
        for h in range(2):
            own["gv"]["cand"][h] = values[h * p.rv : (h + 1) * p.rv]
            at = c + h * LANE
            candidate("a", h, focal[:, at : at + LANE] * mine(0))
        candidate("b", 0, jnp.concatenate([focal[:, c + 2 * LANE :], focal[:, :LANE]], axis=1) * mine(0))
        candidate("b", 1, focal[:, LANE:c] * mine(0))
        loads["modulate"].wait()
        loads["project"].wait()
        candidate("m", 0, land["modulate"][...] * mine(1))
        candidate("m", 1, land["project"][...] * mine(2))
        loads["expand"].wait()
        for h in range(2):
            candidate("e", h, land["expand"][:, h * wide : (h + 1) * wide] * mine(3))
        loads["shrink"].wait()
        for h in range(2):
            candidate("s", h, land["shrink"][h * p.rows2 : (h + 1) * p.rows2, :] * mine(4))
        loads["x"].wait()
        block.first_norm()

    if not p.even:
        own["map"][...] = spread_matrix(p.rows, p.rp, p.fs)

    def compact(values):
        return values if p.even else mm(own["map"][...], values).astype(b16)

    def spread(values):
        values = values.astype(b16)
        return values if p.even else mm_g(own["map"][...], values).astype(b16)

    def matrix(name, h, at, cols):
        part = own["g" + name]["full"][h, :, :, :, at : at + cols]
        return compact(part.reshape(p.fs * p.rp, cols))

    def take_expand(h, at, cols):
        parts = []
        for part in range(2):
            first, last = max(at, part * c), min(at + cols, (part + 1) * c)
            if first < last:
                values = own["ge"]["full"][h, part, :, :, :, first - part * c : last - part * c]
                parts.append(compact(values.reshape(p.fs * p.rp, last - first)))
        return jnp.concatenate(parts, axis=1) if len(parts) > 1 else parts[0]

    def take_context(chunks):
        parts = []
        if chunks[0] < 2:
            parts += [matrix("a", ch, 0, LANE) for ch in chunks if ch < 2]
        if chunks[-1] == 2:
            parts.append(matrix("b", 0, 0, LANE))
        return jnp.concatenate(parts, axis=1) if len(parts) > 1 else parts[0]

    def take_query():
        return jnp.concatenate([matrix("b", 0, LANE, LANE), matrix("b", 1, 0, 2 * LANE)], axis=1)

    def take_shrink(at, rows):
        if p.even:
            return own["gs"]["full"][...].reshape(s.hid, s.c)[at : at + rows]
        return own["w2n"][at : at + rows, :]

    def put(name, h, at, values):
        cols = values.shape[1]
        grads = spread(values).reshape(p.Z, p.Y, p.rp, cols)
        own["r" + name]["grad"][h, :, :, :, at : at + cols] = grads

    def put_expand(h, at, values):
        grads = spread(values).reshape(p.Z, p.Y, p.rp, values.shape[1])
        own["re"]["grad"][h, 1 if at else 0] = grads

    def put_query(values):
        put("q", 0, 0, values[:, : 2 * LANE])
        put("q", 1, 0, values[:, 2 * LANE :])

    def put_context(chunks, values):
        for i, ch in enumerate(chunks):
            name, h = (("t", 0), ("t", 1), ("u", 0))[ch]
            put(name, h, 0, values[:, i * LANE : (i + 1) * LANE])

    def put_shrink(at, rows, values):
        low = values.astype(b16)
        if not p.even:
            own["g2n"][at : at + rows, :] = low
            return
        start = at
        while start < at + rows:
            piece, inner = divmod(start, p.rs)
            size = min(p.rs - inner, at + rows - start)
            (f, h), part, first = divmod(piece // 2, 2), piece % 2, start - at
            own["rs"]["grad"][f // p.Y, f % p.Y, h, part, inner : inner + size, :] = low[first : first + size]
            start += size

    block = Compute(
        s,
        dict(
            x=land["x"],
            cot=land["cot"],
            v=own["v"],
            count=count[0, 0],
            sides=sides[0],
            out=own["out"],
            grad=own["grad"],
            gv=own["gvec"],
            wc=take_context,
            wq=take_query,
            wh=lambda: matrix("m", 0, 0, c),
            wp=lambda: matrix("m", 1, 0, c),
            w1=take_expand,
            w2=take_shrink,
            put_gq=put_query,
            put_gc=put_context,
            put_gh=lambda values: put("m", 0, 0, values),
            put_gp=lambda values: put("m", 1, 0, values),
            put_g1=put_expand,
            put_g2=put_shrink,
        ),
        own["compute"],
    )

    stores = []

    def settle(name):
        reduces[name].six()
        stores.append(local(own["r" + name]["fin"], fin_hbm[name]))

    def take_vector():
        vector = own["gv"]["full"][...].reshape(p.fs * p.rp, LANE)
        if not p.even:
            vector = jnp.dot(own["map"][...].astype(f32), vector, precision=lax.Precision.HIGHEST)
        own["v"][...] = vector.T

    def modulate():
        loads["cot"].wait()
        block.modulate()

    def close_shrink():
        def close(f, carry):
            z, y = lax.div(f, p.Y), lax.rem(f, p.Y)
            parts = [
                own["gs"]["full"][z, y, h].astype(f32).reshape(p.rp2, s.c)[: p.rows2] for h in range(2)
            ]
            at = pl.ds(pl.multiple_of(f * 2 * p.rows2, 2 * p.rows2), 2 * p.rows2)
            own["w2n"][at, :] = jnp.concatenate(parts, axis=0).astype(b16)
            return carry

        if not p.even:
            lax.fori_loop(0, p.fs, close, 0)

    def shrink_grad():
        block.shrink_grad()

        def open_up(f, carry):
            z, y = lax.div(f, p.Y), lax.rem(f, p.Y)
            at = pl.ds(pl.multiple_of(f * 2 * p.rows2, 2 * p.rows2), 2 * p.rows2)
            both = own["g2n"][at, :].astype(f32)
            for h in range(2):
                part = cut(both[h * p.rows2 : (h + 1) * p.rows2], p.rows2, p.rp2)
                own["rs"]["grad"][z, y, h] = part.reshape(2, p.rs, s.c).astype(b16)
            return carry

        if not p.even:
            lax.fori_loop(0, p.fs, open_up, 0)

    def middle():
        block.middle()
        stores.append(local(own["out"], out_hbm.at[0]))

    def last_out():
        block.last_out()
        stores.append(local(own["grad"], grad_hbm.at[0]))

    def put_vector():
        grads = own["gvec"][...].T
        if not p.even:
            grads = mm_g(own["map"][...], grads.astype(b16))
        own["ru"]["grad"][1] = grads.astype(b16).reshape(p.Z, p.Y, p.rp, LANE)

    prepare()
    k.wait_partners()
    gv.one()
    gb.one()
    gs.one()
    ge.one()
    ga.one()
    gm.one()
    ge.two()
    ga.two()
    gv.two()
    gv.three()
    gb.two()
    ga.three()
    gm.two()
    ge.three()
    gs.two()
    gb.three()
    ga.own()
    gb.own()
    gv.own()
    gv.four()
    gm.three()
    ga.four()
    gs.three()
    ge.own()
    gv.five()
    ge.four()
    gs.own()
    gm.own()
    gv.six()
    take_vector()
    ga.five()
    block.first()
    gb.four()
    ga.six()
    block.context((0, 1))
    block.level(0, (0, 1))
    block.level(1, (0, 1))
    gm.four()
    block.level(2, (0, 1))
    ge.four()
    gs.four()
    gb.five()
    gb.six()
    block.context((2,))
    block.level(0, (2,))
    block.query()
    gm.four()
    ge.five()
    gs.four()
    block.level(1, (2,))
    block.level(2, (2,))
    gm.five()
    block.pooling()
    gm.six()
    gs.five()
    ge.cross()
    modulate()
    ge.six()
    block.feed()
    gs.cross()
    shrink_grad()
    rs.one()
    gs.six()
    close_shrink()
    block.feed_back()
    block.expand_grad()
    rs.two()
    block.feed_out()
    re.one()
    middle()
    block.query_grad()
    block.middle_grads()
    rm.one()
    rq.one()
    block.focal_top()
    re.two()
    rm.two()
    rq.two()
    block.level_back(2, (0, 1))
    rs.across()
    block.level_back(1, (0, 1))
    block.level_back(0, (0, 1))
    rm.three()
    block.context_grad((0, 1))
    rt.one()
    block.level_back(2, (2,))
    rt.two()
    block.level_back(1, (2,))
    block.level_back(0, (2,))
    re.across()
    rm.four()
    block.context_grad((2,))
    rq.three()
    block.last_sums()
    rq.five()
    rs.three()
    put_vector()
    ru.one()
    last_out()
    ru.two()
    rt.three()
    re.three()
    settle("q")
    rm.five()
    rs.four()
    ru.three()
    re.four()
    settle("m")
    ru.five()
    rt.five()
    rs.five()
    re.five()
    settle("t")
    settle("u")
    settle("s")
    settle("e")
    k.hear_columns()
    k.finish()
    for store in stores:
        store.wait()


def adam_kernel(p, rates, tree, *refs):
    s = p.s
    owners = refs[0]
    fins = dict(zip(REDUCED, refs[1:7]))
    passed, olds = refs[7:9], refs[9:27]
    passed_out, news = refs[27:29], refs[29:47]
    own = jax.tree.unflatten(tree, refs[47:])
    sems = own["sem"]
    g = lax.axis_index("grp")
    used = []

    def local(source, target):
        copy = pltpu.make_async_copy(source, target, sems.at[len(used)])
        used.append(copy)
        copy.start()
        return copy

    wide = s.hid // 2
    groups = (
        (3, [("e", (h, i), 0, p.rows, h * wide + i * s.c, s.c) for h in range(2) for i in range(2)]),
        (
            4,
            [
                ("s", (h, i), h * p.rows2 + i * p.rs, min(p.rows2 - i * p.rs, p.rs), 0, s.c)
                for h in range(2)
                for i in range(2)
            ],
        ),
        (1, [("m", 0, 0, p.rows, 0, s.c)]),
        (2, [("m", 1, 0, p.rows, 0, s.c)]),
        (
            0,
            [
                ("q", 0, 0, p.rows, 0, 2 * LANE),
                ("q", 1, 0, p.rows, 2 * LANE, LANE),
                ("t", 0, 0, p.rows, s.c, LANE),
                ("t", 1, 0, p.rows, s.c + LANE, LANE),
                ("u", 0, 0, p.rows, s.c + 2 * LANE, LANE),
            ],
        ),
        (5, [("u", 1, 0, p.rows, 0, s.nvec)]),
    )
    waits = {}
    for index, pieces in groups:
        waits[index] = []
        for name in dict.fromkeys(piece[0] for piece in pieces):
            if name not in waits:
                waits[name] = local(fins[name], own["fin"][name])
        for i in range(3):
            waits[index].append(local(olds[3 * index + i], own["old"][3 * index + i]))
    passing = [local(a, b) for a, b in zip(passed, own["passed"])]
    stores, arrived = [], set()
    for index, pieces in groups:
        scale = jnp.where(owners[index] == g, 1.0, 0.0).astype(f32)
        for wait in waits[index]:
            wait.wait()
        for name, h, row, rows, col, cols in pieces:
            if name not in arrived:
                arrived.add(name)
                waits[name].wait()
            at = (0, slice(row, row + rows), slice(col, col + cols))
            gradient = own["fin"][name].at[h][:rows, :cols]
            weight, first, second = (own["old"][3 * index + i][at] for i in range(3))
            first_new = beta_one * first + (1.0 - beta_one) * gradient
            second_new = beta_two * second + (1.0 - beta_two) * gradient * gradient
            first_hat = first_new / (1.0 - beta_one**STEP)
            second_hat = second_new / (1.0 - beta_two**STEP)
            weight_new = weight - rates[index] * (
                first_hat / (jnp.sqrt(second_hat) + adam_eps) + weight_decay * weight
            )
            for i, value in enumerate((weight_new, first_new, second_new)):
                own["new"][3 * index + i][at] = value * scale
        for i in range(3):
            stores.append(local(own["new"][3 * index + i], news[3 * index + i]))
    for wait, a, b in zip(passing, own["passed"], passed_out):
        wait.wait()
        stores.append(local(a, b))
    for store in stores:
        store.wait()


def solution(mesh):
    n_grp, n_fs = mesh.shape["grp"], mesh.shape["fs"]

    def shards(image_patches, cotangent, image_count, resolution, owner_list, *tensors):
        side, channels = image_patches.shape[1], image_patches.shape[3]
        hid = tensors[9].shape[2]
        s = Shape(side, channels, hid)
        p = Plan(n_grp, n_fs, s)
        grid = (side, side, channels)
        scratch = dict(
            compute=compute_scratch(s),
            land=dict(
                x=pltpu.VMEM(grid, b16),
                cot=pltpu.VMEM(grid, b16),
                focal=pltpu.VMEM((p.rows, 2 * channels), f32),
                modulate=pltpu.VMEM((p.rows, channels), f32),
                project=pltpu.VMEM((p.rows, channels), f32),
                expand=pltpu.VMEM((p.rows, hid), f32),
                shrink=pltpu.VMEM((2 * p.rows2, channels), f32),
                vector=pltpu.VMEM((p.rows, s.nvec), f32),
            ),
            out=pltpu.VMEM(grid, b16),
            grad=pltpu.VMEM(grid, f32),
            v=pltpu.VMEM((LANE, s.c), f32),
            gvec=pltpu.VMEM((LANE, s.c), f32),
            local_sem=pltpu.SemaphoreType.DMA((24,)),
            send_sem=pltpu.SemaphoreType.DMA((sem_count(p),)),
            recv_sem=pltpu.SemaphoreType.DMA((sem_count(p),)),
            column_sem=pltpu.SemaphoreType.REGULAR,
        )
        for name in GATHERED:
            scratch["g" + name] = gather_scratch(p, name)
        for name in REDUCED:
            scratch["r" + name] = reduce_scratch(p, name)
        if not p.even:
            scratch["map"] = pltpu.VMEM((s.c, p.fs * p.rp), b16)
            scratch["w2n"] = pltpu.VMEM((s.hid, s.c), b16)
            scratch["g2n"] = pltpu.VMEM((s.hid, s.c), b16)

        def flatten(scratch):
            return jax.tree.flatten(scratch, is_leaf=lambda v: not isinstance(v, (dict, list)))

        leaves, tree = flatten(scratch)
        anywhere = pl.BlockSpec(memory_space=pl.ANY)
        smem = pl.BlockSpec(memory_space=pltpu.SMEM)
        shape = jax.ShapeDtypeStruct
        fins = [shape(fin_shape(p, name), f32) for name in REDUCED]
        images = [shape(image_patches.shape, b16), shape(image_patches.shape, f32)]
        tensors = tensors[:15] + tuple(t.transpose(0, 2, 1) for t in tensors[15:])
        results = pl.pallas_call(
            lambda *refs: block_kernel(p, tree, *refs),
            out_shape=images + fins,
            in_specs=[smem] * 3 + [anywhere] * 8,
            out_specs=[anywhere] * 8,
            scratch_shapes=leaves,
            compiler_params=pltpu.CompilerParams(
                collective_id=0, has_side_effects=True, vmem_limit_bytes=VMEM_BYTES
            ),
            name="block",
        )(
            image_count,
            resolution,
            owner_list,
            image_patches,
            cotangent,
            *tensors[0:16:3],
        )
        wide_rate = 1.5 / math.sqrt(channels)
        rates = (wide_rate,) * 4 + (1.5 / math.sqrt(hid), 0.2)
        adam_leaves, adam_tree = flatten(
            dict(
                fin={name: pltpu.VMEM(fin_shape(p, name), f32) for name in REDUCED},
                old=[pltpu.VMEM(t.shape, f32) for t in tensors],
                new=[pltpu.VMEM(t.shape, f32) for t in tensors],
                passed=[pltpu.VMEM(t.shape, t.dtype) for t in images],
                sem=pltpu.SemaphoreType.DMA((56,)),
            )
        )
        news = pl.pallas_call(
            lambda *refs: adam_kernel(p, rates, adam_tree, *refs),
            out_shape=images + [shape(t.shape, f32) for t in tensors],
            in_specs=[smem] + [anywhere] * 26,
            out_specs=[anywhere] * 20,
            scratch_shapes=adam_leaves,
            compiler_params=pltpu.CompilerParams(vmem_limit_bytes=VMEM_BYTES),
            name="adam",
        )(owner_list, *results[2:], *results[:2], *tensors)
        return tuple(news[:17]) + tuple(t.transpose(0, 2, 1) for t in news[17:])

    images = P(("grp", "fs"), None, None, None)
    weights = (P("grp", "fs", None),) * 15 + (P("grp", None, "fs"),) * 3
    return jax.shard_map(
        shards,
        mesh=mesh,
        in_specs=(images, images, P("grp", "fs"), P(("grp", "fs")), P()) + weights,
        out_specs=(images, images) + weights,
        check_vma=False,
    )
```
